32 devices in a mesh: parts: 2 (over y), space: 4 (over z), comp: 2 (over x), lev: 2 (over core).
Axes of the slice: x: 2, y: 2, z: 4, core: 2. Of those that a mesh axis runs over, the one named last changes fastest.
Arguments:
- atmos_state: float32 [16, 16, 1024], P(('parts', 'lev'), None, ('space', 'comp')), parts along dimension 0, may hold values from -6 to 6
- ocean_state: float32 [32, 8, 512], P(('parts', 'lev'), ('space', 'comp')), parts along dimension 0, may hold values from -6 to 6
- vertical_mixing: float32 [8, 8], replicated, may hold values from -2 to 2
- flux_coupling: float32 [16, 8], replicated, may hold values from -2 to 2
- request_cells: int32 [8, 8, 256], P(('space', 'comp')), may hold values from 0 to 2047, as said below
- margin_slot: int32 [4, 8, 512], P(None, ('space', 'comp')), may hold values from 0 to 2047, as said below
- margin_weight: float32 [4, 8, 512], P(None, ('space', 'comp')), may hold values from 0.1 to 0.5
- sea_mask: int32 [8, 512], P(('space', 'comp')), may hold values from 0 to 1, as said below
Outputs:
- atmos_next: float32 [16, 16, 1024], P(('parts', 'lev'), None, ('space', 'comp')), parts along dimension 0
- ocean_next: float32 [32, 8, 512], P(('parts', 'lev'), ('space', 'comp')), parts along dimension 0
- returned: float32 [32, 16, 1024], P(('parts', 'lev'), None, ('space', 'comp')), parts along dimension 0
The draws below stay inside these ranges and needn't reach their ends.
There are 2 independent parts, one for each index of `parts`. The reference program is written for one: setup_inputs(seed, part) draws one part's arguments, and reference() takes and returns one part's arrays. A program takes and returns all parts, laid end to end along the dimension named above; an argument that names none is the same for every part. Nothing has to cross between parts.
Inputs may be any that keep to these rules, and one draw needn't show every extreme that they name: `request_cells`: entry [s, d, r] is the local cell of atmosphere strip s whose flux fills slot r for ocean strip d; slots that no sea margin names hold 0. `margin_slot`: for ocean cell (x, y) the source strip is s = y // 64. On sea cells the slots in use from strip s to ocean strip d are 0 to 4 times the sea cells of d in s's columns, minus 1, each named by one margin; on land cells slot r = k. The named atmosphere cell lies in column 2 y or 2 y + 1 and a row from 2 x - 1 to 2 x + 2. The last strip fills all 256 slots of every ocean strip; strips further west carry fewer, down to none. `sea_mask`: land lies west of a coastline that varies from row to row, with scattered islands.
All inputs are finite; a program needn't handle non-finite values.
Results may differ from the reference program's by a relative error of at most 0.0001.
Values sent between devices are 32-bit elements; how exact they have to be, the bound alone decides.
No kernel may reach another device: no remote copies, remote signals or barrier semaphores. Data moves between devices by JAX's collectives and lax.ppermute only.
A program may use at most 128 MiB of HBM per device.

```python
import jax
import jax.numpy as jnp
from jax import lax

FLD = 16
LA = 8
ASUB = 2
SUB = 8
K = 4
OXD = 1
AYD = 128
NPEER = 8
NXO = 8
NXA = 16
NYA = 1024
NYO = 512
CAP = 256


def coastline(key):
    key_coast, key_isle, key_tilt = jax.random.split(key, 3)
    coast = jax.random.randint(key_coast, (NXO, 1), 0, NYO // 2 + 1).astype(jnp.int32)
    isles = jax.random.randint(key_isle, (NXO, NYO), 0, 8).astype(jnp.int32)
    columns = jnp.arange(NYO, dtype=jnp.int32)[None, :]
    open_sea = columns >= NYO - AYD // 2
    sea = (columns >= coast) & ((isles != 0) | open_sea)
    tilt = jax.random.randint(key_tilt, (NXO, NYO), -1, 2).astype(jnp.int32)
    return (sea.astype(jnp.int32), tilt)


def slot_tables(key):
    sea, tilt = coastline(key)
    half = AYD // 2
    blocks = sea.reshape(NPEER, OXD, NPEER, half).transpose(0, 2, 1, 3).reshape(NPEER, NPEER, OXD * half)
    before = jnp.cumsum(blocks, axis=2).astype(jnp.int32) - blocks
    ranking = before.reshape(NPEER, NPEER, OXD, half).transpose(0, 2, 1, 3).reshape(NXO, NYO)
    rows = jnp.arange(NXO, dtype=jnp.int32)[:, None]
    columns = jnp.arange(NYO, dtype=jnp.int32)[None, :]
    source = jnp.broadcast_to(columns // half, (NXO, NYO)).astype(jnp.int32)
    target = jnp.broadcast_to(rows // OXD, (NXO, NYO)).astype(jnp.int32)
    margin_ids = jnp.arange(K, dtype=jnp.int32)[:, None, None]
    slot_rank = jnp.where(sea[None] == 1, ranking[None] * K + margin_ids, margin_ids).astype(jnp.int32)
    atmos_row = jnp.clip(2 * rows[None] + tilt[None] + margin_ids // 2, 0, NXA - 1)
    atmos_col = 2 * columns[None] + margin_ids % 2
    local = (atmos_row * AYD + atmos_col - source[None] * AYD).astype(jnp.int32)
    return (sea, source, target, slot_rank, local)


def draw_sea_mask(key, part):
    sea, source, target, slot_rank, local = slot_tables(key)
    return sea.astype(jnp.int32)


def draw_margin_slot(key, part):
    sea, source, target, slot_rank, local = slot_tables(key)
    return (source[None] * CAP + slot_rank).astype(jnp.int32)


def draw_request_cells(key, part):
    sea, source, target, slot_rank, local = slot_tables(key)
    kept_rank = jnp.where(sea[None] == 1, slot_rank, CAP).astype(jnp.int32)
    src_all = jnp.broadcast_to(source[None], (K, NXO, NYO)).reshape(-1)
    dst_all = jnp.broadcast_to(target[None], (K, NXO, NYO)).reshape(-1)
    table = jnp.zeros((NPEER, NPEER, CAP), jnp.int32)
    table = table.at[src_all, dst_all, kept_rank.reshape(-1)].set(local.reshape(-1), mode='drop')
    return table.astype(jnp.int32)


def shard_levels(stream_key, extent, pieces, low, largest):
    def one(position, shards_of):
        draws = jax.random.uniform(jax.random.fold_in(jax.random.fold_in(stream_key, 6), position), (shards_of,), jnp.float32, low / len(pieces), largest / len(pieces))
        return jnp.repeat(jnp.exp(draws), extent[position] // shards_of).reshape((-1,) + (1,) * (len(extent) - position - 1))

    loudness = one(*pieces[0])
    for cut in pieces[1:]:
        loudness = loudness * one(*cut)
    return loudness


def noise(own_key, extent, width, bound, cuts=(), held_as=jnp.bfloat16):
    array = jax.random.normal(own_key, extent, jnp.float32) * width
    if len(cuts) > 0:
        array = shard_levels(own_key, extent, cuts, -0.22, 0.18) * array
    return jnp.clip(array, min=-bound, max=bound).astype(held_as)


def setup_inputs(seed: int = 0, part: int = 0) -> dict:
    arg_keys = jax.random.split(jax.random.key(seed), 9)
    part_splits = jax.random.split(jax.random.fold_in(arg_keys[8], part), 9)
    atmos_state = noise(part_splits[0], (LA, NXA, NYA), 1.0, 6.0, ((0, 2), (2, 8)), jnp.float32)
    ocean_state = noise(part_splits[1], (FLD, NXO, NYO), 1.0, 6.0, ((0, 2), (1, 8)), jnp.float32)
    vertical_mixing = noise(arg_keys[2], (LA, LA), LA ** -0.5, 2.0, (), jnp.float32)
    flux_coupling = noise(arg_keys[3], (FLD, LA), LA ** -0.5, 2.0, (), jnp.float32)
    request_cells = draw_request_cells(jax.random.fold_in(arg_keys[8], 71), part)
    margin_slot = draw_margin_slot(jax.random.fold_in(arg_keys[8], 71), part)
    margin_weight = jnp.clip(0.1 + 0.4 * jax.random.uniform(arg_keys[6], (K, NXO, NYO), jnp.float32) ** shard_levels(arg_keys[6], (K, NXO, NYO), ((1, 8),), -0.2, 0.2), 0.1, 0.5)
    sea_mask = draw_sea_mask(jax.random.fold_in(arg_keys[8], 71), part)
    return dict(atmos_state=atmos_state, ocean_state=ocean_state, vertical_mixing=vertical_mixing, flux_coupling=flux_coupling, request_cells=request_cells, margin_slot=margin_slot, margin_weight=margin_weight, sea_mask=sea_mask)


DIFFUSE = 0.2
TENDENCY = 0.25
OCEAN_MIX = 0.2
FORCING = 0.15


def neighbours(field):
    padded = jnp.pad(field, ((0, 0), (1, 1), (1, 1)))
    return padded[:, 2:, 1:-1] + padded[:, :-2, 1:-1] + padded[:, 1:-1, 2:] + padded[:, 1:-1, :-2]


def reference(atmos_state, ocean_state, vertical_mixing, flux_coupling, request_cells, margin_slot, margin_weight, sea_mask):
    atmos = atmos_state
    for substep in range(ASUB):
        beside = neighbours(atmos)
        column = jnp.dot(vertical_mixing, jnp.tanh(atmos).reshape(LA, -1), precision=lax.Precision.HIGHEST)
        atmos = atmos + DIFFUSE * (beside - 4.0 * atmos) + TENDENCY * column.reshape(atmos.shape)
    fluxes = jnp.dot(flux_coupling, atmos.reshape(LA, -1), precision=lax.Precision.HIGHEST)
    target = jnp.broadcast_to((jnp.arange(NXO, dtype=jnp.int32) // OXD)[:, None], (NXO, NYO)).astype(jnp.int32)
    forcing = jnp.zeros((FLD, NXO, NYO), jnp.float32)
    flat_list = []
    for margin in range(K):
        slot = margin_slot[margin]
        source = (slot // CAP).astype(jnp.int32)
        rank_ids = (slot % CAP).astype(jnp.int32)
        local = request_cells[source, target, rank_ids].astype(jnp.int32)
        flat = ((local // AYD) * NYA + source * AYD + local % AYD).astype(jnp.int32)
        flat_list.append(flat)
        forcing = forcing + margin_weight[margin][None] * fluxes[:, flat]
    wetness = sea_mask.astype(jnp.float32)[None]
    ocean_now = ocean_state
    for substep in range(SUB):
        beside = neighbours(ocean_now)
        ocean_now = wetness * (ocean_now + OCEAN_MIX * (beside - 4.0 * ocean_now) + FORCING * forcing)
    returned = jnp.zeros((FLD, NXA * NYA), jnp.float32)
    for margin in range(K):
        returned = returned.at[:, flat_list[margin]].add(margin_weight[margin][None] * ocean_now)
    return atmos, ocean_now, returned.reshape(FLD, NXA, NYA)
```

```python
import functools

import jax
import jax.numpy as jnp
from jax import lax
from jax.experimental import pallas as pl
from jax.experimental.pallas import tpu as pltpu
from jax.sharding import PartitionSpec as P

ASUB = 2
SUB = 8


DIFFUSE = 0.2
TENDENCY = 0.25
OCEAN_MIX = 0.2
FORCING = 0.15


def with_halo(cells, sides, width):
    for axis, dim in sides:
        count = lax.axis_size(axis)
        ends = count - 1
        head = lax.slice_in_dim(cells, 0, width, axis=dim)
        tail = lax.slice_in_dim(cells, cells.shape[dim] - width, cells.shape[dim], axis=dim)
        cells = jnp.concatenate(
            [
                lax.ppermute(tail, axis, [(i, (i + 1) % count) for i in range(ends)]),
                cells,
                lax.ppermute(head, axis, [((i + 1) % count, i) for i in range(ends)]),
            ],
            axis=dim,
        )
    return cells


def atmos_step(atmos, mixing_rows):
    lev_local = atmos.shape[0]
    padded = with_halo(atmos, ((("space", "comp"), 2),), 1)
    padded = jnp.pad(padded, ((0, 0), (1, 1), (0, 0)))
    beside = padded[:, 2:, 1:-1] + padded[:, :-2, 1:-1] + padded[:, 1:-1, 2:] + padded[:, 1:-1, :-2]
    shaded = jnp.tanh(atmos).reshape(lev_local, -1)
    column = jnp.dot(
        mixing_rows,
        lax.all_gather(shaded, "lev", axis=0, tiled=True),
        precision=lax.Precision.HIGHEST,
    )
    return atmos + DIFFUSE * (beside - 4.0 * atmos) + TENDENCY * column.reshape(atmos.shape)


def advance(padded, wetness, forcing):
    centre = padded[:, 1:-1, 1:-1]
    beside = padded[:, 2:, 1:-1] + padded[:, :-2, 1:-1] + padded[:, 1:-1, 2:] + padded[:, 1:-1, :-2]
    return wetness[None] * (centre + OCEAN_MIX * (beside - 4.0 * centre) + FORCING * forcing)


def shards_by_neighbours(
    atmos_state,
    ocean_state,
    vertical_mixing,
    flux_coupling,
    request_cells,
    margin_slot,
    margin_weight,
    sea_mask,
):
    lev_local, rows_atmos, cols_atmos = atmos_state.shape
    fields_local = ocean_state.shape[0]
    margins = margin_slot.shape[0]
    lev_place = lax.axis_index("lev")
    mixing_rows = lax.dynamic_slice_in_dim(vertical_mixing, lev_place * lev_local, lev_local, 0)
    coupling_cols = lax.dynamic_slice_in_dim(flux_coupling, lev_place * lev_local, lev_local, 1)
    atmos = atmos_state
    for substep in range(ASUB):
        atmos = atmos_step(atmos, mixing_rows)
    flat_atmos = atmos.reshape(lev_local, -1)
    fluxes = lax.psum_scatter(
        jnp.dot(coupling_cols, flat_atmos, precision=lax.Precision.HIGHEST),
        "lev",
        scatter_dimension=0,
        tiled=True,
    )
    requests = request_cells.reshape(-1)
    outgoing = jnp.take(fluxes, requests, axis=1)
    slot_flat = margin_slot.reshape(-1)
    weight_flat = margin_weight.reshape(margins, -1)
    received = lax.all_to_all(outgoing, ("space", "comp"), split_axis=1, concat_axis=1, tiled=True)
    picked = jnp.take(received, slot_flat, axis=1).reshape(received.shape[0], margins, -1)
    remapped = jnp.sum(picked * weight_flat[None], axis=1)
    forcing = remapped.reshape(ocean_state.shape)
    wetness = sea_mask.astype(jnp.float32)
    ocean_now = ocean_state
    for substep in range(SUB):
        padded = with_halo(ocean_now, ((("space", "comp"), 1),), 1)
        padded = jnp.pad(padded, ((0, 0), (0, 0), (1, 1)))
        ocean_now = advance(padded, wetness, forcing)
    weighted = (weight_flat[None] * ocean_now).reshape(fields_local, -1)
    outgoing_back = (
        jnp.zeros((fields_local, requests.shape[0]), jnp.float32).at[:, slot_flat].add(weighted)
    )
    arrived = lax.all_to_all(
        outgoing_back, ("space", "comp"), split_axis=1, concat_axis=1, tiled=True
    )
    returned = (
        jnp.zeros((fields_local, rows_atmos * cols_atmos), jnp.float32).at[:, requests].add(arrived)
    )
    return (atmos, ocean_now, returned.reshape(fields_local, rows_atmos, cols_atmos))


LANES = 128
HALF = 64
ROWS = 8
BLOCK = 32
EDGE = 16
AT_EDGES = 16
AT_REQUESTS = 24


def lane_of(shape=(ROWS, LANES)):
    return lax.broadcasted_iota(jnp.int32, shape, len(shape) - 1)


def pick_lanes(tile, lanes):
    return jnp.take_along_axis(tile, lanes, axis=1, mode="promise_in_bounds")


def rows_down(tile):
    row = lax.broadcasted_iota(jnp.int32, tile.shape, 0)
    return jnp.where(row == 0, 0.0, pltpu.roll(tile, 1, 0))


def rows_up(tile):
    row = lax.broadcasted_iota(jnp.int32, tile.shape, 0)
    return jnp.where(row == tile.shape[0] - 1, 0.0, pltpu.roll(tile, tile.shape[0] - 1, 0))


def place(peers_comp):
    return lax.axis_index("space") * peers_comp + lax.axis_index("comp"), lax.axis_index("lev")


def pack_kernel(peers, peers_comp, ocean_ref, slot_ref, weight_ref, mask_ref, atmos_ref, request_ref, send_ref):
    strip, lev = place(peers_comp)
    lane = lane_of()

    def rings(cells):
        tiles = [cells[:, LANES * t : LANES * (t + 1)] for t in range(peers // 2)]
        beyond = jnp.zeros_like(tiles[0])
        turned = [pltpu.roll(tile, HALF, 1) for tile in tiles]
        place_in = lane[: cells.shape[0]]
        out = []
        for t in range(peers // 2):
            before = tiles[t - 1] if t > 0 else beyond
            after = turned[t + 1] if t + 1 < peers // 2 else beyond
            out.append(jnp.where(place_in < 96, tiles[t], before))
            out.append(jnp.where((place_in >= 64) & (place_in < 96), after, turned[t]))
        return out

    ocean = rings(ocean_ref[:, 0, :])
    slot = rings(slot_ref[:, 0, :].astype(jnp.float32))
    weight = rings(weight_ref[:, 0, :])
    mask = rings(mask_ref[...].astype(jnp.float32))
    to_right = jnp.zeros((ROWS, LANES), jnp.float32)
    to_left = jnp.zeros((ROWS, LANES), jnp.float32)
    for group in range(LANES // EDGE):
        tile = atmos_ref[group // 2, ROWS * (group % 2) : ROWS * (group % 2 + 1), :]
        here = lane // EDGE == group
        to_right = jnp.where(here, pltpu.roll(tile, EDGE * (group + 1) % LANES, 1), to_right)
        to_left = jnp.where(here, pltpu.roll(tile, EDGE * group, 1) if group else tile, to_left)
    requests = request_ref[0].astype(jnp.float32)
    requests = jnp.where(lev == 0, requests[:, :LANES], requests[:, LANES:])
    for peer in range(peers):
        edges = jnp.where(strip < peer, to_right, to_left)
        same = (peer * 2 + lev) * BLOCK
        other = (peer * 2 + 1 - lev) * BLOCK
        send_ref[pl.ds(same, 8), :] = ocean[peer]
        send_ref[pl.ds(other, 4), :] = slot[peer]
        send_ref[pl.ds(other + 4, 4), :] = weight[peer]
        send_ref[pl.ds(other + 8, 8), :] = jnp.broadcast_to(mask[peer], (ROWS, LANES))
        for block in range(2):
            send_ref[pl.ds((peer * 2 + block) * BLOCK + AT_EDGES, 8), :] = edges
            send_ref[pl.ds((peer * 2 + block) * BLOCK + AT_REQUESTS, 8), :] = requests
        send_ref[pl.ds(same + 8, 8), :] = jnp.zeros((ROWS, LANES), jnp.float32)


def column_kernel(
    peers,
    peers_comp,
    mixing_ref,
    coupling_ref,
    got_ref,
    own_ref,
    beside_ref,
    request_ref,
    atmos_ref,
    returned_ref,
    send_ref,
    state_ref,
    flux_ref,
):
    strip, lev = place(peers_comp)
    lane = lane_of()
    row = lax.broadcasted_iota(jnp.int32, (ROWS, LANES), 0)
    levels = 8
    half = levels // 2
    left = jnp.maximum(strip - 1, 0)
    right = jnp.minimum(strip + 1, peers - 1)

    for level in range(half):
        state_ref[lev * half + level, :, :LANES] = own_ref[level]
        state_ref[(1 - lev) * half + level, :, :LANES] = beside_ref[level]
    exists = jnp.where(lane < HALF, strip + 1, peers - strip) < peers
    for block in range(2):
        from_left = got_ref[pl.ds((left * 2 + block) * BLOCK + AT_EDGES, 8), :]
        from_right = got_ref[pl.ds((right * 2 + block) * BLOCK + AT_EDGES, 8), :]
        for group in range(LANES // EDGE):
            west = pltpu.roll(from_left, LANES - EDGE * (group + 1), 1) if group < 7 else from_left
            east = pltpu.roll(from_right, LANES - EDGE * group, 1) if group else from_right
            tile = jnp.where(lane < EDGE, east, jnp.where(lane >= LANES - EDGE, west, 0.0))
            state_ref[block * half + group // 2, ROWS * (group % 2) : ROWS * (group % 2 + 1), LANES:] = jnp.where(
                exists, tile, 0.0
            )
    inside = jnp.concatenate([jnp.ones((16, LANES), jnp.float32), jnp.where(jnp.concatenate([exists] * 2, 0), 1.0, 0.0)], 1)
    atmos = [state_ref[level] for level in range(levels)]
    for substep in range(ASUB):
        shaded = [jnp.tanh(cells) for cells in atmos]
        later = []
        for level in range(levels):
            cells = atmos[level]
            beside = pltpu.roll(cells, 1, 1) + pltpu.roll(cells, 2 * LANES - 1, 1) + rows_down(cells) + rows_up(cells)
            column = sum(mixing_ref[level, other] * shaded[other] for other in range(levels))
            cells = cells + DIFFUSE * (beside - 4.0 * cells) + TENDENCY * column
            later.append(inside * cells)
        atmos = later
    for level in range(levels):
        state_ref[level] = atmos[level]
    for level in range(half):
        atmos_ref[level] = state_ref[lev * half + level, :, :LANES]

    fields = 8
    for field in range(fields):
        flux = sum(coupling_ref[level, lev * fields + field] * atmos[level] for level in range(levels))
        for tile in range(2):
            flux_ref[tile, pl.ds(field * BLOCK, 8), :] = jnp.zeros((ROWS, LANES), jnp.float32)
            flux_ref[tile, pl.ds(field * BLOCK + 8, 16), :] = flux[:, LANES * tile : LANES * (tile + 1)]
            flux_ref[tile, pl.ds(field * BLOCK + 24, 8), :] = jnp.zeros((ROWS, LANES), jnp.float32)

    own_table = request_ref[0].astype(jnp.float32)
    tables = [(own_table[:, :LANES], own_table[:, LANES:])]
    for peer in (right, left):
        tables.append(tuple(got_ref[pl.ds((peer * 2 + block) * BLOCK + AT_REQUESTS, 8), :] for block in range(2)))
    first = ((2 * row - 1) * LANES + 2 * (lane & (HALF - 1))).astype(jnp.float32)

    def table_row(which):
        return got_ref[pl.ds((1 - lev) * BLOCK + which, ROWS, stride=2 * BLOCK), :]

    both = lane >> 1
    named = [[jnp.zeros((ROWS, LANES), jnp.float32) for _ in range(2)] for _ in range(4)]
    for margin in range(4):
        rank = table_row(margin).astype(jnp.int32) & (2 * LANES - 1)
        late = rank >= LANES
        rank = rank & (LANES - 1)
        cells = [jnp.where(late, pick_lanes(high, rank), pick_lanes(low, rank)) for low, high in tables]
        cell = jnp.where(lane < 64, cells[0], jnp.where(lane < 96, cells[1], cells[2])) - first
        weight = table_row(4 + margin)
        for tile in range(2):
            beyond = pick_lanes(cell, both + HALF * tile) - (lane & 1).astype(jnp.float32)
            share = pick_lanes(weight, both + HALF * tile)
            for near in range(4):
                named[near][tile] = named[near][tile] + jnp.where(beyond == float(near * LANES), share, 0.0)

    wetness = table_row(8)
    ocean = []
    forcing = []
    even = (2 * lane) & (LANES - 1)
    for field in range(fields):
        pairs = []
        for tile in range(2):
            total = sum(
                named[near][tile]
                * flux_ref[tile, pl.ds(field * BLOCK + 7 + near, ROWS, stride=2), :]
                for near in range(4)
            )
            pairs.append(pick_lanes(total + pltpu.roll(total, LANES - 1, 1), even))
        forcing.append(wetness * (FORCING * jnp.where(lane < HALF, pairs[0], pairs[1])))
        ocean.append(got_ref[pl.ds(lev * BLOCK + field, ROWS, stride=2 * BLOCK), :])
    for substep in range(SUB):
        for field in range(fields):
            cells = ocean[field]
            beside = pltpu.roll(cells, 1, 1) + pltpu.roll(cells, LANES - 1, 1) + rows_down(cells) + rows_up(cells)
            ocean[field] = wetness * (cells + OCEAN_MIX * (beside - 4.0 * cells)) + forcing[field]
    for field in range(fields):
        cells = ocean[field]
        send_ref[pl.ds(field, ROWS, stride=fields), :] = jnp.where(strip % 2 == 0, cells, pltpu.roll(cells, HALF, 1))
        spread = pick_lanes(cells, both)
        upper = named[1][0] * spread + rows_down(named[3][0] * spread)
        lower = named[2][0] * spread + rows_up(named[0][0] * spread)
        returned_ref[pl.ds(field * 16, ROWS, stride=2), :] = upper
        returned_ref[pl.ds(field * 16 + 1, ROWS, stride=2), :] = lower


def rows_kernel(peers, got_ref, ocean_ref):
    lane = lane_of()
    for tile in range(peers // 2):
        pair = [got_ref[ROWS * strip : ROWS * (strip + 1), :] for strip in (2 * tile, 2 * tile + 1)]
        ocean_ref[:, 0, LANES * tile : LANES * (tile + 1)] = jnp.where(lane < HALF, pair[0], pair[1])


def shards_by_columns(
    atmos_state,
    ocean_state,
    vertical_mixing,
    flux_coupling,
    request_cells,
    margin_slot,
    margin_weight,
    sea_mask,
):
    peers_comp = lax.axis_size("comp")
    peers = lax.axis_size("space") * peers_comp
    vmem = pl.BlockSpec(memory_space=pltpu.VMEM)
    smem = pl.BlockSpec(memory_space=pltpu.SMEM)
    values = functools.partial(jax.ShapeDtypeStruct, dtype=jnp.float32)
    beside = lax.ppermute(atmos_state, "lev", [(0, 1), (1, 0)])
    outgoing = pl.pallas_call(
        functools.partial(pack_kernel, peers, peers_comp),
        out_shape=values((2 * peers * BLOCK, LANES)),
        in_specs=[vmem] * 6,
        out_specs=vmem,
    )(ocean_state, margin_slot, margin_weight, sea_mask, atmos_state, request_cells)
    received = lax.all_to_all(outgoing, ("space", "comp", "lev"), split_axis=0, concat_axis=0, tiled=True)
    atmos, returned, ocean_rows = pl.pallas_call(
        functools.partial(column_kernel, peers, peers_comp),
        out_shape=(values(atmos_state.shape), values((8 * 16, LANES)), values((peers * ROWS, LANES))),
        in_specs=[smem] * 2 + [vmem] * 4,
        out_specs=(vmem,) * 3,
        scratch_shapes=[pltpu.VMEM((8, 16, 2 * LANES), jnp.float32), pltpu.VMEM((2, 8 * BLOCK, LANES), jnp.float32)],
    )(vertical_mixing, flux_coupling.T, received, atmos_state, beside, request_cells)
    gathered = lax.all_to_all(ocean_rows, ("space", "comp"), split_axis=0, concat_axis=0, tiled=True)
    ocean = pl.pallas_call(
        functools.partial(rows_kernel, peers),
        out_shape=values(ocean_state.shape),
        in_specs=[vmem],
        out_specs=vmem,
    )(gathered)
    return (atmos, ocean, returned.reshape(8, 16, LANES))


def shards(*arguments):
    atmos_state, ocean_state, mixing, coupling, request_cells, margin_slot = arguments[:6]
    peers = lax.axis_size("space") * lax.axis_size("comp")
    by_columns = (
        lax.axis_size("lev") == 2
        and peers == ROWS
        and atmos_state.shape == (4, 2 * ROWS, LANES)
        and ocean_state.shape == (8, 1, HALF * peers)
        and request_cells.shape == (1, peers, 2 * LANES)
        and margin_slot.shape[0] == 4
    )
    return (shards_by_columns if by_columns else shards_by_neighbours)(*arguments)


def solution(mesh):
    placed = (
        P(("parts", "lev"), None, ("space", "comp")),
        P(("parts", "lev"), ("space", "comp"), None),
        P(),
        P(),
        P(("space", "comp"), None, None),
        P(None, ("space", "comp"), None),
        P(None, ("space", "comp"), None),
        P(("space", "comp"), None),
    )
    return jax.shard_map(
        shards,
        mesh=mesh,
        in_specs=placed,
        out_specs=(
            P(("parts", "lev"), None, ("space", "comp")),
            P(("parts", "lev"), ("space", "comp"), None),
            P(("parts", "lev"), None, ("space", "comp")),
        ),
        check_vma=False,
    )
```

```python
import jax
import jax.numpy as jnp
from jax import lax
from jax.experimental import pallas as pl
from jax.experimental.pallas import tpu as pltpu
from jax.sharding import PartitionSpec as P

ASUB = 2
SUB = 8


DIFFUSE = 0.2
TENDENCY = 0.25
OCEAN_MIX = 0.2
FORCING = 0.15


def with_halo(cells, sides, width):
    for axis, dim in sides:
        count = lax.axis_size(axis)
        ends = count - 1
        head = lax.slice_in_dim(cells, 0, width, axis=dim)
        tail = lax.slice_in_dim(cells, cells.shape[dim] - width, cells.shape[dim], axis=dim)
        cells = jnp.concatenate(
            [
                lax.ppermute(tail, axis, [(i, (i + 1) % count) for i in range(ends)]),
                cells,
                lax.ppermute(head, axis, [((i + 1) % count, i) for i in range(ends)]),
            ],
            axis=dim,
        )
    return cells


def atmos_step(atmos, mixing_rows):
    lev_local = atmos.shape[0]
    padded = with_halo(atmos, ((("space", "comp"), 2),), 1)
    padded = jnp.pad(padded, ((0, 0), (1, 1), (0, 0)))
    beside = padded[:, 2:, 1:-1] + padded[:, :-2, 1:-1] + padded[:, 1:-1, 2:] + padded[:, 1:-1, :-2]
    shaded = jnp.tanh(atmos).reshape(lev_local, -1)
    column = jnp.dot(
        mixing_rows,
        lax.all_gather(shaded, "lev", axis=0, tiled=True),
        precision=lax.Precision.HIGHEST,
    )
    return atmos + DIFFUSE * (beside - 4.0 * atmos) + TENDENCY * column.reshape(atmos.shape)


def advance(padded, wetness, forcing):
    centre = padded[:, 1:-1, 1:-1]
    beside = padded[:, 2:, 1:-1] + padded[:, :-2, 1:-1] + padded[:, 1:-1, 2:] + padded[:, 1:-1, :-2]
    return wetness[None] * (centre + OCEAN_MIX * (beside - 4.0 * centre) + FORCING * forcing)


def shards_by_neighbours(
    atmos_state,
    ocean_state,
    vertical_mixing,
    flux_coupling,
    request_cells,
    margin_slot,
    margin_weight,
    sea_mask,
):
    lev_local, rows_atmos, cols_atmos = atmos_state.shape
    fields_local = ocean_state.shape[0]
    margins = margin_slot.shape[0]
    lev_place = lax.axis_index("lev")
    mixing_rows = lax.dynamic_slice_in_dim(vertical_mixing, lev_place * lev_local, lev_local, 0)
    coupling_cols = lax.dynamic_slice_in_dim(flux_coupling, lev_place * lev_local, lev_local, 1)
    atmos = atmos_state
    for substep in range(ASUB):
        atmos = atmos_step(atmos, mixing_rows)
    flat_atmos = atmos.reshape(lev_local, -1)
    fluxes = lax.psum_scatter(
        jnp.dot(coupling_cols, flat_atmos, precision=lax.Precision.HIGHEST),
        "lev",
        scatter_dimension=0,
        tiled=True,
    )
    requests = request_cells.reshape(-1)
    outgoing = jnp.take(fluxes, requests, axis=1)
    slot_flat = margin_slot.reshape(-1)
    weight_flat = margin_weight.reshape(margins, -1)
    received = lax.all_to_all(outgoing, ("space", "comp"), split_axis=1, concat_axis=1, tiled=True)
    picked = jnp.take(received, slot_flat, axis=1).reshape(received.shape[0], margins, -1)
    remapped = jnp.sum(picked * weight_flat[None], axis=1)
    forcing = remapped.reshape(ocean_state.shape)
    wetness = sea_mask.astype(jnp.float32)
    ocean_now = ocean_state
    for substep in range(SUB):
        padded = with_halo(ocean_now, ((("space", "comp"), 1),), 1)
        padded = jnp.pad(padded, ((0, 0), (0, 0), (1, 1)))
        ocean_now = advance(padded, wetness, forcing)
    weighted = (weight_flat[None] * ocean_now).reshape(fields_local, -1)
    outgoing_back = (
        jnp.zeros((fields_local, requests.shape[0]), jnp.float32).at[:, slot_flat].add(weighted)
    )
    arrived = lax.all_to_all(
        outgoing_back, ("space", "comp"), split_axis=1, concat_axis=1, tiled=True
    )
    returned = (
        jnp.zeros((fields_local, rows_atmos * cols_atmos), jnp.float32).at[:, requests].add(arrived)
    )
    return (atmos, ocean_now, returned.reshape(fields_local, rows_atmos, cols_atmos))


LANES = 128
HALF = 64
ROWS = 8
LEVELS = 8
FIELDS = 8
MARGINS = 4
TABLE = 24
PACKED = 16
TABLES = 4 * TABLE
AT_LEFT = 16
AT_REQUEST = 32
AT_LEVELS = 48
SHEET = 112
AT_EDGE = 2 * TABLE
AT_ASKED = AT_EDGE + 16
LETTER = AT_ASKED + 16
EDGE = 16
WIDE = 32
VMEM_LIMIT = 4 * 1024 * 1024


def lane_of(shape=(ROWS, LANES)):
    return lax.broadcasted_iota(jnp.int32, shape, 1)


def row_of(shape=(ROWS, LANES)):
    return lax.broadcasted_iota(jnp.int32, shape, 0)


def pick_lanes(tile, lanes):
    return jnp.take_along_axis(tile, lanes, axis=1, mode="promise_in_bounds")


def turn(tile, by):
    by = by % tile.shape[1]
    return pltpu.roll(tile, by, 1) if by else tile


def rows_down(tile):
    return jnp.where(row_of(tile.shape) == 0, 0.0, pltpu.roll(tile, 1, 0))


def rows_up(tile):
    last = tile.shape[0] - 1
    return jnp.where(row_of(tile.shape) == last, 0.0, pltpu.roll(tile, last, 0))


def place():
    return lax.axis_index("space"), lax.axis_index("comp"), lax.axis_index("lev")


def tables_kernel(*refs):
    arrays, (tables_ref, factors_ref, levels_ref, asked_ref), held, arrived = refs[:8], refs[8:12], refs[12:-1], refs[-1]
    copies = [pltpu.make_async_copy(a, h, arrived.at[i]) for i, (a, h) in enumerate(zip(arrays, held))]
    for copy in copies:
        copy.start()
    for copy in copies:
        copy.wait()
    ocean_ref, slot_ref, weight_ref, mask_ref, atmos_ref, request_ref, mixing_ref, coupling_ref = held
    space, comp, lev = place()
    lane, row = lane_of(), row_of()
    near = (lane < EDGE // 2) | (lane >= LANES - EDGE // 2)

    def halo(tiles, z):
        beyond = jnp.zeros_like(tiles[0])
        east = tiles[z + 1] if z + 1 < len(tiles) else beyond
        west = tiles[z - 1] if z > 0 else beyond
        wide = lane[: beyond.shape[0]]
        return jnp.where(near[: beyond.shape[0]], jnp.where(wide < HALF, east, west), 0.0)

    def packed(cells):
        spread = [jnp.where(row == i, turn(cells, EDGE * i), 0.0) for i in range(ROWS)]
        return jnp.sum(sum(spread), axis=0, keepdims=True)

    def tiles_of(cells):
        return [cells[:, LANES * z : LANES * (z + 1)] for z in range(4)]

    ocean = tiles_of(ocean_ref[:, 0, :])
    table = tiles_of(jnp.concatenate([slot_ref[:, 0, :].astype(jnp.float32), weight_ref[:, 0, :]], 0))
    mask = tiles_of(mask_ref[...].astype(jnp.float32))
    for z in range(4):
        base = (z ^ space) * TABLE
        tables_ref[pl.ds(base, 8), :] = ocean[z]
        tables_ref[pl.ds(base + 8, 8), :] = table[z]
        last = jnp.where(row == 0, packed(halo(ocean, z)), 0.0)
        last = jnp.where(row == 1, packed(halo(table, z)), last)
        last = jnp.where(row == 2, mask[z], last)
        tables_ref[pl.ds(base + PACKED, 8), :] = jnp.where(row == 3, halo(mask, z), last)
    for other in range(LEVELS):
        factors_ref[LEVELS * other : LEVELS * (other + 1), :] = jnp.broadcast_to(
            mixing_ref[:, other : other + 1], (ROWS, LANES)
        )
    for field in range(FIELDS):
        mine = [coupling_ref[:, FIELDS * i + field : FIELDS * i + field + 1] for i in range(2)]
        at = LEVELS * (LEVELS + field)
        factors_ref[at : at + LEVELS, :] = jnp.broadcast_to(jnp.where(lev == 0, mine[0], mine[1]), (ROWS, LANES))
    levels_ref[...] = atmos_ref[...]
    requests = request_ref[0].astype(jnp.float32)
    asked_ref[:ROWS, :] = requests[:, :LANES]
    asked_ref[ROWS:, :] = requests[:, LANES:]


def sheet_kernel(levels_ref, other_ref, asked_ref, sheet_ref):
    space, comp, lev = place()
    lane = lane_of()
    for block, ref in ((lev, levels_ref), (1 - lev, other_ref)):
        to_right = jnp.zeros((ROWS, LANES), jnp.float32)
        to_left = jnp.zeros((ROWS, LANES), jnp.float32)
        for group in range(LANES // EDGE):
            tile = ref[group // 2, ROWS * (group % 2) : ROWS * (group % 2 + 1), :]
            here = lane // EDGE == group
            to_right = jnp.where(here, turn(tile, EDGE * (group + 1)), to_right)
            to_left = jnp.where(here, turn(tile, EDGE * group), to_left)
        sheet_ref[pl.ds(ROWS * block, 8), :] = to_right
        sheet_ref[pl.ds(AT_LEFT + ROWS * block, 8), :] = to_left
    sheet_ref[AT_REQUEST:AT_LEVELS, :] = asked_ref[...]
    for level in range(LEVELS // 2):
        at = AT_LEVELS + 2 * ROWS * level
        sheet_ref[at : at + 2 * ROWS, :] = levels_ref[level]


def letter_kernel(own_tables_ref, own_sheet_ref, beside_tables_ref, beside_sheet_ref, *letter_refs):
    space, comp, lev = place()
    sheets = (own_sheet_ref, beside_sheet_ref)
    for k in (1, 2, 3):
        letter_ref = letter_refs[k - 1]
        letter_ref[:TABLE, :] = own_tables_ref[TABLE * k : TABLE * (k + 1), :]
        letter_ref[TABLE : 2 * TABLE, :] = beside_tables_ref[TABLE * k : TABLE * (k + 1), :]
        east = (space ^ k) > space
        mine = comp == jnp.where(east, 1, 0)
        edges = [jnp.where(east, ref[:AT_LEFT, :], ref[AT_LEFT:AT_REQUEST, :]) for ref in sheets]
        asked = [ref[AT_REQUEST:AT_LEVELS, :] for ref in sheets]
        letter_ref[AT_EDGE:AT_ASKED, :] = jnp.where(mine, edges[0], edges[1])
        letter_ref[AT_ASKED:LETTER, :] = jnp.where(mine, asked[0], asked[1])


def margins_kernel(
    own_ref,
    beside_ref,
    own_sheet_ref,
    beside_sheet_ref,
    one_ref,
    two_ref,
    three_ref,
    ocean_ref,
    wet_ref,
    named_ref,
    rows_ref,
):
    space, comp, lev = place()
    strip = 2 * space + comp
    lane, row = lane_of(), row_of()
    blocks = [(own_ref, 0), (beside_ref, 0)]
    for ref in (one_ref, two_ref, three_ref):
        blocks += [(ref, 0), (ref, TABLE)]
    for m, (ref, start) in enumerate(blocks):
        rows_ref[pl.ds((m ^ strip) * TABLE, TABLE), :] = ref[start : start + TABLE, :]

    def table_row(which):
        return rows_ref[pl.ds(which, ROWS, stride=TABLE), :]

    ocean_halo = table_row(PACKED)
    for field in range(FIELDS):
        ocean_ref[field, :, :LANES] = table_row(field)
        ocean_ref[field, :, LANES:] = turn(ocean_halo, -EDGE * field)
    near = (lane < EDGE // 2) | (lane >= LANES - EDGE // 2)
    wet_ref[:, :LANES] = table_row(PACKED + 2)
    wet_ref[:, LANES:] = jnp.where(near, table_row(PACKED + 3), 0.0)

    even = space % 2 == 0
    own = [own_sheet_ref[AT_REQUEST + 8 * i : AT_REQUEST + 8 * (i + 1), :] for i in range(2)]
    beside = [beside_sheet_ref[AT_REQUEST + 8 * i : AT_REQUEST + 8 * (i + 1), :] for i in range(2)]
    one = [one_ref[AT_ASKED + 8 * i : AT_ASKED + 8 * (i + 1), :] for i in range(2)]
    three = [three_ref[AT_ASKED + 8 * i : AT_ASKED + 8 * (i + 1), :] for i in range(2)]

    def either(first_is, first, second):
        return [jnp.where(first_is, a, b) for a, b in zip(first, second)]

    tables = (
        (either(comp == 0, own, beside), either(comp == 0, beside, own)),
        (either(even, one, three), either(even, three, one)),
    )
    first = ((2 * row - 1) * LANES + 2 * (lane & (HALF - 1))).astype(jnp.float32)
    parity = (lane & 1).astype(jnp.float32)
    pairs = lane >> 1
    spread = ((0, pairs), (0, pairs + HALF), (1, jnp.where(lane < HALF, pairs, pairs + HALF)))
    table_halo = table_row(PACKED + 1)
    named = [[jnp.zeros((ROWS, LANES), jnp.float32) for _ in range(3)] for _ in range(4)]
    for margin in range(MARGINS):
        slots = (table_row(8 + margin), turn(table_halo, -EDGE * margin))
        weights = (table_row(8 + MARGINS + margin), turn(table_halo, -EDGE * (MARGINS + margin)))
        cells = []
        for slot, (low_strip, high_strip) in zip(slots, tables):
            rank = slot.astype(jnp.int32) & (2 * LANES - 1)
            late = rank >= LANES
            rank = rank & (LANES - 1)
            found = [jnp.where(late, pick_lanes(high, rank), pick_lanes(low, rank)) for low, high in (low_strip, high_strip)]
            cells.append(jnp.where(lane < HALF, found[0], found[1]) - first)
        for tile, (ring, lanes) in enumerate(spread):
            beyond = pick_lanes(cells[ring], lanes) - parity
            share = pick_lanes(weights[ring], lanes)
            for step in range(4):
                named[step][tile] = named[step][tile] + jnp.where(beyond == float(step * LANES), share, 0.0)
    for step in range(4):
        for tile in range(3):
            named_ref[step, tile] = named[step][tile]


def column_kernel(
    factors_ref,
    own_ref,
    own_other_ref,
    beside_ref,
    beside_other_ref,
    one_ref,
    three_ref,
    ocean_ref,
    wet_ref,
    named_ref,
    atmos_ref,
    final_ref,
    first_ref,
    second_ref,
    third_ref,
    fourth_ref,
    state_ref,
    flux_ref,
    back_ref,
):
    space, comp, lev = place()
    lane, row = lane_of(), row_of()
    half = LEVELS // 2

    mine = pl.ds(pl.multiple_of(comp * LANES, LANES), LANES)
    theirs = pl.ds(pl.multiple_of((1 - comp) * LANES, LANES), LANES)
    for level in range(half):
        here, there = lev * half + level, (1 - lev) * half + level
        state_ref[here, :, mine] = own_ref[level]
        state_ref[there, :, mine] = own_other_ref[level]
        at = 2 * ROWS * level
        state_ref[here, :, theirs] = beside_ref[AT_LEVELS + at : AT_LEVELS + at + 2 * ROWS, :]
        state_ref[there, :, theirs] = beside_other_ref[at : at + 2 * ROWS, :]
    even = space % 2 == 0
    exists = jnp.where(lane < HALF, space + 1, 4 - space) < 4
    for block in range(2):
        one, three = [ref[AT_EDGE + ROWS * block : AT_EDGE + ROWS * (block + 1), :] for ref in (one_ref, three_ref)]
        east, west = jnp.where(even, one, three), jnp.where(even, three, one)
        for group in range(LANES // EDGE):
            tile = jnp.where(
                lane < EDGE,
                turn(east, -EDGE * group),
                jnp.where(lane >= LANES - EDGE, turn(west, -EDGE * (group + 1)), 0.0),
            )
            state_ref[block * half + group // 2, ROWS * (group % 2) : ROWS * (group % 2 + 1), 2 * LANES :] = jnp.where(
                exists, tile, 0.0
            )
    edge_inside = jnp.where(jnp.concatenate([exists] * 2, 0), 1.0, 0.0)
    inside = jnp.concatenate([jnp.ones((2 * ROWS, 2 * LANES), jnp.float32), edge_inside], 1)

    def factor(which):
        return jnp.broadcast_to(jnp.concatenate([factors_ref[which : which + 1, :]] * 3, 1), (2 * ROWS, 3 * LANES))

    atmos = [state_ref[level] for level in range(LEVELS)]
    for substep in range(ASUB):
        shaded = [jnp.tanh(cells) for cells in atmos]
        later = []
        for level in range(LEVELS):
            cells = atmos[level]
            beside = turn(cells, 1) + turn(cells, -1) + rows_down(cells) + rows_up(cells)
            column = sum(factor(LEVELS * other + level) * shaded[other] for other in range(LEVELS))
            cells = cells + DIFFUSE * (beside - 4.0 * cells) + TENDENCY * column
            later.append(inside * cells)
        atmos = later
    for level in range(LEVELS):
        state_ref[level] = atmos[level]
    for level in range(half):
        atmos_ref[level] = state_ref[lev * half + level, :, mine]

    for field in range(FIELDS):
        flux = sum(factor(LEVELS * (LEVELS + field) + level) * atmos[level] for level in range(LEVELS))
        for tile in range(3):
            flux_ref[tile, WIDE * field : WIDE * field + 8, :] = jnp.zeros((ROWS, LANES), jnp.float32)
            flux_ref[tile, WIDE * field + 8 : WIDE * field + 24, :] = flux[:, LANES * tile : LANES * (tile + 1)]
            flux_ref[tile, WIDE * field + 24 : WIDE * field + 32, :] = jnp.zeros((ROWS, LANES), jnp.float32)

    wetness = wet_ref[...]
    pairs = (2 * lane) & (LANES - 1)
    ocean = []
    forcing = []
    for field in range(FIELDS):
        sums = []
        for tile in range(3):
            total = sum(
                named_ref[step, tile] * flux_ref[tile, pl.ds(WIDE * field + 7 + step, ROWS, stride=2), :] for step in range(4)
            )
            sums.append(pick_lanes(total + turn(total, -1), pairs))
        remapped = jnp.concatenate([jnp.where(lane < HALF, sums[0], sums[1]), sums[2]], 1)
        forcing.append(wetness * (FORCING * remapped))
        ocean.append(ocean_ref[field])
    for substep in range(SUB):
        for field in range(FIELDS):
            cells = ocean[field]
            beside = turn(cells, 1) + turn(cells, -1) + rows_down(cells) + rows_up(cells)
            ocean[field] = wetness * (cells + OCEAN_MIX * (beside - 4.0 * cells)) + forcing[field]
    for field in range(FIELDS):
        cells = ocean[field][:, :LANES]
        final_ref[field] = cells
        back_ref[pl.ds(field, ROWS, stride=FIELDS), :] = cells
    for k, ref in enumerate((first_ref, second_ref, third_ref, fourth_ref)):
        ref[...] = back_ref[pl.ds((2 * (space ^ k) + comp) * FIELDS, FIELDS), :]


def returned_kernel(atmos_ref, final_ref, named_ref, atmos_next_ref, returned_ref):
    space, comp, lev = place()
    lane = lane_of()
    atmos_next_ref[...] = atmos_ref[...]
    named = [jnp.where(comp == 0, named_ref[step, 0], named_ref[step, 1]) for step in range(4)]
    pairs = (lane >> 1) + HALF * comp
    for field in range(FIELDS):
        spread = pick_lanes(final_ref[field], pairs)
        upper = named[1] * spread + rows_down(named[3] * spread)
        lower = named[2] * spread + rows_up(named[0] * spread)
        returned_ref[pl.ds(2 * ROWS * field, ROWS, stride=2), :] = upper
        returned_ref[pl.ds(2 * ROWS * field + 1, ROWS, stride=2), :] = lower


def rows_kernel(own_ref, one_ref, two_ref, three_ref, ocean_ref):
    space, comp, lev = place()
    for k, ref in enumerate((own_ref, one_ref, two_ref, three_ref)):
        ocean_ref[:, 0, pl.ds(pl.multiple_of((space ^ k) * LANES, LANES), LANES)] = ref[...]


def over(axis, k, array):
    return lax.ppermute(array, axis, [(i, i ^ k) for i in range(lax.axis_size(axis))])


def local(kernel, out_shape, spaces, scratch=()):
    single = not isinstance(out_shape, tuple)
    vmem = pl.BlockSpec(memory_space=pltpu.VMEM)
    return pl.pallas_call(
        kernel,
        out_shape=out_shape,
        in_specs=[pl.BlockSpec(memory_space=space) for space in spaces],
        out_specs=vmem if single else (vmem,) * len(out_shape),
        scratch_shapes=list(scratch),
        compiler_params=pltpu.CompilerParams(vmem_limit_bytes=VMEM_LIMIT),
    )


def shards_by_columns(
    atmos_state,
    ocean_state,
    vertical_mixing,
    flux_coupling,
    request_cells,
    margin_slot,
    margin_weight,
    sea_mask,
):
    def values(*shape):
        return jax.ShapeDtypeStruct(shape, jnp.float32)

    arrays = (ocean_state, margin_slot, margin_weight, sea_mask, atmos_state, request_cells)
    arrays += (vertical_mixing, flux_coupling.T)
    own_other = over("lev", 1, atmos_state)
    tables, factors, levels, asked = local(
        tables_kernel,
        (values(TABLES, LANES), values(2 * LEVELS * LEVELS, LANES), values(*atmos_state.shape), values(2 * ROWS, LANES)),
        [pltpu.HBM] * 8,
        [pltpu.VMEM(a.shape, a.dtype) for a in arrays] + [pltpu.SemaphoreType.DMA((8,))],
    )(*(pltpu.with_memory_space_constraint(a, pltpu.HBM) for a in arrays))
    tables_beside = over("comp", 1, tables)
    sheet = local(sheet_kernel, values(SHEET, LANES), [pltpu.VMEM] * 3)(levels, own_other, asked)
    sheet_beside = over("comp", 1, sheet)
    letters = local(letter_kernel, (values(LETTER, LANES),) * 3, [pltpu.VMEM] * 4)(
        tables, sheet, tables_beside, sheet_beside
    )
    one, two, three = (over("space", k, letter) for k, letter in zip((1, 2, 3), letters))
    beside_other = over("lev", 1, sheet_beside[AT_LEVELS:])
    ocean, wet, named = local(
        margins_kernel,
        (values(FIELDS, ROWS, 2 * LANES), values(ROWS, 2 * LANES), values(4, 3, ROWS, LANES)),
        [pltpu.VMEM] * 7,
        [pltpu.VMEM((ROWS * TABLE, LANES), jnp.float32)],
    )(tables, tables_beside, sheet, sheet_beside, one, two, three)
    atmos, final, *back = local(
        column_kernel,
        (values(*atmos_state.shape), values(FIELDS, ROWS, LANES)) + (values(FIELDS, LANES),) * 4,
        [pltpu.VMEM] * 10,
        [
            pltpu.VMEM((LEVELS, 2 * ROWS, 3 * LANES), jnp.float32),
            pltpu.VMEM((3, FIELDS * WIDE, LANES), jnp.float32),
            pltpu.VMEM((ROWS * FIELDS, LANES), jnp.float32),
        ],
    )(factors, levels, own_other, sheet_beside, beside_other, one, three, ocean, wet, named)
    pieces = [over("space", k, piece) for k, piece in zip((1, 2, 3), back[1:])]
    atmos_next, returned = local(
        returned_kernel,
        (values(*atmos_state.shape), values(FIELDS * 2 * ROWS, LANES)),
        [pltpu.VMEM] * 3,
    )(atmos, final, named)
    ocean_next = local(rows_kernel, values(*ocean_state.shape), [pltpu.VMEM] * 4)(back[0], *pieces)
    return (atmos_next, ocean_next, returned.reshape(FIELDS, 2 * ROWS, LANES))


def shards(*arguments):
    atmos_state, ocean_state, mixing, coupling, request_cells, margin_slot = arguments[:6]
    by_columns = (
        (lax.axis_size("space"), lax.axis_size("comp"), lax.axis_size("lev")) == (4, 2, 2)
        and atmos_state.shape == (LEVELS // 2, 2 * ROWS, LANES)
        and ocean_state.shape == (FIELDS, 1, 4 * LANES)
        and request_cells.shape == (1, ROWS, 2 * LANES)
        and margin_slot.shape[0] == MARGINS
    )
    return (shards_by_columns if by_columns else shards_by_neighbours)(*arguments)


def solution(mesh):
    placed = (
        P(("parts", "lev"), None, ("space", "comp")),
        P(("parts", "lev"), ("space", "comp"), None),
        P(),
        P(),
        P(("space", "comp"), None, None),
        P(None, ("space", "comp"), None),
        P(None, ("space", "comp"), None),
        P(("space", "comp"), None),
    )
    return jax.shard_map(
        shards,
        mesh=mesh,
        in_specs=placed,
        out_specs=(
            P(("parts", "lev"), None, ("space", "comp")),
            P(("parts", "lev"), ("space", "comp"), None),
            P(("parts", "lev"), None, ("space", "comp")),
        ),
        check_vma=False,
    )
```

```python
import jax
import jax.numpy as jnp
from jax import lax
from jax.experimental import pallas as pl
from jax.experimental.pallas import tpu as pltpu
from jax.sharding import PartitionSpec as P

ASUB = 2
SUB = 8


DIFFUSE = 0.2
TENDENCY = 0.25
OCEAN_MIX = 0.2
FORCING = 0.15


def with_halo(cells, sides, width):
    for axis, dim in sides:
        count = lax.axis_size(axis)
        ends = count - 1
        head = lax.slice_in_dim(cells, 0, width, axis=dim)
        tail = lax.slice_in_dim(cells, cells.shape[dim] - width, cells.shape[dim], axis=dim)
        cells = jnp.concatenate(
            [
                lax.ppermute(tail, axis, [(i, (i + 1) % count) for i in range(ends)]),
                cells,
                lax.ppermute(head, axis, [((i + 1) % count, i) for i in range(ends)]),
            ],
            axis=dim,
        )
    return cells


def atmos_step(atmos, mixing_rows):
    lev_local = atmos.shape[0]
    padded = with_halo(atmos, ((("space", "comp"), 2),), 1)
    padded = jnp.pad(padded, ((0, 0), (1, 1), (0, 0)))
    beside = padded[:, 2:, 1:-1] + padded[:, :-2, 1:-1] + padded[:, 1:-1, 2:] + padded[:, 1:-1, :-2]
    shaded = jnp.tanh(atmos).reshape(lev_local, -1)
    column = jnp.dot(
        mixing_rows,
        lax.all_gather(shaded, "lev", axis=0, tiled=True),
        precision=lax.Precision.HIGHEST,
    )
    return atmos + DIFFUSE * (beside - 4.0 * atmos) + TENDENCY * column.reshape(atmos.shape)


def advance(padded, wetness, forcing):
    centre = padded[:, 1:-1, 1:-1]
    beside = padded[:, 2:, 1:-1] + padded[:, :-2, 1:-1] + padded[:, 1:-1, 2:] + padded[:, 1:-1, :-2]
    return wetness[None] * (centre + OCEAN_MIX * (beside - 4.0 * centre) + FORCING * forcing)


def shards_by_neighbours(
    atmos_state,
    ocean_state,
    vertical_mixing,
    flux_coupling,
    request_cells,
    margin_slot,
    margin_weight,
    sea_mask,
):
    lev_local, rows_atmos, cols_atmos = atmos_state.shape
    fields_local = ocean_state.shape[0]
    margins = margin_slot.shape[0]
    lev_place = lax.axis_index("lev")
    mixing_rows = lax.dynamic_slice_in_dim(vertical_mixing, lev_place * lev_local, lev_local, 0)
    coupling_cols = lax.dynamic_slice_in_dim(flux_coupling, lev_place * lev_local, lev_local, 1)
    atmos = atmos_state
    for substep in range(ASUB):
        atmos = atmos_step(atmos, mixing_rows)
    flat_atmos = atmos.reshape(lev_local, -1)
    fluxes = lax.psum_scatter(
        jnp.dot(coupling_cols, flat_atmos, precision=lax.Precision.HIGHEST),
        "lev",
        scatter_dimension=0,
        tiled=True,
    )
    requests = request_cells.reshape(-1)
    outgoing = jnp.take(fluxes, requests, axis=1)
    slot_flat = margin_slot.reshape(-1)
    weight_flat = margin_weight.reshape(margins, -1)
    received = lax.all_to_all(outgoing, ("space", "comp"), split_axis=1, concat_axis=1, tiled=True)
    picked = jnp.take(received, slot_flat, axis=1).reshape(received.shape[0], margins, -1)
    remapped = jnp.sum(picked * weight_flat[None], axis=1)
    forcing = remapped.reshape(ocean_state.shape)
    wetness = sea_mask.astype(jnp.float32)
    ocean_now = ocean_state
    for substep in range(SUB):
        padded = with_halo(ocean_now, ((("space", "comp"), 1),), 1)
        padded = jnp.pad(padded, ((0, 0), (0, 0), (1, 1)))
        ocean_now = advance(padded, wetness, forcing)
    weighted = (weight_flat[None] * ocean_now).reshape(fields_local, -1)
    outgoing_back = (
        jnp.zeros((fields_local, requests.shape[0]), jnp.float32).at[:, slot_flat].add(weighted)
    )
    arrived = lax.all_to_all(
        outgoing_back, ("space", "comp"), split_axis=1, concat_axis=1, tiled=True
    )
    returned = (
        jnp.zeros((fields_local, rows_atmos * cols_atmos), jnp.float32).at[:, requests].add(arrived)
    )
    return (atmos, ocean_now, returned.reshape(fields_local, rows_atmos, cols_atmos))


LANES = 128
HALF = 64
ROWS = 8
LEVELS = 8
FIELDS = 8
MARGINS = 4
TABLE = 24
PACKED = 16
TABLES = 4 * TABLE
AT_EDGE = TABLE
AT_ASKED = AT_EDGE + 8
LETTER = AT_ASKED + 16
AT_REQUEST = 64
STRIP = AT_REQUEST + 16
AT_HALO = 4 * TABLE
AT_HALO_ASKED = AT_HALO + 8
SHEET = AT_HALO_ASKED + 16
OTHER_HALO = TABLE
BESIDE_BLOCKS = OTHER_HALO + 8
BESIDE_HALO = BESIDE_BLOCKS + 3 * TABLE
OTHER_LEVELS = BESIDE_HALO + 8
BESIDE_LEVELS = OTHER_LEVELS + 64
EDGE = 16
WIDE = 32
VMEM_LIMIT = 4 * 1024 * 1024


def lane_of(shape=(ROWS, LANES)):
    return lax.broadcasted_iota(jnp.int32, shape, 1)


def row_of(shape=(ROWS, LANES)):
    return lax.broadcasted_iota(jnp.int32, shape, 0)


def pick_lanes(tile, lanes):
    return jnp.take_along_axis(tile, lanes, axis=1, mode="promise_in_bounds")


def turn(tile, by):
    by = by % tile.shape[1]
    return pltpu.roll(tile, by, 1) if by else tile


def rows_down(tile):
    return jnp.where(row_of(tile.shape) == 0, 0.0, pltpu.roll(tile, 1, 0))


def rows_up(tile):
    last = tile.shape[0] - 1
    return jnp.where(row_of(tile.shape) == last, 0.0, pltpu.roll(tile, last, 0))


def place():
    return lax.axis_index("space"), lax.axis_index("comp"), lax.axis_index("lev")


def tables_kernel(*refs):
    arrays, (letters_ref, factors_ref, strip_ref), held, arrived = refs[:8], refs[8:11], refs[11:-1], refs[-1]
    copies = [pltpu.make_async_copy(a, h, arrived.at[i]) for i, (a, h) in enumerate(zip(arrays, held))]
    for copy in copies:
        copy.start()
    for copy in copies:
        copy.wait()
    ocean_ref, slot_ref, weight_ref, mask_ref, atmos_ref, request_ref, mixing_ref, coupling_ref = held
    space, comp, lev = place()
    lane, row = lane_of(), row_of()
    near = (lane < EDGE // 2) | (lane >= LANES - EDGE // 2)

    def halo(tiles, z):
        beyond = jnp.zeros_like(tiles[0])
        east = tiles[z + 1] if z + 1 < len(tiles) else beyond
        west = tiles[z - 1] if z > 0 else beyond
        wide = lane[: beyond.shape[0]]
        return jnp.where(near[: beyond.shape[0]], jnp.where(wide < HALF, east, west), 0.0)

    def packed(cells):
        return jnp.sum(pltpu.roll(cells, 0, 1, stride=EDGE, stride_axis=0), axis=0, keepdims=True)

    def tiles_of(cells):
        return [cells[:, LANES * z : LANES * (z + 1)] for z in range(4)]

    ocean = tiles_of(ocean_ref[:, 0, :])
    table = tiles_of(jnp.concatenate([slot_ref[:, 0, :].astype(jnp.float32), weight_ref[:, 0, :]], 0))
    mask = tiles_of(mask_ref[...].astype(jnp.float32))
    to_right = jnp.zeros((ROWS, LANES), jnp.float32)
    to_left = jnp.zeros((ROWS, LANES), jnp.float32)
    for group in range(LANES // EDGE):
        tile = atmos_ref[group // 2, ROWS * (group % 2) : ROWS * (group % 2 + 1), :]
        here = lane // EDGE == group
        to_right = jnp.where(here, turn(tile, EDGE * (group + 1)), to_right)
        to_left = jnp.where(here, turn(tile, EDGE * group), to_left)
    edge = jnp.where(comp == 0, to_left, to_right)
    requests = request_ref[0].astype(jnp.float32)
    for z in range(4):
        k = z ^ space
        letters_ref[k, :8, :] = ocean[z]
        letters_ref[k, 8:16, :] = table[z]
        last = jnp.where(row == 0, packed(halo(ocean, z)), 0.0)
        last = jnp.where(row == 1, packed(halo(table, z)), last)
        last = jnp.where(row == 2, mask[z], last)
        letters_ref[k, PACKED:TABLE, :] = jnp.where(row == 3, halo(mask, z), last)
        letters_ref[k, AT_EDGE:AT_ASKED, :] = edge
        letters_ref[k, AT_ASKED : AT_ASKED + 8, :] = requests[:, :LANES]
        letters_ref[k, AT_ASKED + 8 :, :] = requests[:, LANES:]
    for other in range(LEVELS):
        factors_ref[LEVELS * other : LEVELS * (other + 1), :] = jnp.broadcast_to(
            TENDENCY * mixing_ref[:, other : other + 1], (ROWS, LANES)
        )
    for field in range(FIELDS):
        other = [coupling_ref[:, FIELDS * i + field : FIELDS * i + field + 1] for i in range(2)]
        at = LEVELS * (LEVELS + field)
        factors_ref[at : at + LEVELS, :] = jnp.broadcast_to(jnp.where(lev == 0, other[1], other[0]), (ROWS, LANES))
    for level in range(LEVELS // 2):
        strip_ref[2 * ROWS * level : 2 * ROWS * (level + 1), :] = atmos_ref[level]
    strip_ref[AT_REQUEST : AT_REQUEST + 8, :] = requests[:, :LANES]
    strip_ref[AT_REQUEST + 8 :, :] = requests[:, LANES:]


def sheet_kernel(own_ref, three_ref, two_ref, one_ref, sheet_ref):
    space, comp, lev = place()
    for k, ref in enumerate((own_ref, one_ref, two_ref, three_ref)):
        sheet_ref[TABLE * k : TABLE * (k + 1), :] = ref[:TABLE, :]
    near = (space + comp) % 2 == 0
    sheet_ref[AT_HALO:, :] = jnp.where(near, one_ref[AT_EDGE:, :], three_ref[AT_EDGE:, :])


def margins_kernel(strip_ref, strip_beside_ref, own_ref, beside_ref, wet_ref, named_ref, rows_ref):
    space, comp, lev = place()
    lane, row = lane_of(), row_of()
    for k in range(4):
        for ref, c in ((own_ref, comp), (beside_ref, 1 - comp)):
            at = (2 * (space ^ k) + c) * TABLE
            rows_ref[pl.ds(at, TABLE), :] = ref[TABLE * k : TABLE * (k + 1), :]

    def table_row(which):
        return rows_ref[pl.ds(which, ROWS, stride=TABLE), :]

    near = (lane < EDGE // 2) | (lane >= LANES - EDGE // 2)
    wet_ref[:, :LANES] = table_row(PACKED + 2)
    wet_ref[:, LANES:] = jnp.where(near, table_row(PACKED + 3), 0.0)

    def halves(ref, at):
        return [ref[at + 8 * i : at + 8 * (i + 1), :] for i in range(2)]

    def by_comp(mine, theirs):
        return [jnp.where(comp == 0, a, b) for a, b in zip(mine, theirs)]

    strips = halves(strip_ref, AT_REQUEST), halves(strip_beside_ref, AT_REQUEST)
    halos = halves(own_ref, AT_HALO_ASKED), halves(beside_ref, AT_HALO_ASKED)
    tables = (
        (by_comp(*strips), by_comp(*strips[::-1])),
        (by_comp(*halos), by_comp(*halos[::-1])),
    )
    first = ((2 * row - 1) * LANES + 2 * (lane & (HALF - 1))).astype(jnp.float32)
    parity = (lane & 1).astype(jnp.float32)
    pairs = lane >> 1
    spread = ((0, pairs), (0, pairs + HALF), (1, jnp.where(lane < HALF, pairs, pairs + HALF)))
    table_halo = table_row(PACKED + 1)
    named = [[jnp.zeros((ROWS, LANES), jnp.float32) for _ in range(3)] for _ in range(4)]
    for margin in range(MARGINS):
        slots = (table_row(8 + margin), turn(table_halo, -EDGE * margin))
        weights = (table_row(8 + MARGINS + margin), turn(table_halo, -EDGE * (MARGINS + margin)))
        cells = []
        for slot, (low_strip, high_strip) in zip(slots, tables):
            rank = slot.astype(jnp.int32) & (2 * LANES - 1)
            late = rank >= LANES
            rank = rank & (LANES - 1)
            found = [jnp.where(late, pick_lanes(high, rank), pick_lanes(low, rank)) for low, high in (low_strip, high_strip)]
            cells.append(jnp.where(lane < HALF, found[0], found[1]) - first)
        for tile, (ring, lanes) in enumerate(spread):
            beyond = pick_lanes(cells[ring], lanes) - parity
            share = pick_lanes(weights[ring], lanes)
            for step in range(4):
                named[step][tile] = named[step][tile] + jnp.where(beyond == float(step * LANES), share, 0.0)
    for step in range(4):
        for tile in range(3):
            named_ref[step, tile] = named[step][tile]


def column_kernel(
    factors_ref,
    strip_ref,
    strip_beside_ref,
    own_ref,
    beside_ref,
    others_ref,
    wet_ref,
    named_ref,
    atmos_ref,
    final_ref,
    first_ref,
    second_ref,
    third_ref,
    state_ref,
    flux_ref,
    rows_ref,
    back_ref,
):
    space, comp, lev = place()
    lane, row = lane_of(), row_of()
    half = LEVELS // 2

    mine = pl.ds(pl.multiple_of(comp * LANES, LANES), LANES)
    theirs = pl.ds(pl.multiple_of((1 - comp) * LANES, LANES), LANES)
    for level in range(half):
        here, there = lev * half + level, (1 - lev) * half + level
        at = 2 * ROWS * level
        state_ref[here, :, mine] = strip_ref[at : at + 2 * ROWS, :]
        state_ref[there, :, mine] = others_ref[OTHER_LEVELS + at : OTHER_LEVELS + at + 2 * ROWS, :]
        state_ref[there, :, theirs] = strip_beside_ref[at : at + 2 * ROWS, :]
        state_ref[here, :, theirs] = others_ref[BESIDE_LEVELS + at : BESIDE_LEVELS + at + 2 * ROWS, :]
    exists = jnp.where(lane < HALF, space + 1, 4 - space) < 4
    halos = (
        (lev, others_ref[OTHER_HALO:BESIDE_BLOCKS, :], beside_ref[AT_HALO:AT_HALO_ASKED, :]),
        (1 - lev, own_ref[AT_HALO:AT_HALO_ASKED, :], others_ref[BESIDE_HALO:OTHER_LEVELS, :]),
    )
    for block, own, beside in halos:
        east, west = jnp.where(comp == 0, own, beside), jnp.where(comp == 0, beside, own)
        for group in range(LANES // EDGE):
            tile = jnp.where(
                lane < EDGE,
                turn(east, -EDGE * group),
                jnp.where(lane >= LANES - EDGE, turn(west, -EDGE * (group + 1)), 0.0),
            )
            state_ref[block * half + group // 2, ROWS * (group % 2) : ROWS * (group % 2 + 1), 2 * LANES :] = jnp.where(
                exists, tile, 0.0
            )
    edge_inside = jnp.where(jnp.concatenate([exists] * 2, 0), 1.0, 0.0)
    inside = jnp.concatenate([jnp.ones((2 * ROWS, 2 * LANES), jnp.float32), edge_inside], 1)

    def factor(which):
        return jnp.broadcast_to(jnp.concatenate([factors_ref[which : which + 1, :]] * 3, 1), (2 * ROWS, 3 * LANES))

    atmos = [state_ref[level] for level in range(LEVELS)]
    for substep in range(ASUB):
        shaded = [jnp.tanh(cells) for cells in atmos]
        later = []
        for level in range(LEVELS):
            cells = atmos[level]
            beside = turn(cells, 1) + turn(cells, -1) + rows_down(cells) + rows_up(cells)
            column = sum(factor(LEVELS * other + level) * shaded[other] for other in range(LEVELS))
            cells = DIFFUSE * (cells + beside) + column
            later.append(inside * cells)
        atmos = later
    for level in range(LEVELS):
        state_ref[level] = atmos[level]
    for level in range(half):
        atmos_ref[level] = state_ref[lev * half + level, :, mine]

    for field in range(FIELDS):
        flux = sum(factor(LEVELS * (LEVELS + field) + level) * atmos[level] for level in range(LEVELS))
        for tile in range(3):
            flux_ref[tile, WIDE * field : WIDE * field + 8, :] = jnp.zeros((ROWS, LANES), jnp.float32)
            flux_ref[tile, WIDE * field + 8 : WIDE * field + 24, :] = flux[:, LANES * tile : LANES * (tile + 1)]
            flux_ref[tile, WIDE * field + 24 : WIDE * field + 32, :] = jnp.zeros((ROWS, LANES), jnp.float32)

    for k in range(4):
        own, beside = 2 * (space ^ k) + comp, 2 * (space ^ k) + 1 - comp
        block = slice(TABLE * k, TABLE * (k + 1))
        came = slice(BESIDE_BLOCKS + TABLE * (k - 1), BESIDE_BLOCKS + TABLE * k)
        rows_ref[pl.ds(own * TABLE, TABLE), :] = own_ref[block, :] if k else others_ref[:TABLE, :]
        rows_ref[pl.ds(beside * TABLE, TABLE), :] = others_ref[came, :] if k else beside_ref[block, :]
    ocean_halo = rows_ref[pl.ds(PACKED, ROWS, stride=TABLE), :]

    wetness = wet_ref[...]
    pairs = (2 * lane) & (LANES - 1)
    ocean = []
    forcing = []
    for field in range(FIELDS):
        sums = []
        for tile in range(3):
            total = sum(
                named_ref[step, tile] * flux_ref[tile, pl.ds(WIDE * field + 7 + step, ROWS, stride=2), :] for step in range(4)
            )
            sums.append(pick_lanes(total + turn(total, -1), pairs))
        remapped = jnp.concatenate([jnp.where(lane < HALF, sums[0], sums[1]), sums[2]], 1)
        forcing.append(wetness * (FORCING * remapped))
        main = rows_ref[pl.ds(field, ROWS, stride=TABLE), :]
        ocean.append(jnp.concatenate([main, turn(ocean_halo, -EDGE * field)], 1))
    spreading = OCEAN_MIX * wetness
    for substep in range(SUB):
        for field in range(FIELDS):
            cells = ocean[field]
            beside = turn(cells, 1) + turn(cells, -1) + rows_down(cells) + rows_up(cells)
            ocean[field] = spreading * (cells + beside) + forcing[field]
    for field in range(FIELDS):
        cells = ocean[field][:, :LANES]
        final_ref[ROWS * field : ROWS * (field + 1), :] = cells
        back_ref[pl.ds(field, ROWS, stride=FIELDS), :] = cells
    for k, ref in zip((1, 2, 3), (first_ref, second_ref, third_ref)):
        ref[...] = back_ref[pl.ds((2 * (space ^ k) + comp) * FIELDS, FIELDS), :]


def returned_kernel(atmos_ref, final_ref, named_ref, atmos_next_ref, returned_ref):
    space, comp, lev = place()
    lane = lane_of()
    atmos_next_ref[...] = atmos_ref[...]
    named = [jnp.where(comp == 0, named_ref[step, 0], named_ref[step, 1]) for step in range(4)]
    pairs = (lane >> 1) + HALF * comp
    for field in range(FIELDS):
        spread = pick_lanes(final_ref[ROWS * field : ROWS * (field + 1), :], pairs)
        upper = named[1] * spread + rows_down(named[3] * spread)
        lower = named[2] * spread + rows_up(named[0] * spread)
        returned_ref[pl.ds(2 * ROWS * field, ROWS, stride=2), :] = upper
        returned_ref[pl.ds(2 * ROWS * field + 1, ROWS, stride=2), :] = lower


def rows_kernel(three_ref, two_ref, one_ref, final_ref, ocean_ref):
    space, comp, lev = place()
    own = final_ref[pl.ds(2 * space + comp, FIELDS, stride=ROWS), :]
    for k, cells in enumerate((own, one_ref[...], two_ref[...], three_ref[...])):
        ocean_ref[:, 0, pl.ds(pl.multiple_of((space ^ k) * LANES, LANES), LANES)] = cells


def over(axis, k, array):
    return lax.ppermute(array, axis, [(i, i ^ k) for i in range(lax.axis_size(axis))])


def across(axis, k, array):
    pairs = [(2 * i + core, 2 * (i ^ k) + 1 - core) for i in range(lax.axis_size(axis)) for core in range(2)]
    return lax.ppermute(array, (axis, "lev"), pairs)


def local(kernel, out_shape, spaces, scratch=()):
    single = not isinstance(out_shape, tuple)
    vmem = pl.BlockSpec(memory_space=pltpu.VMEM)
    return pl.pallas_call(
        kernel,
        out_shape=out_shape,
        in_specs=[pl.BlockSpec(memory_space=space) for space in spaces],
        out_specs=vmem if single else (vmem,) * len(out_shape),
        scratch_shapes=list(scratch),
        compiler_params=pltpu.CompilerParams(vmem_limit_bytes=VMEM_LIMIT),
    )


def shards_by_columns(
    atmos_state,
    ocean_state,
    vertical_mixing,
    flux_coupling,
    request_cells,
    margin_slot,
    margin_weight,
    sea_mask,
):
    def values(*shape):
        return jax.ShapeDtypeStruct(shape, jnp.float32)

    arrays = (ocean_state, margin_slot, margin_weight, sea_mask, atmos_state, request_cells)
    arrays += (vertical_mixing, flux_coupling.T)
    letters, factors, strip = local(
        tables_kernel,
        (values(4, LETTER, LANES), values(2 * LEVELS * LEVELS, LANES), values(STRIP, LANES)),
        [pltpu.HBM] * 8,
        [pltpu.VMEM(a.shape, a.dtype) for a in arrays] + [pltpu.SemaphoreType.DMA((8,))],
    )(*(pltpu.with_memory_space_constraint(a, pltpu.HBM) for a in arrays))
    one, three = (across("space", k, letters[k]) for k in (1, 3))
    two = across("space", 2, letters[2, :TABLE])
    strip_beside = across("comp", 1, strip)
    sheet = local(sheet_kernel, values(SHEET, LANES), [pltpu.VMEM] * 4)(letters[0], three, two, one)
    sheet_beside = across("comp", 1, sheet)
    swapped = (sheet[:TABLE], sheet[AT_HALO:AT_HALO_ASKED], sheet_beside[TABLE:AT_HALO_ASKED])
    swapped += (strip[:AT_REQUEST], strip_beside[:AT_REQUEST])
    others = over("lev", 1, jnp.concatenate(swapped, 0))
    wet, named = local(
        margins_kernel,
        (values(ROWS, 2 * LANES), values(4, 3, ROWS, LANES)),
        [pltpu.VMEM] * 4,
        [pltpu.VMEM((ROWS * TABLE, LANES), jnp.float32)],
    )(strip, strip_beside, sheet, sheet_beside)
    atmos, final, *back = local(
        column_kernel,
        (values(*atmos_state.shape), values(FIELDS * ROWS, LANES)) + (values(FIELDS, LANES),) * 3,
        [pltpu.VMEM] * 8,
        [
            pltpu.VMEM((LEVELS, 2 * ROWS, 3 * LANES), jnp.float32),
            pltpu.VMEM((3, FIELDS * WIDE, LANES), jnp.float32),
            pltpu.VMEM((ROWS * TABLE, LANES), jnp.float32),
            pltpu.VMEM((ROWS * FIELDS, LANES), jnp.float32),
        ],
    )(factors, strip, strip_beside, sheet, sheet_beside, others, wet, named)
    one, two, three = (across("space", k, piece) for k, piece in zip((1, 2, 3), back))
    final = over("lev", 1, final)
    atmos_next, returned = local(
        returned_kernel,
        (values(*atmos_state.shape), values(FIELDS * 2 * ROWS, LANES)),
        [pltpu.VMEM] * 3,
    )(atmos, final, named)
    ocean_next = local(rows_kernel, values(*ocean_state.shape), [pltpu.VMEM] * 4)(three, two, one, final)
    return (atmos_next, ocean_next, returned.reshape(FIELDS, 2 * ROWS, LANES))


def shards(*arguments):
    atmos_state, ocean_state, mixing, coupling, request_cells, margin_slot = arguments[:6]
    by_columns = (
        (lax.axis_size("space"), lax.axis_size("comp"), lax.axis_size("lev")) == (4, 2, 2)
        and atmos_state.shape == (LEVELS // 2, 2 * ROWS, LANES)
        and ocean_state.shape == (FIELDS, 1, 4 * LANES)
        and request_cells.shape == (1, ROWS, 2 * LANES)
        and margin_slot.shape[0] == MARGINS
    )
    return (shards_by_columns if by_columns else shards_by_neighbours)(*arguments)


def solution(mesh):
    placed = (
        P(("parts", "lev"), None, ("space", "comp")),
        P(("parts", "lev"), ("space", "comp"), None),
        P(),
        P(),
        P(("space", "comp"), None, None),
        P(None, ("space", "comp"), None),
        P(None, ("space", "comp"), None),
        P(("space", "comp"), None),
    )
    return jax.shard_map(
        shards,
        mesh=mesh,
        in_specs=placed,
        out_specs=(
            P(("parts", "lev"), None, ("space", "comp")),
            P(("parts", "lev"), ("space", "comp"), None),
            P(("parts", "lev"), None, ("space", "comp")),
        ),
        check_vma=False,
    )
```

```python
import jax
import jax.numpy as jnp
from jax import lax
from jax.experimental import pallas as pl
from jax.experimental.pallas import tpu as pltpu
from jax.sharding import PartitionSpec as P

ASUB = 2
SUB = 8


DIFFUSE = 0.2
TENDENCY = 0.25
OCEAN_MIX = 0.2
FORCING = 0.15


def with_halo(cells, sides, width):
    for axis, dim in sides:
        count = lax.axis_size(axis)
        ends = count - 1
        head = lax.slice_in_dim(cells, 0, width, axis=dim)
        tail = lax.slice_in_dim(cells, cells.shape[dim] - width, cells.shape[dim], axis=dim)
        cells = jnp.concatenate(
            [
                lax.ppermute(tail, axis, [(i, (i + 1) % count) for i in range(ends)]),
                cells,
                lax.ppermute(head, axis, [((i + 1) % count, i) for i in range(ends)]),
            ],
            axis=dim,
        )
    return cells


def atmos_step(atmos, mixing_rows):
    lev_local = atmos.shape[0]
    padded = with_halo(atmos, ((("space", "comp"), 2),), 1)
    padded = jnp.pad(padded, ((0, 0), (1, 1), (0, 0)))
    beside = padded[:, 2:, 1:-1] + padded[:, :-2, 1:-1] + padded[:, 1:-1, 2:] + padded[:, 1:-1, :-2]
    shaded = jnp.tanh(atmos).reshape(lev_local, -1)
    column = jnp.dot(
        mixing_rows,
        lax.all_gather(shaded, "lev", axis=0, tiled=True),
        precision=lax.Precision.HIGHEST,
    )
    return atmos + DIFFUSE * (beside - 4.0 * atmos) + TENDENCY * column.reshape(atmos.shape)


def advance(padded, wetness, forcing):
    centre = padded[:, 1:-1, 1:-1]
    beside = padded[:, 2:, 1:-1] + padded[:, :-2, 1:-1] + padded[:, 1:-1, 2:] + padded[:, 1:-1, :-2]
    return wetness[None] * (centre + OCEAN_MIX * (beside - 4.0 * centre) + FORCING * forcing)


def shards_by_neighbours(
    atmos_state,
    ocean_state,
    vertical_mixing,
    flux_coupling,
    request_cells,
    margin_slot,
    margin_weight,
    sea_mask,
):
    lev_local, rows_atmos, cols_atmos = atmos_state.shape
    fields_local = ocean_state.shape[0]
    margins = margin_slot.shape[0]
    lev_place = lax.axis_index("lev")
    mixing_rows = lax.dynamic_slice_in_dim(vertical_mixing, lev_place * lev_local, lev_local, 0)
    coupling_cols = lax.dynamic_slice_in_dim(flux_coupling, lev_place * lev_local, lev_local, 1)
    atmos = atmos_state
    for substep in range(ASUB):
        atmos = atmos_step(atmos, mixing_rows)
    flat_atmos = atmos.reshape(lev_local, -1)
    fluxes = lax.psum_scatter(
        jnp.dot(coupling_cols, flat_atmos, precision=lax.Precision.HIGHEST),
        "lev",
        scatter_dimension=0,
        tiled=True,
    )
    requests = request_cells.reshape(-1)
    outgoing = jnp.take(fluxes, requests, axis=1)
    slot_flat = margin_slot.reshape(-1)
    weight_flat = margin_weight.reshape(margins, -1)
    received = lax.all_to_all(outgoing, ("space", "comp"), split_axis=1, concat_axis=1, tiled=True)
    picked = jnp.take(received, slot_flat, axis=1).reshape(received.shape[0], margins, -1)
    remapped = jnp.sum(picked * weight_flat[None], axis=1)
    forcing = remapped.reshape(ocean_state.shape)
    wetness = sea_mask.astype(jnp.float32)
    ocean_now = ocean_state
    for substep in range(SUB):
        padded = with_halo(ocean_now, ((("space", "comp"), 1),), 1)
        padded = jnp.pad(padded, ((0, 0), (0, 0), (1, 1)))
        ocean_now = advance(padded, wetness, forcing)
    weighted = (weight_flat[None] * ocean_now).reshape(fields_local, -1)
    outgoing_back = (
        jnp.zeros((fields_local, requests.shape[0]), jnp.float32).at[:, slot_flat].add(weighted)
    )
    arrived = lax.all_to_all(
        outgoing_back, ("space", "comp"), split_axis=1, concat_axis=1, tiled=True
    )
    returned = (
        jnp.zeros((fields_local, rows_atmos * cols_atmos), jnp.float32).at[:, requests].add(arrived)
    )
    return (atmos, ocean_now, returned.reshape(fields_local, rows_atmos, cols_atmos))


LANES = 128
HALF = 64
ROWS = 8
LEVELS = 8
FIELDS = 8
MARGINS = 4
TABLE = 24
PACKED = 16
TABLES = 4 * TABLE
AT_EDGE = TABLE
AT_ASKED = AT_EDGE + 8
LETTER = AT_ASKED + 16
AT_REQUEST = 64
STRIP = AT_REQUEST + 16
AT_HALO = 4 * TABLE
AT_HALO_ASKED = AT_HALO + 8
SHEET = AT_HALO_ASKED + 16
OTHER_HALO = TABLE
BESIDE_BLOCKS = OTHER_HALO + 8
BESIDE_HALO = BESIDE_BLOCKS + 3 * TABLE
OTHER_LEVELS = BESIDE_HALO + 8
BESIDE_LEVELS = OTHER_LEVELS + 64
EDGE = 16
WIDE = 32
VMEM_LIMIT = 4 * 1024 * 1024


def lane_of(shape=(ROWS, LANES)):
    return lax.broadcasted_iota(jnp.int32, shape, 1)


def row_of(shape=(ROWS, LANES)):
    return lax.broadcasted_iota(jnp.int32, shape, 0)


def pick_lanes(tile, lanes):
    return jnp.take_along_axis(tile, lanes, axis=1, mode="promise_in_bounds")


def turn(tile, by):
    by = by % tile.shape[1]
    return pltpu.roll(tile, by, 1) if by else tile


def rows_down(tile):
    return jnp.where(row_of(tile.shape) == 0, 0.0, pltpu.roll(tile, 1, 0))


def rows_up(tile):
    last = tile.shape[0] - 1
    return jnp.where(row_of(tile.shape) == last, 0.0, pltpu.roll(tile, last, 0))


def place():
    return lax.axis_index("space"), lax.axis_index("comp"), lax.axis_index("lev")


def tables_kernel(*refs):
    arrays, (letters_ref, factors_ref, strip_ref), held, arrived = refs[:8], refs[8:11], refs[11:-1], refs[-1]
    copies = [pltpu.make_async_copy(a, h, arrived.at[i]) for i, (a, h) in enumerate(zip(arrays, held))]
    for copy in copies:
        copy.start()
    for copy in copies:
        copy.wait()
    ocean_ref, slot_ref, weight_ref, mask_ref, atmos_ref, request_ref, mixing_ref, coupling_ref = held
    space, comp, lev = place()
    lane, row = lane_of(), row_of()
    near = (lane < EDGE // 2) | (lane >= LANES - EDGE // 2)

    def halo(tiles, z):
        beyond = jnp.zeros_like(tiles[0])
        east = tiles[z + 1] if z + 1 < len(tiles) else beyond
        west = tiles[z - 1] if z > 0 else beyond
        wide = lane[: beyond.shape[0]]
        return jnp.where(near[: beyond.shape[0]], jnp.where(wide < HALF, east, west), 0.0)

    def packed(cells):
        return jnp.sum(pltpu.roll(cells, 0, 1, stride=EDGE, stride_axis=0), axis=0, keepdims=True)

    def tiles_of(cells):
        return [cells[:, LANES * z : LANES * (z + 1)] for z in range(4)]

    ocean = tiles_of(ocean_ref[:, 0, :])
    table = tiles_of(jnp.concatenate([slot_ref[:, 0, :].astype(jnp.float32), weight_ref[:, 0, :]], 0))
    mask = tiles_of(mask_ref[...].astype(jnp.float32))
    to_right = jnp.zeros((ROWS, LANES), jnp.float32)
    to_left = jnp.zeros((ROWS, LANES), jnp.float32)
    for group in range(LANES // EDGE):
        tile = atmos_ref[group // 2, ROWS * (group % 2) : ROWS * (group % 2 + 1), :]
        here = lane // EDGE == group
        to_right = jnp.where(here, turn(tile, EDGE * (group + 1)), to_right)
        to_left = jnp.where(here, turn(tile, EDGE * group), to_left)
    edge = jnp.where(comp == 0, to_left, to_right)
    requests = request_ref[0].astype(jnp.float32)
    for z in range(4):
        k = z ^ space
        letters_ref[k, :8, :] = ocean[z]
        letters_ref[k, 8:16, :] = table[z]
        last = jnp.where(row == 0, packed(halo(ocean, z)), 0.0)
        last = jnp.where(row == 1, packed(halo(table, z)), last)
        last = jnp.where(row == 2, mask[z], last)
        letters_ref[k, PACKED:TABLE, :] = jnp.where(row == 3, halo(mask, z), last)
        letters_ref[k, AT_EDGE:AT_ASKED, :] = edge
        letters_ref[k, AT_ASKED : AT_ASKED + 8, :] = requests[:, :LANES]
        letters_ref[k, AT_ASKED + 8 :, :] = requests[:, LANES:]
    for other in range(LEVELS):
        factors_ref[LEVELS * other : LEVELS * (other + 1), :] = jnp.broadcast_to(
            TENDENCY * mixing_ref[:, other : other + 1], (ROWS, LANES)
        )
    for field in range(FIELDS):
        other = [coupling_ref[:, FIELDS * i + field : FIELDS * i + field + 1] for i in range(2)]
        at = LEVELS * (LEVELS + field)
        factors_ref[at : at + LEVELS, :] = jnp.broadcast_to(jnp.where(lev == 0, other[1], other[0]), (ROWS, LANES))
    for level in range(LEVELS // 2):
        strip_ref[2 * ROWS * level : 2 * ROWS * (level + 1), :] = atmos_ref[level]
    strip_ref[AT_REQUEST : AT_REQUEST + 8, :] = requests[:, :LANES]
    strip_ref[AT_REQUEST + 8 :, :] = requests[:, LANES:]


def sheet_kernel(own_ref, three_ref, two_ref, one_ref, sheet_ref):
    space, comp, lev = place()
    for k, ref in enumerate((own_ref, one_ref, two_ref, three_ref)):
        sheet_ref[TABLE * k : TABLE * (k + 1), :] = ref[:TABLE, :]
    near = (space + comp) % 2 == 0
    sheet_ref[AT_HALO:, :] = jnp.where(near, one_ref[AT_EDGE:, :], three_ref[AT_EDGE:, :])


def margins_kernel(strip_ref, strip_beside_ref, own_ref, beside_ref, wet_ref, named_ref, rows_ref):
    space, comp, lev = place()
    lane, row = lane_of(), row_of()
    for k in range(4):
        for ref, c in ((own_ref, comp), (beside_ref, 1 - comp)):
            at = (2 * (space ^ k) + c) * TABLE
            rows_ref[pl.ds(at, TABLE), :] = ref[TABLE * k : TABLE * (k + 1), :]

    def table_row(which):
        return rows_ref[pl.ds(which, ROWS, stride=TABLE), :]

    near = (lane < EDGE // 2) | (lane >= LANES - EDGE // 2)
    wet_ref[:, :LANES] = table_row(PACKED + 2)
    wet_ref[:, LANES:] = jnp.where(near, table_row(PACKED + 3), 0.0)

    def halves(ref, at):
        return [ref[at + 8 * i : at + 8 * (i + 1), :] for i in range(2)]

    def by_comp(mine, theirs):
        return [jnp.where(comp == 0, a, b) for a, b in zip(mine, theirs)]

    strips = halves(strip_ref, AT_REQUEST), halves(strip_beside_ref, AT_REQUEST)
    halos = halves(own_ref, AT_HALO_ASKED), halves(beside_ref, AT_HALO_ASKED)
    tables = (
        (by_comp(*strips), by_comp(*strips[::-1])),
        (by_comp(*halos), by_comp(*halos[::-1])),
    )
    first = ((2 * row - 1) * LANES + 2 * (lane & (HALF - 1))).astype(jnp.float32)
    parity = (lane & 1).astype(jnp.float32)
    pairs = lane >> 1
    spread = ((0, pairs), (0, pairs + HALF), (1, jnp.where(lane < HALF, pairs, pairs + HALF)))
    table_halo = table_row(PACKED + 1)
    named = [[jnp.zeros((ROWS, LANES), jnp.float32) for _ in range(3)] for _ in range(4)]
    for margin in range(MARGINS):
        slots = (table_row(8 + margin), turn(table_halo, -EDGE * margin))
        weights = (table_row(8 + MARGINS + margin), turn(table_halo, -EDGE * (MARGINS + margin)))
        cells = []
        for slot, (low_strip, high_strip) in zip(slots, tables):
            rank = slot.astype(jnp.int32) & (2 * LANES - 1)
            late = rank >= LANES
            rank = rank & (LANES - 1)
            found = [jnp.where(late, pick_lanes(high, rank), pick_lanes(low, rank)) for low, high in (low_strip, high_strip)]
            cells.append(jnp.where(lane < HALF, found[0], found[1]) - first)
        for tile, (ring, lanes) in enumerate(spread):
            beyond = pick_lanes(cells[ring], lanes) - parity
            share = pick_lanes(weights[ring], lanes)
            for step in range(4):
                named[step][tile] = named[step][tile] + jnp.where(beyond == float(step * LANES), share, 0.0)
    for step in range(4):
        for tile in range(3):
            named_ref[step, tile] = named[step][tile]


def column_kernel(
    factors_ref,
    strip_ref,
    strip_beside_ref,
    own_ref,
    beside_ref,
    others_ref,
    wet_ref,
    named_ref,
    atmos_ref,
    final_ref,
    first_ref,
    second_ref,
    third_ref,
    state_ref,
    flux_ref,
    rows_ref,
    back_ref,
):
    space, comp, lev = place()
    lane, row = lane_of(), row_of()
    half = LEVELS // 2

    mine = pl.ds(pl.multiple_of(comp * LANES, LANES), LANES)
    theirs = pl.ds(pl.multiple_of((1 - comp) * LANES, LANES), LANES)
    for level in range(half):
        here, there = lev * half + level, (1 - lev) * half + level
        at = 2 * ROWS * level
        state_ref[here, :, mine] = strip_ref[at : at + 2 * ROWS, :]
        state_ref[there, :, mine] = others_ref[OTHER_LEVELS + at : OTHER_LEVELS + at + 2 * ROWS, :]
        state_ref[there, :, theirs] = strip_beside_ref[at : at + 2 * ROWS, :]
        state_ref[here, :, theirs] = others_ref[BESIDE_LEVELS + at : BESIDE_LEVELS + at + 2 * ROWS, :]
    exists = jnp.where(lane < HALF, space + 1, 4 - space) < 4
    halos = (
        (lev, others_ref[OTHER_HALO:BESIDE_BLOCKS, :], beside_ref[AT_HALO:AT_HALO_ASKED, :]),
        (1 - lev, own_ref[AT_HALO:AT_HALO_ASKED, :], others_ref[BESIDE_HALO:OTHER_LEVELS, :]),
    )
    for block, own, beside in halos:
        east, west = jnp.where(comp == 0, own, beside), jnp.where(comp == 0, beside, own)
        for group in range(LANES // EDGE):
            tile = jnp.where(
                lane < EDGE,
                turn(east, -EDGE * group),
                jnp.where(lane >= LANES - EDGE, turn(west, -EDGE * (group + 1)), 0.0),
            )
            state_ref[block * half + group // 2, ROWS * (group % 2) : ROWS * (group % 2 + 1), 2 * LANES :] = jnp.where(
                exists, tile, 0.0
            )
    edge_inside = jnp.where(jnp.concatenate([exists] * 2, 0), 1.0, 0.0)
    inside = jnp.concatenate([jnp.ones((2 * ROWS, 2 * LANES), jnp.float32), edge_inside], 1)

    def factor(which):
        return jnp.broadcast_to(jnp.concatenate([factors_ref[which : which + 1, :]] * 3, 1), (2 * ROWS, 3 * LANES))

    atmos = [state_ref[level] for level in range(LEVELS)]
    for substep in range(ASUB):
        shaded = [jnp.tanh(cells) for cells in atmos]
        later = []
        for level in range(LEVELS):
            cells = atmos[level]
            beside = turn(cells, 1) + turn(cells, -1) + rows_down(cells) + rows_up(cells)
            column = sum(factor(LEVELS * other + level) * shaded[other] for other in range(LEVELS))
            cells = DIFFUSE * (cells + beside) + column
            later.append(inside * cells)
        atmos = later
    for level in range(LEVELS):
        state_ref[level] = atmos[level]
    for level in range(half):
        atmos_ref[level] = state_ref[lev * half + level, :, mine]

    for field in range(FIELDS):
        flux = sum(factor(LEVELS * (LEVELS + field) + level) * atmos[level] for level in range(LEVELS))
        for tile in range(3):
            flux_ref[tile, WIDE * field : WIDE * field + 8, :] = jnp.zeros((ROWS, LANES), jnp.float32)
            flux_ref[tile, WIDE * field + 8 : WIDE * field + 24, :] = flux[:, LANES * tile : LANES * (tile + 1)]
            flux_ref[tile, WIDE * field + 24 : WIDE * field + 32, :] = jnp.zeros((ROWS, LANES), jnp.float32)

    for k in range(4):
        own, beside = 2 * (space ^ k) + comp, 2 * (space ^ k) + 1 - comp
        block = slice(TABLE * k, TABLE * (k + 1))
        came = slice(BESIDE_BLOCKS + TABLE * (k - 1), BESIDE_BLOCKS + TABLE * k)
        rows_ref[pl.ds(own * TABLE, TABLE), :] = own_ref[block, :] if k else others_ref[:TABLE, :]
        rows_ref[pl.ds(beside * TABLE, TABLE), :] = others_ref[came, :] if k else beside_ref[block, :]
    ocean_halo = rows_ref[pl.ds(PACKED, ROWS, stride=TABLE), :]

    wetness = wet_ref[...]
    pairs = (2 * lane) & (LANES - 1)
    ocean = []
    forcing = []
    for field in range(FIELDS):
        sums = []
        for tile in range(3):
            total = sum(
                named_ref[step, tile] * flux_ref[tile, pl.ds(WIDE * field + 7 + step, ROWS, stride=2), :] for step in range(4)
            )
            sums.append(pick_lanes(total + turn(total, -1), pairs))
        remapped = jnp.concatenate([jnp.where(lane < HALF, sums[0], sums[1]), sums[2]], 1)
        forcing.append(wetness * (FORCING * remapped))
        main = rows_ref[pl.ds(field, ROWS, stride=TABLE), :]
        ocean.append(jnp.concatenate([main, turn(ocean_halo, -EDGE * field)], 1))
    spreading = OCEAN_MIX * wetness
    for substep in range(SUB):
        for field in range(FIELDS):
            cells = ocean[field]
            beside = turn(cells, 1) + turn(cells, -1) + rows_down(cells) + rows_up(cells)
            ocean[field] = spreading * (cells + beside) + forcing[field]
    for field in range(FIELDS):
        cells = ocean[field][:, :LANES]
        final_ref[ROWS * field : ROWS * (field + 1), :] = cells
        back_ref[pl.ds(field, ROWS, stride=FIELDS), :] = cells
    for k, ref in zip((1, 2, 3), (first_ref, second_ref, third_ref)):
        ref[...] = back_ref[pl.ds((2 * (space ^ k) + comp) * FIELDS, FIELDS), :]


def returned_kernel(atmos_ref, final_ref, named_ref, atmos_next_ref, returned_ref):
    space, comp, lev = place()
    lane = lane_of()
    atmos_next_ref[...] = atmos_ref[...]
    named = [jnp.where(comp == 0, named_ref[step, 0], named_ref[step, 1]) for step in range(4)]
    pairs = (lane >> 1) + HALF * comp
    for field in range(FIELDS):
        spread = pick_lanes(final_ref[ROWS * field : ROWS * (field + 1), :], pairs)
        upper = named[1] * spread + rows_down(named[3] * spread)
        lower = named[2] * spread + rows_up(named[0] * spread)
        returned_ref[pl.ds(2 * ROWS * field, ROWS, stride=2), :] = upper
        returned_ref[pl.ds(2 * ROWS * field + 1, ROWS, stride=2), :] = lower


def rows_kernel(three_ref, two_ref, one_ref, final_ref, ocean_ref):
    space, comp, lev = place()
    own = final_ref[pl.ds(2 * space + comp, FIELDS, stride=ROWS), :]
    for k, cells in enumerate((own, one_ref[...], two_ref[...], three_ref[...])):
        ocean_ref[:, 0, pl.ds(pl.multiple_of((space ^ k) * LANES, LANES), LANES)] = cells


def over(axis, k, array):
    return lax.ppermute(array, axis, [(i, i ^ k) for i in range(lax.axis_size(axis))])


def across(axis, k, array):
    pairs = [(2 * i + core, 2 * (i ^ k) + 1 - core) for i in range(lax.axis_size(axis)) for core in range(2)]
    return lax.ppermute(array, (axis, "lev"), pairs)


def local(kernel, out_shape, spaces, scratch=()):
    single = not isinstance(out_shape, tuple)
    vmem = pl.BlockSpec(memory_space=pltpu.VMEM)
    return pl.pallas_call(
        kernel,
        out_shape=out_shape,
        in_specs=[pl.BlockSpec(memory_space=space) for space in spaces],
        out_specs=vmem if single else (vmem,) * len(out_shape),
        scratch_shapes=list(scratch),
        compiler_params=pltpu.CompilerParams(vmem_limit_bytes=VMEM_LIMIT),
    )


def shards_by_columns(
    atmos_state,
    ocean_state,
    vertical_mixing,
    flux_coupling,
    request_cells,
    margin_slot,
    margin_weight,
    sea_mask,
):
    def values(*shape):
        return jax.ShapeDtypeStruct(shape, jnp.float32)

    arrays = (ocean_state, margin_slot, margin_weight, sea_mask, atmos_state, request_cells)
    arrays += (vertical_mixing, flux_coupling.T)
    letters, factors, strip = local(
        tables_kernel,
        (values(4, LETTER, LANES), values(2 * LEVELS * LEVELS, LANES), values(STRIP, LANES)),
        [pltpu.HBM] * 8,
        [pltpu.VMEM(a.shape, a.dtype) for a in arrays] + [pltpu.SemaphoreType.DMA((8,))],
    )(*(pltpu.with_memory_space_constraint(a, pltpu.HBM) for a in arrays))
    one, two, three = (across("space", k, letters[k]) for k in (1, 2, 3))
    strip_beside = across("comp", 1, strip)
    sheet = local(sheet_kernel, values(SHEET, LANES), [pltpu.VMEM] * 4)(letters[0], three, two, one)
    sheet_beside = across("comp", 1, sheet)
    swapped = (sheet[:TABLE], sheet[AT_HALO:AT_HALO_ASKED], sheet_beside[TABLE:AT_HALO_ASKED])
    swapped += (strip[:AT_REQUEST], strip_beside[:AT_REQUEST])
    others = over("lev", 1, jnp.concatenate(swapped, 0))
    wet, named = local(
        margins_kernel,
        (values(ROWS, 2 * LANES), values(4, 3, ROWS, LANES)),
        [pltpu.VMEM] * 4,
        [pltpu.VMEM((ROWS * TABLE, LANES), jnp.float32)],
    )(strip, strip_beside, sheet, sheet_beside)
    atmos, final, *back = local(
        column_kernel,
        (values(*atmos_state.shape), values(FIELDS * ROWS, LANES)) + (values(FIELDS, LANES),) * 3,
        [pltpu.VMEM] * 8,
        [
            pltpu.VMEM((LEVELS, 2 * ROWS, 3 * LANES), jnp.float32),
            pltpu.VMEM((3, FIELDS * WIDE, LANES), jnp.float32),
            pltpu.VMEM((ROWS * TABLE, LANES), jnp.float32),
            pltpu.VMEM((ROWS * FIELDS, LANES), jnp.float32),
        ],
    )(factors, strip, strip_beside, sheet, sheet_beside, others, wet, named)
    one, two, three = (across("space", k, piece) for k, piece in zip((1, 2, 3), back))
    final = over("lev", 1, final)
    atmos_next, returned = local(
        returned_kernel,
        (values(*atmos_state.shape), values(FIELDS * 2 * ROWS, LANES)),
        [pltpu.VMEM] * 3,
    )(atmos, final, named)
    ocean_next = local(rows_kernel, values(*ocean_state.shape), [pltpu.VMEM] * 4)(three, two, one, final)
    return (atmos_next, ocean_next, returned.reshape(FIELDS, 2 * ROWS, LANES))


def shards(*arguments):
    atmos_state, ocean_state, mixing, coupling, request_cells, margin_slot = arguments[:6]
    by_columns = (
        (lax.axis_size("space"), lax.axis_size("comp"), lax.axis_size("lev")) == (4, 2, 2)
        and atmos_state.shape == (LEVELS // 2, 2 * ROWS, LANES)
        and ocean_state.shape == (FIELDS, 1, 4 * LANES)
        and request_cells.shape == (1, ROWS, 2 * LANES)
        and margin_slot.shape[0] == MARGINS
    )
    return (shards_by_columns if by_columns else shards_by_neighbours)(*arguments)


def solution(mesh):
    placed = (
        P(("parts", "lev"), None, ("space", "comp")),
        P(("parts", "lev"), ("space", "comp"), None),
        P(),
        P(),
        P(("space", "comp"), None, None),
        P(None, ("space", "comp"), None),
        P(None, ("space", "comp"), None),
        P(("space", "comp"), None),
    )
    return jax.shard_map(
        shards,
        mesh=mesh,
        in_specs=placed,
        out_specs=(
            P(("parts", "lev"), None, ("space", "comp")),
            P(("parts", "lev"), ("space", "comp"), None),
            P(("parts", "lev"), None, ("space", "comp")),
        ),
        check_vma=False,
    )
```

```python
import jax
import jax.numpy as jnp
from jax import lax
from jax.experimental import pallas as pl
from jax.experimental.pallas import tpu as pltpu
from jax.sharding import PartitionSpec as P

ASUB = 2
SUB = 8


DIFFUSE = 0.2
TENDENCY = 0.25
OCEAN_MIX = 0.2
FORCING = 0.15


def with_halo(cells, sides, width):
    for axis, dim in sides:
        count = lax.axis_size(axis)
        ends = count - 1
        head = lax.slice_in_dim(cells, 0, width, axis=dim)
        tail = lax.slice_in_dim(cells, cells.shape[dim] - width, cells.shape[dim], axis=dim)
        cells = jnp.concatenate(
            [
                lax.ppermute(tail, axis, [(i, (i + 1) % count) for i in range(ends)]),
                cells,
                lax.ppermute(head, axis, [((i + 1) % count, i) for i in range(ends)]),
            ],
            axis=dim,
        )
    return cells


def atmos_step(atmos, mixing_rows):
    lev_local = atmos.shape[0]
    padded = with_halo(atmos, ((("space", "comp"), 2),), 1)
    padded = jnp.pad(padded, ((0, 0), (1, 1), (0, 0)))
    beside = padded[:, 2:, 1:-1] + padded[:, :-2, 1:-1] + padded[:, 1:-1, 2:] + padded[:, 1:-1, :-2]
    shaded = jnp.tanh(atmos).reshape(lev_local, -1)
    column = jnp.dot(
        mixing_rows,
        lax.all_gather(shaded, "lev", axis=0, tiled=True),
        precision=lax.Precision.HIGHEST,
    )
    return atmos + DIFFUSE * (beside - 4.0 * atmos) + TENDENCY * column.reshape(atmos.shape)


def advance(padded, wetness, forcing):
    centre = padded[:, 1:-1, 1:-1]
    beside = padded[:, 2:, 1:-1] + padded[:, :-2, 1:-1] + padded[:, 1:-1, 2:] + padded[:, 1:-1, :-2]
    return wetness[None] * (centre + OCEAN_MIX * (beside - 4.0 * centre) + FORCING * forcing)


def shards_by_neighbours(
    atmos_state,
    ocean_state,
    vertical_mixing,
    flux_coupling,
    request_cells,
    margin_slot,
    margin_weight,
    sea_mask,
):
    lev_local, rows_atmos, cols_atmos = atmos_state.shape
    fields_local = ocean_state.shape[0]
    margins = margin_slot.shape[0]
    lev_place = lax.axis_index("lev")
    mixing_rows = lax.dynamic_slice_in_dim(vertical_mixing, lev_place * lev_local, lev_local, 0)
    coupling_cols = lax.dynamic_slice_in_dim(flux_coupling, lev_place * lev_local, lev_local, 1)
    atmos = atmos_state
    for substep in range(ASUB):
        atmos = atmos_step(atmos, mixing_rows)
    flat_atmos = atmos.reshape(lev_local, -1)
    fluxes = lax.psum_scatter(
        jnp.dot(coupling_cols, flat_atmos, precision=lax.Precision.HIGHEST),
        "lev",
        scatter_dimension=0,
        tiled=True,
    )
    requests = request_cells.reshape(-1)
    outgoing = jnp.take(fluxes, requests, axis=1)
    slot_flat = margin_slot.reshape(-1)
    weight_flat = margin_weight.reshape(margins, -1)
    received = lax.all_to_all(outgoing, ("space", "comp"), split_axis=1, concat_axis=1, tiled=True)
    picked = jnp.take(received, slot_flat, axis=1).reshape(received.shape[0], margins, -1)
    remapped = jnp.sum(picked * weight_flat[None], axis=1)
    forcing = remapped.reshape(ocean_state.shape)
    wetness = sea_mask.astype(jnp.float32)
    ocean_now = ocean_state
    for substep in range(SUB):
        padded = with_halo(ocean_now, ((("space", "comp"), 1),), 1)
        padded = jnp.pad(padded, ((0, 0), (0, 0), (1, 1)))
        ocean_now = advance(padded, wetness, forcing)
    weighted = (weight_flat[None] * ocean_now).reshape(fields_local, -1)
    outgoing_back = (
        jnp.zeros((fields_local, requests.shape[0]), jnp.float32).at[:, slot_flat].add(weighted)
    )
    arrived = lax.all_to_all(
        outgoing_back, ("space", "comp"), split_axis=1, concat_axis=1, tiled=True
    )
    returned = (
        jnp.zeros((fields_local, rows_atmos * cols_atmos), jnp.float32).at[:, requests].add(arrived)
    )
    return (atmos, ocean_now, returned.reshape(fields_local, rows_atmos, cols_atmos))


LANES = 128
HALF = 64
ROWS = 8
LEVELS = 8
FIELDS = 8
MARGINS = 4
TABLE = 24
PACKED = 16
TABLES = 4 * TABLE
AT_EDGE = TABLE
AT_ASKED = AT_EDGE + 8
LETTER = AT_ASKED + 16
AT_REQUEST = 64
STRIP = AT_REQUEST + 16
AT_HALO = 4 * TABLE
AT_HALO_ASKED = AT_HALO + 8
SHEET = AT_HALO_ASKED + 16
OTHER_HALO = TABLE
BESIDE_BLOCKS = OTHER_HALO + 8
BESIDE_HALO = BESIDE_BLOCKS + 3 * TABLE
OTHER_LEVELS = BESIDE_HALO + 8
BESIDE_LEVELS = OTHER_LEVELS + 64
EDGE = 16
WIDE = 32
VMEM_LIMIT = 4 * 1024 * 1024


def lane_of(shape=(ROWS, LANES)):
    return lax.broadcasted_iota(jnp.int32, shape, 1)


def row_of(shape=(ROWS, LANES)):
    return lax.broadcasted_iota(jnp.int32, shape, 0)


def pick_lanes(tile, lanes):
    return jnp.take_along_axis(tile, lanes, axis=1, mode="promise_in_bounds")


def turn(tile, by):
    by = by % tile.shape[1]
    return pltpu.roll(tile, by, 1) if by else tile


def rows_down(tile):
    return jnp.where(row_of(tile.shape) == 0, 0.0, pltpu.roll(tile, 1, 0))


def rows_up(tile):
    last = tile.shape[0] - 1
    return jnp.where(row_of(tile.shape) == last, 0.0, pltpu.roll(tile, last, 0))


def place():
    return lax.axis_index("space"), lax.axis_index("comp"), lax.axis_index("lev")


FIRST = (1, 3, 0, 2)
SECOND = (3, 2, 1, 0)
LAST = (2, 0, 3, 1)


def at_end(space):
    return (space == 0) | (space == 3)


def letter_of(k, space):
    return jnp.where((k == 1) | (k == 2), jnp.where(at_end(space), k, 3 - k), k)


def tables_kernel(*refs):
    arrays, (letters_ref, factors_ref, strip_ref), held, arrived = refs[:8], refs[8:11], refs[11:-1], refs[-1]
    copies = [pltpu.make_async_copy(a, h, arrived.at[i]) for i, (a, h) in enumerate(zip(arrays, held))]
    for copy in copies:
        copy.start()
    for copy in copies:
        copy.wait()
    ocean_ref, slot_ref, weight_ref, mask_ref, atmos_ref, request_ref, mixing_ref, coupling_ref = held
    space, comp, lev = place()
    lane, row = lane_of(), row_of()
    near = (lane < EDGE // 2) | (lane >= LANES - EDGE // 2)

    def halo(tiles, z):
        beyond = jnp.zeros_like(tiles[0])
        east = tiles[z + 1] if z + 1 < len(tiles) else beyond
        west = tiles[z - 1] if z > 0 else beyond
        wide = lane[: beyond.shape[0]]
        return jnp.where(near[: beyond.shape[0]], jnp.where(wide < HALF, east, west), 0.0)

    def packed(cells):
        return jnp.sum(pltpu.roll(cells, 0, 1, stride=EDGE, stride_axis=0), axis=0, keepdims=True)

    def tiles_of(cells):
        return [cells[:, LANES * z : LANES * (z + 1)] for z in range(4)]

    ocean = tiles_of(ocean_ref[:, 0, :])
    table = tiles_of(jnp.concatenate([slot_ref[:, 0, :].astype(jnp.float32), weight_ref[:, 0, :]], 0))
    mask = tiles_of(mask_ref[...].astype(jnp.float32))
    to_right = jnp.zeros((ROWS, LANES), jnp.float32)
    to_left = jnp.zeros((ROWS, LANES), jnp.float32)
    for group in range(LANES // EDGE):
        tile = atmos_ref[group // 2, ROWS * (group % 2) : ROWS * (group % 2 + 1), :]
        here = lane // EDGE == group
        to_right = jnp.where(here, turn(tile, EDGE * (group + 1)), to_right)
        to_left = jnp.where(here, turn(tile, EDGE * group), to_left)
    edge = jnp.where(comp == 0, to_left, to_right)
    requests = request_ref[0].astype(jnp.float32)
    for z in range(4):
        k = letter_of(z ^ space, space)
        letters_ref[k, :8, :] = ocean[z]
        letters_ref[k, 8:16, :] = table[z]
        last = jnp.where(row == 0, packed(halo(ocean, z)), 0.0)
        last = jnp.where(row == 1, packed(halo(table, z)), last)
        last = jnp.where(row == 2, mask[z], last)
        letters_ref[k, PACKED:TABLE, :] = jnp.where(row == 3, halo(mask, z), last)
        letters_ref[k, AT_EDGE:AT_ASKED, :] = edge
        letters_ref[k, AT_ASKED : AT_ASKED + 8, :] = requests[:, :LANES]
        letters_ref[k, AT_ASKED + 8 :, :] = requests[:, LANES:]
    for other in range(LEVELS):
        factors_ref[LEVELS * other : LEVELS * (other + 1), :] = jnp.broadcast_to(
            TENDENCY * mixing_ref[:, other : other + 1], (ROWS, LANES)
        )
    for field in range(FIELDS):
        other = [coupling_ref[:, FIELDS * i + field : FIELDS * i + field + 1] for i in range(2)]
        at = LEVELS * (LEVELS + field)
        factors_ref[at : at + LEVELS, :] = jnp.broadcast_to(jnp.where(lev == 0, other[1], other[0]), (ROWS, LANES))
    for level in range(LEVELS // 2):
        strip_ref[2 * ROWS * level : 2 * ROWS * (level + 1), :] = atmos_ref[level]
    strip_ref[AT_REQUEST : AT_REQUEST + 8, :] = requests[:, :LANES]
    strip_ref[AT_REQUEST + 8 :, :] = requests[:, LANES:]


def sheet_kernel(own_ref, first_ref, second_ref, last_ref, sheet_ref):
    space, comp, lev = place()
    end = at_end(space)
    sheet_ref[:TABLE, :] = own_ref[:TABLE, :]
    sheet_ref[pl.ds(jnp.where(end, 2, 1) * TABLE, TABLE), :] = first_ref[:TABLE, :]
    sheet_ref[pl.ds(jnp.where(end, 1, 2) * TABLE, TABLE), :] = last_ref[:TABLE, :]
    sheet_ref[3 * TABLE : 4 * TABLE, :] = second_ref[:TABLE, :]
    near = (space + comp) % 2 == 0
    one = jnp.where(end, last_ref[AT_EDGE:, :], first_ref[AT_EDGE:, :])
    sheet_ref[AT_HALO:, :] = jnp.where(near, one, second_ref[AT_EDGE:, :])


def margins_kernel(strip_ref, strip_beside_ref, own_ref, beside_ref, wet_ref, named_ref, rows_ref):
    space, comp, lev = place()
    lane, row = lane_of(), row_of()
    for k in range(4):
        for ref, c in ((own_ref, comp), (beside_ref, 1 - comp)):
            at = (2 * (space ^ k) + c) * TABLE
            rows_ref[pl.ds(at, TABLE), :] = ref[TABLE * k : TABLE * (k + 1), :]

    def table_row(which):
        return rows_ref[pl.ds(which, ROWS, stride=TABLE), :]

    near = (lane < EDGE // 2) | (lane >= LANES - EDGE // 2)
    wet_ref[:, :LANES] = table_row(PACKED + 2)
    wet_ref[:, LANES:] = jnp.where(near, table_row(PACKED + 3), 0.0)

    def halves(ref, at):
        return [ref[at + 8 * i : at + 8 * (i + 1), :] for i in range(2)]

    def by_comp(mine, theirs):
        return [jnp.where(comp == 0, a, b) for a, b in zip(mine, theirs)]

    strips = halves(strip_ref, AT_REQUEST), halves(strip_beside_ref, AT_REQUEST)
    halos = halves(own_ref, AT_HALO_ASKED), halves(beside_ref, AT_HALO_ASKED)
    tables = (
        (by_comp(*strips), by_comp(*strips[::-1])),
        (by_comp(*halos), by_comp(*halos[::-1])),
    )
    first = ((2 * row - 1) * LANES + 2 * (lane & (HALF - 1))).astype(jnp.float32)
    parity = (lane & 1).astype(jnp.float32)
    pairs = lane >> 1
    spread = ((0, pairs), (0, pairs + HALF), (1, jnp.where(lane < HALF, pairs, pairs + HALF)))
    table_halo = table_row(PACKED + 1)
    named = [[jnp.zeros((ROWS, LANES), jnp.float32) for _ in range(3)] for _ in range(4)]
    for margin in range(MARGINS):
        slots = (table_row(8 + margin), turn(table_halo, -EDGE * margin))
        weights = (table_row(8 + MARGINS + margin), turn(table_halo, -EDGE * (MARGINS + margin)))
        cells = []
        for slot, (low_strip, high_strip) in zip(slots, tables):
            rank = slot.astype(jnp.int32) & (2 * LANES - 1)
            late = rank >= LANES
            rank = rank & (LANES - 1)
            found = [jnp.where(late, pick_lanes(high, rank), pick_lanes(low, rank)) for low, high in (low_strip, high_strip)]
            cells.append(jnp.where(lane < HALF, found[0], found[1]) - first)
        for tile, (ring, lanes) in enumerate(spread):
            beyond = pick_lanes(cells[ring], lanes) - parity
            share = pick_lanes(weights[ring], lanes)
            for step in range(4):
                named[step][tile] = named[step][tile] + jnp.where(beyond == float(step * LANES), share, 0.0)
    for step in range(4):
        for tile in range(3):
            named_ref[step, tile] = named[step][tile]


def column_kernel(
    factors_ref,
    strip_ref,
    strip_beside_ref,
    own_ref,
    beside_ref,
    others_ref,
    wet_ref,
    named_ref,
    atmos_ref,
    final_ref,
    first_ref,
    second_ref,
    third_ref,
    state_ref,
    flux_ref,
    rows_ref,
    back_ref,
):
    space, comp, lev = place()
    lane, row = lane_of(), row_of()
    half = LEVELS // 2

    mine = pl.ds(pl.multiple_of(comp * LANES, LANES), LANES)
    theirs = pl.ds(pl.multiple_of((1 - comp) * LANES, LANES), LANES)
    for level in range(half):
        here, there = lev * half + level, (1 - lev) * half + level
        at = 2 * ROWS * level
        state_ref[here, :, mine] = strip_ref[at : at + 2 * ROWS, :]
        state_ref[there, :, mine] = others_ref[OTHER_LEVELS + at : OTHER_LEVELS + at + 2 * ROWS, :]
        state_ref[there, :, theirs] = strip_beside_ref[at : at + 2 * ROWS, :]
        state_ref[here, :, theirs] = others_ref[BESIDE_LEVELS + at : BESIDE_LEVELS + at + 2 * ROWS, :]
    exists = jnp.where(lane < HALF, space + 1, 4 - space) < 4
    halos = (
        (lev, others_ref[OTHER_HALO:BESIDE_BLOCKS, :], beside_ref[AT_HALO:AT_HALO_ASKED, :]),
        (1 - lev, own_ref[AT_HALO:AT_HALO_ASKED, :], others_ref[BESIDE_HALO:OTHER_LEVELS, :]),
    )
    for block, own, beside in halos:
        east, west = jnp.where(comp == 0, own, beside), jnp.where(comp == 0, beside, own)
        for group in range(LANES // EDGE):
            tile = jnp.where(
                lane < EDGE,
                turn(east, -EDGE * group),
                jnp.where(lane >= LANES - EDGE, turn(west, -EDGE * (group + 1)), 0.0),
            )
            state_ref[block * half + group // 2, ROWS * (group % 2) : ROWS * (group % 2 + 1), 2 * LANES :] = jnp.where(
                exists, tile, 0.0
            )
    edge_inside = jnp.where(jnp.concatenate([exists] * 2, 0), 1.0, 0.0)
    inside = jnp.concatenate([jnp.ones((2 * ROWS, 2 * LANES), jnp.float32), edge_inside], 1)

    def factor(which):
        return jnp.broadcast_to(jnp.concatenate([factors_ref[which : which + 1, :]] * 3, 1), (2 * ROWS, 3 * LANES))

    atmos = [state_ref[level] for level in range(LEVELS)]
    for substep in range(ASUB):
        shaded = [jnp.tanh(cells) for cells in atmos]
        later = []
        for level in range(LEVELS):
            cells = atmos[level]
            beside = turn(cells, 1) + turn(cells, -1) + rows_down(cells) + rows_up(cells)
            column = sum(factor(LEVELS * other + level) * shaded[other] for other in range(LEVELS))
            cells = DIFFUSE * (cells + beside) + column
            later.append(inside * cells)
        atmos = later
    for level in range(LEVELS):
        state_ref[level] = atmos[level]
    for level in range(half):
        atmos_ref[level] = state_ref[lev * half + level, :, mine]

    for field in range(FIELDS):
        flux = sum(factor(LEVELS * (LEVELS + field) + level) * atmos[level] for level in range(LEVELS))
        for tile in range(3):
            flux_ref[tile, WIDE * field : WIDE * field + 8, :] = jnp.zeros((ROWS, LANES), jnp.float32)
            flux_ref[tile, WIDE * field + 8 : WIDE * field + 24, :] = flux[:, LANES * tile : LANES * (tile + 1)]
            flux_ref[tile, WIDE * field + 24 : WIDE * field + 32, :] = jnp.zeros((ROWS, LANES), jnp.float32)

    for k in range(4):
        own, beside = 2 * (space ^ k) + comp, 2 * (space ^ k) + 1 - comp
        block = slice(TABLE * k, TABLE * (k + 1))
        came = slice(BESIDE_BLOCKS + TABLE * (k - 1), BESIDE_BLOCKS + TABLE * k)
        rows_ref[pl.ds(own * TABLE, TABLE), :] = own_ref[block, :] if k else others_ref[:TABLE, :]
        rows_ref[pl.ds(beside * TABLE, TABLE), :] = others_ref[came, :] if k else beside_ref[block, :]
    ocean_halo = rows_ref[pl.ds(PACKED, ROWS, stride=TABLE), :]

    wetness = wet_ref[...]
    pairs = (2 * lane) & (LANES - 1)
    ocean = []
    forcing = []
    for field in range(FIELDS):
        sums = []
        for tile in range(3):
            total = sum(
                named_ref[step, tile] * flux_ref[tile, pl.ds(WIDE * field + 7 + step, ROWS, stride=2), :] for step in range(4)
            )
            sums.append(pick_lanes(total + turn(total, -1), pairs))
        remapped = jnp.concatenate([jnp.where(lane < HALF, sums[0], sums[1]), sums[2]], 1)
        forcing.append(wetness * (FORCING * remapped))
        main = rows_ref[pl.ds(field, ROWS, stride=TABLE), :]
        ocean.append(jnp.concatenate([main, turn(ocean_halo, -EDGE * field)], 1))
    spreading = OCEAN_MIX * wetness
    for substep in range(SUB):
        for field in range(FIELDS):
            cells = ocean[field]
            beside = turn(cells, 1) + turn(cells, -1) + rows_down(cells) + rows_up(cells)
            ocean[field] = spreading * (cells + beside) + forcing[field]
    for field in range(FIELDS):
        cells = ocean[field][:, :LANES]
        final_ref[ROWS * field : ROWS * (field + 1), :] = cells
        back_ref[pl.ds(field, ROWS, stride=FIELDS), :] = cells
    for k, ref in zip((1, 2, 3), (first_ref, second_ref, third_ref)):
        ref[...] = back_ref[pl.ds((2 * (space ^ k) + comp) * FIELDS, FIELDS), :]


def returned_kernel(atmos_ref, final_ref, named_ref, atmos_next_ref, returned_ref):
    space, comp, lev = place()
    lane = lane_of()
    atmos_next_ref[...] = atmos_ref[...]
    named = [jnp.where(comp == 0, named_ref[step, 0], named_ref[step, 1]) for step in range(4)]
    pairs = (lane >> 1) + HALF * comp
    for field in range(FIELDS):
        spread = pick_lanes(final_ref[ROWS * field : ROWS * (field + 1), :], pairs)
        upper = named[1] * spread + rows_down(named[3] * spread)
        lower = named[2] * spread + rows_up(named[0] * spread)
        returned_ref[pl.ds(2 * ROWS * field, ROWS, stride=2), :] = upper
        returned_ref[pl.ds(2 * ROWS * field + 1, ROWS, stride=2), :] = lower


def rows_kernel(three_ref, two_ref, one_ref, final_ref, ocean_ref):
    space, comp, lev = place()
    own = final_ref[pl.ds(2 * space + comp, FIELDS, stride=ROWS), :]
    for k, cells in enumerate((own, one_ref[...], two_ref[...], three_ref[...])):
        ocean_ref[:, 0, pl.ds(pl.multiple_of((space ^ k) * LANES, LANES), LANES)] = cells


def over(axis, k, array):
    return lax.ppermute(array, axis, [(i, i ^ k) for i in range(lax.axis_size(axis))])


def across(axis, targets, array):
    pairs = [(2 * i + core, 2 * target + 1 - core) for i, target in enumerate(targets) for core in range(2)]
    return lax.ppermute(array, (axis, "lev"), pairs)


def local(kernel, out_shape, spaces, scratch=()):
    single = not isinstance(out_shape, tuple)
    vmem = pl.BlockSpec(memory_space=pltpu.VMEM)
    return pl.pallas_call(
        kernel,
        out_shape=out_shape,
        in_specs=[pl.BlockSpec(memory_space=space) for space in spaces],
        out_specs=vmem if single else (vmem,) * len(out_shape),
        scratch_shapes=list(scratch),
        compiler_params=pltpu.CompilerParams(vmem_limit_bytes=VMEM_LIMIT),
    )


def shards_by_columns(
    atmos_state,
    ocean_state,
    vertical_mixing,
    flux_coupling,
    request_cells,
    margin_slot,
    margin_weight,
    sea_mask,
):
    def values(*shape):
        return jax.ShapeDtypeStruct(shape, jnp.float32)

    arrays = (ocean_state, margin_slot, margin_weight, sea_mask, atmos_state, request_cells)
    arrays += (vertical_mixing, flux_coupling.T)
    letters, factors, strip = local(
        tables_kernel,
        (values(4, LETTER, LANES), values(2 * LEVELS * LEVELS, LANES), values(STRIP, LANES)),
        [pltpu.HBM] * 8,
        [pltpu.VMEM(a.shape, a.dtype) for a in arrays] + [pltpu.SemaphoreType.DMA((8,))],
    )(*(pltpu.with_memory_space_constraint(a, pltpu.HBM) for a in arrays))
    first, second, last = (across("space", turns, letters[at]) for at, turns in ((1, FIRST), (3, SECOND), (2, LAST)))
    strip_beside = across("comp", (1, 0), strip)
    sheet = local(sheet_kernel, values(SHEET, LANES), [pltpu.VMEM] * 4)(letters[0], first, second, last)
    sheet_beside = across("comp", (1, 0), sheet)
    swapped = (sheet[:TABLE], sheet[AT_HALO:AT_HALO_ASKED], sheet_beside[TABLE:AT_HALO_ASKED])
    swapped += (strip[:AT_REQUEST], strip_beside[:AT_REQUEST])
    others = over("lev", 1, jnp.concatenate(swapped, 0))
    wet, named = local(
        margins_kernel,
        (values(ROWS, 2 * LANES), values(4, 3, ROWS, LANES)),
        [pltpu.VMEM] * 4,
        [pltpu.VMEM((ROWS * TABLE, LANES), jnp.float32)],
    )(strip, strip_beside, sheet, sheet_beside)
    atmos, final, *back = local(
        column_kernel,
        (values(*atmos_state.shape), values(FIELDS * ROWS, LANES)) + (values(FIELDS, LANES),) * 3,
        [pltpu.VMEM] * 8,
        [
            pltpu.VMEM((LEVELS, 2 * ROWS, 3 * LANES), jnp.float32),
            pltpu.VMEM((3, FIELDS * WIDE, LANES), jnp.float32),
            pltpu.VMEM((ROWS * TABLE, LANES), jnp.float32),
            pltpu.VMEM((ROWS * FIELDS, LANES), jnp.float32),
        ],
    )(factors, strip, strip_beside, sheet, sheet_beside, others, wet, named)
    one, two, three = (across("space", [z ^ k for z in range(4)], piece) for k, piece in zip((1, 2, 3), back))
    final = over("lev", 1, final)
    atmos_next, returned = local(
        returned_kernel,
        (values(*atmos_state.shape), values(FIELDS * 2 * ROWS, LANES)),
        [pltpu.VMEM] * 3,
    )(atmos, final, named)
    ocean_next = local(rows_kernel, values(*ocean_state.shape), [pltpu.VMEM] * 4)(three, two, one, final)
    return (atmos_next, ocean_next, returned.reshape(FIELDS, 2 * ROWS, LANES))


def shards(*arguments):
    atmos_state, ocean_state, mixing, coupling, request_cells, margin_slot = arguments[:6]
    by_columns = (
        (lax.axis_size("space"), lax.axis_size("comp"), lax.axis_size("lev")) == (4, 2, 2)
        and atmos_state.shape == (LEVELS // 2, 2 * ROWS, LANES)
        and ocean_state.shape == (FIELDS, 1, 4 * LANES)
        and request_cells.shape == (1, ROWS, 2 * LANES)
        and margin_slot.shape[0] == MARGINS
    )
    return (shards_by_columns if by_columns else shards_by_neighbours)(*arguments)


def solution(mesh):
    placed = (
        P(("parts", "lev"), None, ("space", "comp")),
        P(("parts", "lev"), ("space", "comp"), None),
        P(),
        P(),
        P(("space", "comp"), None, None),
        P(None, ("space", "comp"), None),
        P(None, ("space", "comp"), None),
        P(("space", "comp"), None),
    )
    return jax.shard_map(
        shards,
        mesh=mesh,
        in_specs=placed,
        out_specs=(
            P(("parts", "lev"), None, ("space", "comp")),
            P(("parts", "lev"), ("space", "comp"), None),
            P(("parts", "lev"), None, ("space", "comp")),
        ),
        check_vma=False,
    )
```

```python
import jax
import jax.numpy as jnp
from jax import lax
from jax.experimental import pallas as pl
from jax.experimental.pallas import tpu as pltpu
from jax.sharding import PartitionSpec as P

ASUB = 2
SUB = 8


DIFFUSE = 0.2
TENDENCY = 0.25
OCEAN_MIX = 0.2
FORCING = 0.15


def with_halo(cells, sides, width):
    for axis, dim in sides:
        count = lax.axis_size(axis)
        ends = count - 1
        head = lax.slice_in_dim(cells, 0, width, axis=dim)
        tail = lax.slice_in_dim(cells, cells.shape[dim] - width, cells.shape[dim], axis=dim)
        cells = jnp.concatenate(
            [
                lax.ppermute(tail, axis, [(i, (i + 1) % count) for i in range(ends)]),
                cells,
                lax.ppermute(head, axis, [((i + 1) % count, i) for i in range(ends)]),
            ],
            axis=dim,
        )
    return cells


def atmos_step(atmos, mixing_rows):
    lev_local = atmos.shape[0]
    padded = with_halo(atmos, ((("space", "comp"), 2),), 1)
    padded = jnp.pad(padded, ((0, 0), (1, 1), (0, 0)))
    beside = padded[:, 2:, 1:-1] + padded[:, :-2, 1:-1] + padded[:, 1:-1, 2:] + padded[:, 1:-1, :-2]
    shaded = jnp.tanh(atmos).reshape(lev_local, -1)
    column = jnp.dot(
        mixing_rows,
        lax.all_gather(shaded, "lev", axis=0, tiled=True),
        precision=lax.Precision.HIGHEST,
    )
    return atmos + DIFFUSE * (beside - 4.0 * atmos) + TENDENCY * column.reshape(atmos.shape)


def advance(padded, wetness, forcing):
    centre = padded[:, 1:-1, 1:-1]
    beside = padded[:, 2:, 1:-1] + padded[:, :-2, 1:-1] + padded[:, 1:-1, 2:] + padded[:, 1:-1, :-2]
    return wetness[None] * (centre + OCEAN_MIX * (beside - 4.0 * centre) + FORCING * forcing)


def shards_by_neighbours(
    atmos_state,
    ocean_state,
    vertical_mixing,
    flux_coupling,
    request_cells,
    margin_slot,
    margin_weight,
    sea_mask,
):
    lev_local, rows_atmos, cols_atmos = atmos_state.shape
    fields_local = ocean_state.shape[0]
    margins = margin_slot.shape[0]
    lev_place = lax.axis_index("lev")
    mixing_rows = lax.dynamic_slice_in_dim(vertical_mixing, lev_place * lev_local, lev_local, 0)
    coupling_cols = lax.dynamic_slice_in_dim(flux_coupling, lev_place * lev_local, lev_local, 1)
    atmos = atmos_state
    for substep in range(ASUB):
        atmos = atmos_step(atmos, mixing_rows)
    flat_atmos = atmos.reshape(lev_local, -1)
    fluxes = lax.psum_scatter(
        jnp.dot(coupling_cols, flat_atmos, precision=lax.Precision.HIGHEST),
        "lev",
        scatter_dimension=0,
        tiled=True,
    )
    requests = request_cells.reshape(-1)
    outgoing = jnp.take(fluxes, requests, axis=1)
    slot_flat = margin_slot.reshape(-1)
    weight_flat = margin_weight.reshape(margins, -1)
    received = lax.all_to_all(outgoing, ("space", "comp"), split_axis=1, concat_axis=1, tiled=True)
    picked = jnp.take(received, slot_flat, axis=1).reshape(received.shape[0], margins, -1)
    remapped = jnp.sum(picked * weight_flat[None], axis=1)
    forcing = remapped.reshape(ocean_state.shape)
    wetness = sea_mask.astype(jnp.float32)
    ocean_now = ocean_state
    for substep in range(SUB):
        padded = with_halo(ocean_now, ((("space", "comp"), 1),), 1)
        padded = jnp.pad(padded, ((0, 0), (0, 0), (1, 1)))
        ocean_now = advance(padded, wetness, forcing)
    weighted = (weight_flat[None] * ocean_now).reshape(fields_local, -1)
    outgoing_back = (
        jnp.zeros((fields_local, requests.shape[0]), jnp.float32).at[:, slot_flat].add(weighted)
    )
    arrived = lax.all_to_all(
        outgoing_back, ("space", "comp"), split_axis=1, concat_axis=1, tiled=True
    )
    returned = (
        jnp.zeros((fields_local, rows_atmos * cols_atmos), jnp.float32).at[:, requests].add(arrived)
    )
    return (atmos, ocean_now, returned.reshape(fields_local, rows_atmos, cols_atmos))


LANES = 128
HALF = 64
ROWS = 8
LEVELS = 8
FIELDS = 8
MARGINS = 4
TABLE = 24
PACKED = 16
TABLES = 4 * TABLE
AT_EDGE = TABLE
AT_ASKED = AT_EDGE + 8
LETTER = AT_ASKED + 16
AT_LEVELS = TABLE
AT_REQUEST = AT_LEVELS + 64
STRIP = AT_REQUEST + 16
AT_HALO = 3 * TABLE
AT_HALO_ASKED = AT_HALO + 8
AT_MORE_LEVELS = AT_HALO_ASKED + 16
SHEET = AT_MORE_LEVELS + 64
OTHER_HALO = AT_REQUEST
EDGE = 16
WIDE = 32
VMEM_LIMIT = 4 * 1024 * 1024


def lane_of(shape=(ROWS, LANES)):
    return lax.broadcasted_iota(jnp.int32, shape, 1)


def row_of(shape=(ROWS, LANES)):
    return lax.broadcasted_iota(jnp.int32, shape, 0)


def pick_lanes(tile, lanes):
    return jnp.take_along_axis(tile, lanes, axis=1, mode="promise_in_bounds")


def turn(tile, by):
    by = by % tile.shape[1]
    return pltpu.roll(tile, by, 1) if by else tile


def rows_down(tile):
    return jnp.where(row_of(tile.shape) == 0, 0.0, pltpu.roll(tile, 1, 0))


def rows_up(tile):
    last = tile.shape[0] - 1
    return jnp.where(row_of(tile.shape) == last, 0.0, pltpu.roll(tile, last, 0))


def place():
    return lax.axis_index("space"), lax.axis_index("comp"), lax.axis_index("lev")


FIRST = (1, 3, 0, 2)
SECOND = (3, 2, 1, 0)
LAST = (2, 0, 3, 1)


def at_end(space):
    return (space == 0) | (space == 3)


def letter_of(k, space):
    return jnp.where((k == 1) | (k == 2), jnp.where(at_end(space), k, 3 - k), k)


def tables_kernel(*refs):
    arrays, (letters_ref, factors_ref, strip_ref), held, arrived = refs[:8], refs[8:11], refs[11:-1], refs[-1]
    copies = [pltpu.make_async_copy(a, h, arrived.at[i]) for i, (a, h) in enumerate(zip(arrays, held))]
    for copy in copies:
        copy.start()
    for copy in copies:
        copy.wait()
    ocean_ref, slot_ref, weight_ref, mask_ref, atmos_ref, request_ref, mixing_ref, coupling_ref = held
    space, comp, lev = place()
    lane, row = lane_of(), row_of()
    near = (lane < EDGE // 2) | (lane >= LANES - EDGE // 2)

    def halo(tiles, z):
        beyond = jnp.zeros_like(tiles[0])
        east = tiles[z + 1] if z + 1 < len(tiles) else beyond
        west = tiles[z - 1] if z > 0 else beyond
        wide = lane[: beyond.shape[0]]
        return jnp.where(near[: beyond.shape[0]], jnp.where(wide < HALF, east, west), 0.0)

    def packed(cells):
        return jnp.sum(pltpu.roll(cells, 0, 1, stride=EDGE, stride_axis=0), axis=0, keepdims=True)

    def tiles_of(cells):
        return [cells[:, LANES * z : LANES * (z + 1)] for z in range(4)]

    ocean = tiles_of(ocean_ref[:, 0, :])
    table = tiles_of(jnp.concatenate([slot_ref[:, 0, :].astype(jnp.float32), weight_ref[:, 0, :]], 0))
    mask = tiles_of(mask_ref[...].astype(jnp.float32))
    to_right = jnp.zeros((ROWS, LANES), jnp.float32)
    to_left = jnp.zeros((ROWS, LANES), jnp.float32)
    for group in range(LANES // EDGE):
        tile = atmos_ref[group // 2, ROWS * (group % 2) : ROWS * (group % 2 + 1), :]
        here = lane // EDGE == group
        to_right = jnp.where(here, turn(tile, EDGE * (group + 1)), to_right)
        to_left = jnp.where(here, turn(tile, EDGE * group), to_left)
    edge = jnp.where(comp == 0, to_left, to_right)
    requests = request_ref[0].astype(jnp.float32)
    for z in range(4):
        k = letter_of(z ^ space, space)
        letters_ref[k, :8, :] = ocean[z]
        letters_ref[k, 8:16, :] = table[z]
        last = jnp.where(row == 0, packed(halo(ocean, z)), 0.0)
        last = jnp.where(row == 1, packed(halo(table, z)), last)
        last = jnp.where(row == 2, mask[z], last)
        letters_ref[k, PACKED:TABLE, :] = jnp.where(row == 3, halo(mask, z), last)
        letters_ref[k, AT_EDGE:AT_ASKED, :] = edge
        letters_ref[k, AT_ASKED : AT_ASKED + 8, :] = requests[:, :LANES]
        letters_ref[k, AT_ASKED + 8 :, :] = requests[:, LANES:]
    for other in range(LEVELS):
        factors_ref[LEVELS * other : LEVELS * (other + 1), :] = jnp.broadcast_to(
            TENDENCY * mixing_ref[:, other : other + 1], (ROWS, LANES)
        )
    for field in range(FIELDS):
        other = [coupling_ref[:, FIELDS * i + field : FIELDS * i + field + 1] for i in range(2)]
        at = LEVELS * (LEVELS + field)
        factors_ref[at : at + LEVELS, :] = jnp.broadcast_to(jnp.where(lev == 0, other[1], other[0]), (ROWS, LANES))
    for level in range(LEVELS // 2):
        strip_ref[AT_LEVELS + 2 * ROWS * level : AT_LEVELS + 2 * ROWS * (level + 1), :] = atmos_ref[level]
    strip_ref[:TABLE, :] = letters_ref[0, :TABLE, :]
    strip_ref[AT_REQUEST : AT_REQUEST + 8, :] = requests[:, :LANES]
    strip_ref[AT_REQUEST + 8 :, :] = requests[:, LANES:]


def sheet_kernel(strip_ref, last_ref, second_ref, first_ref, sheet_ref):
    space, comp, lev = place()
    end = at_end(space)
    sheet_ref[pl.ds(jnp.where(end, 1, 0) * TABLE, TABLE), :] = first_ref[:TABLE, :]
    sheet_ref[pl.ds(jnp.where(end, 0, 1) * TABLE, TABLE), :] = last_ref[:TABLE, :]
    sheet_ref[2 * TABLE : 3 * TABLE, :] = second_ref[:TABLE, :]
    near = (space + comp) % 2 == 0
    one = jnp.where(end, last_ref[AT_EDGE:, :], first_ref[AT_EDGE:, :])
    sheet_ref[AT_HALO:AT_MORE_LEVELS, :] = jnp.where(near, one, second_ref[AT_EDGE:, :])
    sheet_ref[AT_MORE_LEVELS:, :] = strip_ref[AT_LEVELS:AT_REQUEST, :]


def gather_rows(rows_ref, own, beside):
    space, comp, lev = place()
    for k in range(4):
        for (start_ref, came_ref), c in ((own, comp), (beside, 1 - comp)):
            block = came_ref[TABLE * (k - 1) : TABLE * k, :] if k else start_ref[:TABLE, :]
            rows_ref[pl.ds((2 * (space ^ k) + c) * TABLE, TABLE), :] = block


def margins_kernel(strip_ref, strip_beside_ref, own_ref, beside_ref, wet_ref, named_ref, rows_ref):
    space, comp, lev = place()
    lane, row = lane_of(), row_of()
    gather_rows(rows_ref, (strip_ref, own_ref), (strip_beside_ref, beside_ref))

    def table_row(which):
        return rows_ref[pl.ds(which, ROWS, stride=TABLE), :]

    near = (lane < EDGE // 2) | (lane >= LANES - EDGE // 2)
    wet_ref[:, :LANES] = table_row(PACKED + 2)
    wet_ref[:, LANES:] = jnp.where(near, table_row(PACKED + 3), 0.0)

    def halves(ref, at):
        return [ref[at + 8 * i : at + 8 * (i + 1), :] for i in range(2)]

    def by_comp(mine, theirs):
        return [jnp.where(comp == 0, a, b) for a, b in zip(mine, theirs)]

    strips = halves(strip_ref, AT_REQUEST), halves(strip_beside_ref, AT_REQUEST)
    halos = halves(own_ref, AT_HALO_ASKED), halves(beside_ref, AT_HALO_ASKED)
    tables = (
        (by_comp(*strips), by_comp(*strips[::-1])),
        (by_comp(*halos), by_comp(*halos[::-1])),
    )
    first = ((2 * row - 1) * LANES + 2 * (lane & (HALF - 1))).astype(jnp.float32)
    parity = (lane & 1).astype(jnp.float32)
    pairs = lane >> 1
    spread = ((0, pairs), (0, pairs + HALF), (1, jnp.where(lane < HALF, pairs, pairs + HALF)))
    table_halo = table_row(PACKED + 1)
    named = [[jnp.zeros((ROWS, LANES), jnp.float32) for _ in range(3)] for _ in range(4)]
    for margin in range(MARGINS):
        slots = (table_row(8 + margin), turn(table_halo, -EDGE * margin))
        weights = (table_row(8 + MARGINS + margin), turn(table_halo, -EDGE * (MARGINS + margin)))
        cells = []
        for slot, (low_strip, high_strip) in zip(slots, tables):
            rank = slot.astype(jnp.int32) & (2 * LANES - 1)
            late = rank >= LANES
            rank = rank & (LANES - 1)
            found = [jnp.where(late, pick_lanes(high, rank), pick_lanes(low, rank)) for low, high in (low_strip, high_strip)]
            cells.append(jnp.where(lane < HALF, found[0], found[1]) - first)
        for tile, (ring, lanes) in enumerate(spread):
            beyond = pick_lanes(cells[ring], lanes) - parity
            share = pick_lanes(weights[ring], lanes)
            for step in range(4):
                named[step][tile] = named[step][tile] + jnp.where(beyond == float(step * LANES), share, 0.0)
    for step in range(4):
        for tile in range(3):
            named_ref[step, tile] = named[step][tile]


def column_kernel(
    factors_ref,
    strip_ref,
    strip_beside_ref,
    own_ref,
    beside_ref,
    other_ref,
    halo_beside_ref,
    wet_ref,
    named_ref,
    atmos_ref,
    final_ref,
    first_ref,
    second_ref,
    third_ref,
    state_ref,
    flux_ref,
    rows_ref,
    back_ref,
):
    space, comp, lev = place()
    lane, row = lane_of(), row_of()
    half = LEVELS // 2

    mine = pl.ds(pl.multiple_of(comp * LANES, LANES), LANES)
    theirs = pl.ds(pl.multiple_of((1 - comp) * LANES, LANES), LANES)
    for level in range(half):
        here, there = lev * half + level, (1 - lev) * half + level
        at = 2 * ROWS * level
        rows = slice(AT_LEVELS + at, AT_LEVELS + at + 2 * ROWS)
        state_ref[here, :, mine] = strip_ref[rows, :]
        state_ref[there, :, mine] = other_ref[rows, :]
        state_ref[there, :, theirs] = strip_beside_ref[rows, :]
        state_ref[here, :, theirs] = beside_ref[AT_MORE_LEVELS + at : AT_MORE_LEVELS + at + 2 * ROWS, :]
    exists = jnp.where(lane < HALF, space + 1, 4 - space) < 4
    halos = (
        (lev, other_ref[OTHER_HALO:, :], halo_beside_ref[...]),
        (1 - lev, own_ref[AT_HALO:AT_HALO_ASKED, :], beside_ref[AT_HALO:AT_HALO_ASKED, :]),
    )
    for block, own, beside in halos:
        east, west = jnp.where(comp == 0, own, beside), jnp.where(comp == 0, beside, own)
        for group in range(LANES // EDGE):
            tile = jnp.where(
                lane < EDGE,
                turn(east, -EDGE * group),
                jnp.where(lane >= LANES - EDGE, turn(west, -EDGE * (group + 1)), 0.0),
            )
            state_ref[block * half + group // 2, ROWS * (group % 2) : ROWS * (group % 2 + 1), 2 * LANES :] = jnp.where(
                exists, tile, 0.0
            )
    edge_inside = jnp.where(jnp.concatenate([exists] * 2, 0), 1.0, 0.0)
    inside = jnp.concatenate([jnp.ones((2 * ROWS, 2 * LANES), jnp.float32), edge_inside], 1)

    def factor(which):
        return jnp.broadcast_to(jnp.concatenate([factors_ref[which : which + 1, :]] * 3, 1), (2 * ROWS, 3 * LANES))

    atmos = [state_ref[level] for level in range(LEVELS)]
    for substep in range(ASUB):
        shaded = [jnp.tanh(cells) for cells in atmos]
        later = []
        for level in range(LEVELS):
            cells = atmos[level]
            beside = turn(cells, 1) + turn(cells, -1) + rows_down(cells) + rows_up(cells)
            column = sum(factor(LEVELS * other + level) * shaded[other] for other in range(LEVELS))
            cells = DIFFUSE * (cells + beside) + column
            later.append(inside * cells)
        atmos = later
    for level in range(LEVELS):
        state_ref[level] = atmos[level]
    for level in range(half):
        atmos_ref[level] = state_ref[lev * half + level, :, mine]

    for field in range(FIELDS):
        flux = sum(factor(LEVELS * (LEVELS + field) + level) * atmos[level] for level in range(LEVELS))
        for tile in range(3):
            flux_ref[tile, WIDE * field : WIDE * field + 8, :] = jnp.zeros((ROWS, LANES), jnp.float32)
            flux_ref[tile, WIDE * field + 8 : WIDE * field + 24, :] = flux[:, LANES * tile : LANES * (tile + 1)]
            flux_ref[tile, WIDE * field + 24 : WIDE * field + 32, :] = jnp.zeros((ROWS, LANES), jnp.float32)

    gather_rows(rows_ref, (other_ref, own_ref), (strip_beside_ref, beside_ref))
    ocean_halo = rows_ref[pl.ds(PACKED, ROWS, stride=TABLE), :]

    wetness = wet_ref[...]
    pairs = (2 * lane) & (LANES - 1)
    ocean = []
    forcing = []
    for field in range(FIELDS):
        sums = []
        for tile in range(3):
            total = sum(
                named_ref[step, tile] * flux_ref[tile, pl.ds(WIDE * field + 7 + step, ROWS, stride=2), :] for step in range(4)
            )
            sums.append(pick_lanes(total + turn(total, -1), pairs))
        remapped = jnp.concatenate([jnp.where(lane < HALF, sums[0], sums[1]), sums[2]], 1)
        forcing.append(wetness * (FORCING * remapped))
        main = rows_ref[pl.ds(field, ROWS, stride=TABLE), :]
        ocean.append(jnp.concatenate([main, turn(ocean_halo, -EDGE * field)], 1))
    spreading = OCEAN_MIX * wetness
    for substep in range(SUB):
        for field in range(FIELDS):
            cells = ocean[field]
            beside = turn(cells, 1) + turn(cells, -1) + rows_down(cells) + rows_up(cells)
            ocean[field] = spreading * (cells + beside) + forcing[field]
    for field in range(FIELDS):
        cells = ocean[field][:, :LANES]
        final_ref[ROWS * field : ROWS * (field + 1), :] = cells
        back_ref[pl.ds(field, ROWS, stride=FIELDS), :] = cells
    for k, ref in zip((1, 2, 3), (first_ref, second_ref, third_ref)):
        ref[...] = back_ref[pl.ds((2 * (space ^ k) + comp) * FIELDS, FIELDS), :]


def returned_kernel(atmos_ref, final_ref, named_ref, atmos_next_ref, returned_ref):
    space, comp, lev = place()
    lane = lane_of()
    atmos_next_ref[...] = atmos_ref[...]
    named = [jnp.where(comp == 0, named_ref[step, 0], named_ref[step, 1]) for step in range(4)]
    pairs = (lane >> 1) + HALF * comp
    for field in range(FIELDS):
        spread = pick_lanes(final_ref[ROWS * field : ROWS * (field + 1), :], pairs)
        upper = named[1] * spread + rows_down(named[3] * spread)
        lower = named[2] * spread + rows_up(named[0] * spread)
        returned_ref[pl.ds(2 * ROWS * field, ROWS, stride=2), :] = upper
        returned_ref[pl.ds(2 * ROWS * field + 1, ROWS, stride=2), :] = lower


def rows_kernel(three_ref, two_ref, one_ref, final_ref, ocean_ref):
    space, comp, lev = place()
    own = final_ref[pl.ds(2 * space + comp, FIELDS, stride=ROWS), :]
    for k, cells in enumerate((own, one_ref[...], two_ref[...], three_ref[...])):
        ocean_ref[:, 0, pl.ds(pl.multiple_of((space ^ k) * LANES, LANES), LANES)] = cells


def over(axis, k, array):
    return lax.ppermute(array, axis, [(i, i ^ k) for i in range(lax.axis_size(axis))])


def across(axis, targets, array):
    pairs = [(2 * i + core, 2 * target + 1 - core) for i, target in enumerate(targets) for core in range(2)]
    return lax.ppermute(array, (axis, "lev"), pairs)


def local(kernel, out_shape, spaces, scratch=()):
    single = not isinstance(out_shape, tuple)
    vmem = pl.BlockSpec(memory_space=pltpu.VMEM)
    return pl.pallas_call(
        kernel,
        out_shape=out_shape,
        in_specs=[pl.BlockSpec(memory_space=space) for space in spaces],
        out_specs=vmem if single else (vmem,) * len(out_shape),
        scratch_shapes=list(scratch),
        compiler_params=pltpu.CompilerParams(vmem_limit_bytes=VMEM_LIMIT),
    )


def shards_by_columns(
    atmos_state,
    ocean_state,
    vertical_mixing,
    flux_coupling,
    request_cells,
    margin_slot,
    margin_weight,
    sea_mask,
):
    def values(*shape):
        return jax.ShapeDtypeStruct(shape, jnp.float32)

    arrays = (ocean_state, margin_slot, margin_weight, sea_mask, atmos_state, request_cells)
    arrays += (vertical_mixing, flux_coupling.T)
    letters, factors, strip = local(
        tables_kernel,
        (values(4, LETTER, LANES), values(2 * LEVELS * LEVELS, LANES), values(STRIP, LANES)),
        [pltpu.HBM] * 8,
        [pltpu.VMEM(a.shape, a.dtype) for a in arrays] + [pltpu.SemaphoreType.DMA((8,))],
    )(*(pltpu.with_memory_space_constraint(a, pltpu.HBM) for a in arrays))
    first, second, last = (across("space", turns, letters[at]) for at, turns in ((1, FIRST), (3, SECOND), (2, LAST)))
    strip_beside = across("comp", (1, 0), strip)
    sheet = local(sheet_kernel, values(SHEET, LANES), [pltpu.VMEM] * 4)(strip, last, second, first)
    sheet_beside = over("comp", 1, sheet)
    halo = sheet[AT_HALO:AT_HALO_ASKED]
    halo_beside = lax.ppermute(halo, ("comp", "lev"), [(0, 3), (3, 0), (1, 2), (2, 1)])
    other = over("lev", 1, jnp.concatenate([strip[:AT_REQUEST], halo], 0))
    wet, named = local(
        margins_kernel,
        (values(ROWS, 2 * LANES), values(4, 3, ROWS, LANES)),
        [pltpu.VMEM] * 4,
        [pltpu.VMEM((ROWS * TABLE, LANES), jnp.float32)],
    )(strip, strip_beside, sheet, sheet_beside)
    atmos, final, *back = local(
        column_kernel,
        (values(*atmos_state.shape), values(FIELDS * ROWS, LANES)) + (values(FIELDS, LANES),) * 3,
        [pltpu.VMEM] * 9,
        [
            pltpu.VMEM((LEVELS, 2 * ROWS, 3 * LANES), jnp.float32),
            pltpu.VMEM((3, FIELDS * WIDE, LANES), jnp.float32),
            pltpu.VMEM((ROWS * TABLE, LANES), jnp.float32),
            pltpu.VMEM((ROWS * FIELDS, LANES), jnp.float32),
        ],
    )(factors, strip, strip_beside, sheet, sheet_beside, other, halo_beside, wet, named)
    one, two, three = (across("space", [z ^ k for z in range(4)], piece) for k, piece in zip((1, 2, 3), back))
    final = over("lev", 1, final)
    atmos_next, returned = local(
        returned_kernel,
        (values(*atmos_state.shape), values(FIELDS * 2 * ROWS, LANES)),
        [pltpu.VMEM] * 3,
    )(atmos, final, named)
    ocean_next = local(rows_kernel, values(*ocean_state.shape), [pltpu.VMEM] * 4)(three, two, one, final)
    return (atmos_next, ocean_next, returned.reshape(FIELDS, 2 * ROWS, LANES))


def shards(*arguments):
    atmos_state, ocean_state, mixing, coupling, request_cells, margin_slot = arguments[:6]
    by_columns = (
        (lax.axis_size("space"), lax.axis_size("comp"), lax.axis_size("lev")) == (4, 2, 2)
        and atmos_state.shape == (LEVELS // 2, 2 * ROWS, LANES)
        and ocean_state.shape == (FIELDS, 1, 4 * LANES)
        and request_cells.shape == (1, ROWS, 2 * LANES)
        and margin_slot.shape[0] == MARGINS
    )
    return (shards_by_columns if by_columns else shards_by_neighbours)(*arguments)


def solution(mesh):
    placed = (
        P(("parts", "lev"), None, ("space", "comp")),
        P(("parts", "lev"), ("space", "comp"), None),
        P(),
        P(),
        P(("space", "comp"), None, None),
        P(None, ("space", "comp"), None),
        P(None, ("space", "comp"), None),
        P(("space", "comp"), None),
    )
    return jax.shard_map(
        shards,
        mesh=mesh,
        in_specs=placed,
        out_specs=(
            P(("parts", "lev"), None, ("space", "comp")),
            P(("parts", "lev"), ("space", "comp"), None),
            P(("parts", "lev"), None, ("space", "comp")),
        ),
        check_vma=False,
    )
```

```python
import jax
import jax.numpy as jnp
from jax import lax
from jax.experimental import pallas as pl
from jax.experimental.pallas import tpu as pltpu
from jax.sharding import PartitionSpec as P

ASUB = 2
SUB = 8


DIFFUSE = 0.2
TENDENCY = 0.25
OCEAN_MIX = 0.2
FORCING = 0.15


def with_halo(cells, sides, width):
    for axis, dim in sides:
        count = lax.axis_size(axis)
        ends = count - 1
        head = lax.slice_in_dim(cells, 0, width, axis=dim)
        tail = lax.slice_in_dim(cells, cells.shape[dim] - width, cells.shape[dim], axis=dim)
        cells = jnp.concatenate(
            [
                lax.ppermute(tail, axis, [(i, (i + 1) % count) for i in range(ends)]),
                cells,
                lax.ppermute(head, axis, [((i + 1) % count, i) for i in range(ends)]),
            ],
            axis=dim,
        )
    return cells


def atmos_step(atmos, mixing_rows):
    lev_local = atmos.shape[0]
    padded = with_halo(atmos, ((("space", "comp"), 2),), 1)
    padded = jnp.pad(padded, ((0, 0), (1, 1), (0, 0)))
    beside = padded[:, 2:, 1:-1] + padded[:, :-2, 1:-1] + padded[:, 1:-1, 2:] + padded[:, 1:-1, :-2]
    shaded = jnp.tanh(atmos).reshape(lev_local, -1)
    column = jnp.dot(
        mixing_rows,
        lax.all_gather(shaded, "lev", axis=0, tiled=True),
        precision=lax.Precision.HIGHEST,
    )
    return atmos + DIFFUSE * (beside - 4.0 * atmos) + TENDENCY * column.reshape(atmos.shape)


def advance(padded, wetness, forcing):
    centre = padded[:, 1:-1, 1:-1]
    beside = padded[:, 2:, 1:-1] + padded[:, :-2, 1:-1] + padded[:, 1:-1, 2:] + padded[:, 1:-1, :-2]
    return wetness[None] * (centre + OCEAN_MIX * (beside - 4.0 * centre) + FORCING * forcing)


def shards_by_neighbours(
    atmos_state,
    ocean_state,
    vertical_mixing,
    flux_coupling,
    request_cells,
    margin_slot,
    margin_weight,
    sea_mask,
):
    lev_local, rows_atmos, cols_atmos = atmos_state.shape
    fields_local = ocean_state.shape[0]
    margins = margin_slot.shape[0]
    lev_place = lax.axis_index("lev")
    mixing_rows = lax.dynamic_slice_in_dim(vertical_mixing, lev_place * lev_local, lev_local, 0)
    coupling_cols = lax.dynamic_slice_in_dim(flux_coupling, lev_place * lev_local, lev_local, 1)
    atmos = atmos_state
    for substep in range(ASUB):
        atmos = atmos_step(atmos, mixing_rows)
    flat_atmos = atmos.reshape(lev_local, -1)
    fluxes = lax.psum_scatter(
        jnp.dot(coupling_cols, flat_atmos, precision=lax.Precision.HIGHEST),
        "lev",
        scatter_dimension=0,
        tiled=True,
    )
    requests = request_cells.reshape(-1)
    outgoing = jnp.take(fluxes, requests, axis=1)
    slot_flat = margin_slot.reshape(-1)
    weight_flat = margin_weight.reshape(margins, -1)
    received = lax.all_to_all(outgoing, ("space", "comp"), split_axis=1, concat_axis=1, tiled=True)
    picked = jnp.take(received, slot_flat, axis=1).reshape(received.shape[0], margins, -1)
    remapped = jnp.sum(picked * weight_flat[None], axis=1)
    forcing = remapped.reshape(ocean_state.shape)
    wetness = sea_mask.astype(jnp.float32)
    ocean_now = ocean_state
    for substep in range(SUB):
        padded = with_halo(ocean_now, ((("space", "comp"), 1),), 1)
        padded = jnp.pad(padded, ((0, 0), (0, 0), (1, 1)))
        ocean_now = advance(padded, wetness, forcing)
    weighted = (weight_flat[None] * ocean_now).reshape(fields_local, -1)
    outgoing_back = (
        jnp.zeros((fields_local, requests.shape[0]), jnp.float32).at[:, slot_flat].add(weighted)
    )
    arrived = lax.all_to_all(
        outgoing_back, ("space", "comp"), split_axis=1, concat_axis=1, tiled=True
    )
    returned = (
        jnp.zeros((fields_local, rows_atmos * cols_atmos), jnp.float32).at[:, requests].add(arrived)
    )
    return (atmos, ocean_now, returned.reshape(fields_local, rows_atmos, cols_atmos))


LANES = 128
HALF = 64
ROWS = 8
LEVELS = 8
FIELDS = 8
MARGINS = 4
TABLE = 24
PACKED = 16
TABLES = 4 * TABLE
AT_EDGE = TABLE
AT_ASKED = AT_EDGE + 8
LETTER = AT_ASKED + 16
AT_LEVELS = TABLE
AT_REQUEST = AT_LEVELS + 64
STRIP = AT_REQUEST + 16
AT_HALO = 3 * TABLE
AT_HALO_ASKED = AT_HALO + 8
AT_MORE_LEVELS = AT_HALO_ASKED + 16
SHEET = AT_MORE_LEVELS + 64
OTHER_HALO = AT_REQUEST
EDGE = 16
WIDE = 32
VMEM_LIMIT = 4 * 1024 * 1024


def lane_of(shape=(ROWS, LANES)):
    return lax.broadcasted_iota(jnp.int32, shape, 1)


def row_of(shape=(ROWS, LANES)):
    return lax.broadcasted_iota(jnp.int32, shape, 0)


def pick_lanes(tile, lanes):
    return jnp.take_along_axis(tile, lanes, axis=1, mode="promise_in_bounds")


def turn(tile, by):
    by = by % tile.shape[1]
    return pltpu.roll(tile, by, 1) if by else tile


def rows_down(tile):
    return jnp.where(row_of(tile.shape) == 0, 0.0, pltpu.roll(tile, 1, 0))


def rows_up(tile):
    last = tile.shape[0] - 1
    return jnp.where(row_of(tile.shape) == last, 0.0, pltpu.roll(tile, last, 0))


def place():
    return lax.axis_index("space"), lax.axis_index("comp"), lax.axis_index("lev")


FIRST = (1, 3, 0, 2)
SECOND = (3, 2, 1, 0)
LAST = (2, 0, 3, 1)


def at_end(space):
    return (space == 0) | (space == 3)


def letter_of(k, space):
    return jnp.where((k == 1) | (k == 2), jnp.where(at_end(space), k, 3 - k), k)


def tables_kernel(*refs):
    arrays, (letters_ref, strip_ref, mixed_ref, coupled_ref), held, arrived = refs[:8], refs[8:12], refs[12:-1], refs[-1]
    copies = [pltpu.make_async_copy(a, h, arrived.at[i]) for i, (a, h) in enumerate(zip(arrays, held))]
    for copy in copies:
        copy.start()
    for copy in copies:
        copy.wait()
    ocean_ref, slot_ref, weight_ref, mask_ref, atmos_ref, request_ref, mixing_ref, coupling_ref = held
    space, comp, lev = place()
    lane, row = lane_of(), row_of()
    near = (lane < EDGE // 2) | (lane >= LANES - EDGE // 2)

    def halo(tiles, z):
        beyond = jnp.zeros_like(tiles[0])
        east = tiles[z + 1] if z + 1 < len(tiles) else beyond
        west = tiles[z - 1] if z > 0 else beyond
        wide = lane[: beyond.shape[0]]
        return jnp.where(near[: beyond.shape[0]], jnp.where(wide < HALF, east, west), 0.0)

    def packed(cells):
        return jnp.sum(pltpu.roll(cells, 0, 1, stride=EDGE, stride_axis=0), axis=0, keepdims=True)

    def tiles_of(cells):
        return [cells[:, LANES * z : LANES * (z + 1)] for z in range(4)]

    ocean = tiles_of(ocean_ref[:, 0, :])
    table = tiles_of(jnp.concatenate([slot_ref[:, 0, :].astype(jnp.float32), weight_ref[:, 0, :]], 0))
    mask = tiles_of(mask_ref[...].astype(jnp.float32))
    to_right = jnp.zeros((ROWS, LANES), jnp.float32)
    to_left = jnp.zeros((ROWS, LANES), jnp.float32)
    for group in range(LANES // EDGE):
        tile = atmos_ref[group // 2, ROWS * (group % 2) : ROWS * (group % 2 + 1), :]
        here = lane // EDGE == group
        to_right = jnp.where(here, turn(tile, EDGE * (group + 1)), to_right)
        to_left = jnp.where(here, turn(tile, EDGE * group), to_left)
    edge = jnp.where(comp == 0, to_left, to_right)
    requests = request_ref[0].astype(jnp.float32)
    for z in range(4):
        k = letter_of(z ^ space, space)
        letters_ref[k, :8, :] = ocean[z]
        letters_ref[k, 8:16, :] = table[z]
        last = jnp.where(row == 0, packed(halo(ocean, z)), 0.0)
        last = jnp.where(row == 1, packed(halo(table, z)), last)
        last = jnp.where(row == 2, mask[z], last)
        letters_ref[k, PACKED:TABLE, :] = jnp.where(row == 3, halo(mask, z), last)
        letters_ref[k, AT_EDGE:AT_ASKED, :] = edge
        letters_ref[k, AT_ASKED : AT_ASKED + 8, :] = requests[:, :LANES]
        letters_ref[k, AT_ASKED + 8 :, :] = requests[:, LANES:]
    mixed_ref[...] = mixing_ref[...]
    coupled_ref[...] = coupling_ref[...]
    for level in range(LEVELS // 2):
        strip_ref[AT_LEVELS + 2 * ROWS * level : AT_LEVELS + 2 * ROWS * (level + 1), :] = atmos_ref[level]
    strip_ref[:TABLE, :] = letters_ref[0, :TABLE, :]
    strip_ref[AT_REQUEST : AT_REQUEST + 8, :] = requests[:, :LANES]
    strip_ref[AT_REQUEST + 8 :, :] = requests[:, LANES:]


def factors_kernel(mixing_ref, coupling_ref, factors_ref):
    space, comp, lev = place()
    for other in range(LEVELS):
        factors_ref[LEVELS * other : LEVELS * (other + 1), :] = jnp.broadcast_to(
            TENDENCY * mixing_ref[:, other : other + 1], (ROWS, LANES)
        )
    for field in range(FIELDS):
        other = [coupling_ref[:, FIELDS * i + field : FIELDS * i + field + 1] for i in range(2)]
        at = LEVELS * (LEVELS + field)
        factors_ref[at : at + LEVELS, :] = jnp.broadcast_to(jnp.where(lev == 0, other[1], other[0]), (ROWS, LANES))


def sheet_kernel(strip_ref, last_ref, second_ref, first_ref, sheet_ref):
    space, comp, lev = place()
    end = at_end(space)
    sheet_ref[pl.ds(jnp.where(end, 1, 0) * TABLE, TABLE), :] = first_ref[:TABLE, :]
    sheet_ref[pl.ds(jnp.where(end, 0, 1) * TABLE, TABLE), :] = last_ref[:TABLE, :]
    sheet_ref[2 * TABLE : 3 * TABLE, :] = second_ref[:TABLE, :]
    near = (space + comp) % 2 == 0
    one = jnp.where(end, last_ref[AT_EDGE:, :], first_ref[AT_EDGE:, :])
    sheet_ref[AT_HALO:AT_MORE_LEVELS, :] = jnp.where(near, one, second_ref[AT_EDGE:, :])
    sheet_ref[AT_MORE_LEVELS:, :] = strip_ref[AT_LEVELS:AT_REQUEST, :]


def gather_rows(rows_ref, own, beside):
    space, comp, lev = place()
    for k in range(4):
        for (start_ref, came_ref), c in ((own, comp), (beside, 1 - comp)):
            block = came_ref[TABLE * (k - 1) : TABLE * k, :] if k else start_ref[:TABLE, :]
            rows_ref[pl.ds((2 * (space ^ k) + c) * TABLE, TABLE), :] = block


def margins_kernel(strip_ref, strip_beside_ref, own_ref, beside_ref, wet_ref, named_ref, rows_ref):
    space, comp, lev = place()
    lane, row = lane_of(), row_of()
    gather_rows(rows_ref, (strip_ref, own_ref), (strip_beside_ref, beside_ref))

    def table_row(which):
        return rows_ref[pl.ds(which, ROWS, stride=TABLE), :]

    near = (lane < EDGE // 2) | (lane >= LANES - EDGE // 2)
    wet_ref[:, :LANES] = table_row(PACKED + 2)
    wet_ref[:, LANES:] = jnp.where(near, table_row(PACKED + 3), 0.0)

    def halves(ref, at):
        return [ref[at + 8 * i : at + 8 * (i + 1), :] for i in range(2)]

    def by_comp(mine, theirs):
        return [jnp.where(comp == 0, a, b) for a, b in zip(mine, theirs)]

    strips = halves(strip_ref, AT_REQUEST), halves(strip_beside_ref, AT_REQUEST)
    halos = halves(own_ref, AT_HALO_ASKED), halves(beside_ref, AT_HALO_ASKED)
    tables = (
        (by_comp(*strips), by_comp(*strips[::-1])),
        (by_comp(*halos), by_comp(*halos[::-1])),
    )
    first = ((2 * row - 1) * LANES + 2 * (lane & (HALF - 1))).astype(jnp.float32)
    parity = (lane & 1).astype(jnp.float32)
    pairs = lane >> 1
    spread = ((0, pairs), (0, pairs + HALF), (1, jnp.where(lane < HALF, pairs, pairs + HALF)))
    table_halo = table_row(PACKED + 1)
    named = [[jnp.zeros((ROWS, LANES), jnp.float32) for _ in range(3)] for _ in range(4)]
    for margin in range(MARGINS):
        slots = (table_row(8 + margin), turn(table_halo, -EDGE * margin))
        weights = (table_row(8 + MARGINS + margin), turn(table_halo, -EDGE * (MARGINS + margin)))
        cells = []
        for slot, (low_strip, high_strip) in zip(slots, tables):
            rank = slot.astype(jnp.int32) & (2 * LANES - 1)
            late = rank >= LANES
            rank = rank & (LANES - 1)
            found = [jnp.where(late, pick_lanes(high, rank), pick_lanes(low, rank)) for low, high in (low_strip, high_strip)]
            cells.append(jnp.where(lane < HALF, found[0], found[1]) - first)
        for tile, (ring, lanes) in enumerate(spread):
            beyond = pick_lanes(cells[ring], lanes) - parity
            share = pick_lanes(weights[ring], lanes)
            for step in range(4):
                named[step][tile] = named[step][tile] + jnp.where(beyond == float(step * LANES), share, 0.0)
    for step in range(4):
        for tile in range(3):
            named_ref[step, tile] = named[step][tile]


def column_kernel(
    factors_ref,
    strip_ref,
    strip_beside_ref,
    own_ref,
    beside_ref,
    other_ref,
    halo_beside_ref,
    wet_ref,
    named_ref,
    atmos_ref,
    final_ref,
    first_ref,
    second_ref,
    third_ref,
    state_ref,
    flux_ref,
    rows_ref,
    back_ref,
):
    space, comp, lev = place()
    lane, row = lane_of(), row_of()
    half = LEVELS // 2

    mine = pl.ds(pl.multiple_of(comp * LANES, LANES), LANES)
    theirs = pl.ds(pl.multiple_of((1 - comp) * LANES, LANES), LANES)
    for level in range(half):
        here, there = lev * half + level, (1 - lev) * half + level
        at = 2 * ROWS * level
        rows = slice(AT_LEVELS + at, AT_LEVELS + at + 2 * ROWS)
        state_ref[here, :, mine] = strip_ref[rows, :]
        state_ref[there, :, mine] = other_ref[rows, :]
        state_ref[there, :, theirs] = strip_beside_ref[rows, :]
        state_ref[here, :, theirs] = beside_ref[AT_MORE_LEVELS + at : AT_MORE_LEVELS + at + 2 * ROWS, :]
    exists = jnp.where(lane < HALF, space + 1, 4 - space) < 4
    halos = (
        (lev, other_ref[OTHER_HALO:, :], halo_beside_ref[...]),
        (1 - lev, own_ref[AT_HALO:AT_HALO_ASKED, :], beside_ref[AT_HALO:AT_HALO_ASKED, :]),
    )
    for block, own, beside in halos:
        east, west = jnp.where(comp == 0, own, beside), jnp.where(comp == 0, beside, own)
        for group in range(LANES // EDGE):
            tile = jnp.where(
                lane < EDGE,
                turn(east, -EDGE * group),
                jnp.where(lane >= LANES - EDGE, turn(west, -EDGE * (group + 1)), 0.0),
            )
            state_ref[block * half + group // 2, ROWS * (group % 2) : ROWS * (group % 2 + 1), 2 * LANES :] = jnp.where(
                exists, tile, 0.0
            )
    edge_inside = jnp.where(jnp.concatenate([exists] * 2, 0), 1.0, 0.0)
    inside = jnp.concatenate([jnp.ones((2 * ROWS, 2 * LANES), jnp.float32), edge_inside], 1)

    def factor(which):
        return jnp.broadcast_to(jnp.concatenate([factors_ref[which : which + 1, :]] * 3, 1), (2 * ROWS, 3 * LANES))

    atmos = [state_ref[level] for level in range(LEVELS)]
    for substep in range(ASUB):
        shaded = [jnp.tanh(cells) for cells in atmos]
        later = []
        for level in range(LEVELS):
            cells = atmos[level]
            beside = turn(cells, 1) + turn(cells, -1) + rows_down(cells) + rows_up(cells)
            column = sum(factor(LEVELS * other + level) * shaded[other] for other in range(LEVELS))
            cells = DIFFUSE * (cells + beside) + column
            later.append(inside * cells)
        atmos = later
    for level in range(LEVELS):
        state_ref[level] = atmos[level]
    for level in range(half):
        atmos_ref[level] = state_ref[lev * half + level, :, mine]

    for field in range(FIELDS):
        flux = sum(factor(LEVELS * (LEVELS + field) + level) * atmos[level] for level in range(LEVELS))
        for tile in range(3):
            flux_ref[tile, WIDE * field : WIDE * field + 8, :] = jnp.zeros((ROWS, LANES), jnp.float32)
            flux_ref[tile, WIDE * field + 8 : WIDE * field + 24, :] = flux[:, LANES * tile : LANES * (tile + 1)]
            flux_ref[tile, WIDE * field + 24 : WIDE * field + 32, :] = jnp.zeros((ROWS, LANES), jnp.float32)

    gather_rows(rows_ref, (other_ref, own_ref), (strip_beside_ref, beside_ref))
    ocean_halo = rows_ref[pl.ds(PACKED, ROWS, stride=TABLE), :]

    wetness = wet_ref[...]
    pairs = (2 * lane) & (LANES - 1)
    ocean = []
    forcing = []
    for field in range(FIELDS):
        sums = []
        for tile in range(3):
            total = sum(
                named_ref[step, tile] * flux_ref[tile, pl.ds(WIDE * field + 7 + step, ROWS, stride=2), :] for step in range(4)
            )
            sums.append(pick_lanes(total + turn(total, -1), pairs))
        remapped = jnp.concatenate([jnp.where(lane < HALF, sums[0], sums[1]), sums[2]], 1)
        forcing.append(wetness * (FORCING * remapped))
        main = rows_ref[pl.ds(field, ROWS, stride=TABLE), :]
        ocean.append(jnp.concatenate([main, turn(ocean_halo, -EDGE * field)], 1))
    spreading = OCEAN_MIX * wetness
    for substep in range(SUB):
        for field in range(FIELDS):
            cells = ocean[field]
            beside = turn(cells, 1) + turn(cells, -1) + rows_down(cells) + rows_up(cells)
            ocean[field] = spreading * (cells + beside) + forcing[field]
    for field in range(FIELDS):
        cells = ocean[field][:, :LANES]
        final_ref[ROWS * field : ROWS * (field + 1), :] = cells
        back_ref[pl.ds(field, ROWS, stride=FIELDS), :] = cells
    for k, ref in zip((1, 2, 3), (first_ref, second_ref, third_ref)):
        ref[...] = back_ref[pl.ds((2 * (space ^ k) + comp) * FIELDS, FIELDS), :]


def returned_kernel(atmos_ref, final_ref, named_ref, atmos_next_ref, returned_ref):
    space, comp, lev = place()
    lane = lane_of()
    atmos_next_ref[...] = atmos_ref[...]
    named = [jnp.where(comp == 0, named_ref[step, 0], named_ref[step, 1]) for step in range(4)]
    pairs = (lane >> 1) + HALF * comp
    for field in range(FIELDS):
        spread = pick_lanes(final_ref[ROWS * field : ROWS * (field + 1), :], pairs)
        upper = named[1] * spread + rows_down(named[3] * spread)
        lower = named[2] * spread + rows_up(named[0] * spread)
        returned_ref[pl.ds(2 * ROWS * field, ROWS, stride=2), :] = upper
        returned_ref[pl.ds(2 * ROWS * field + 1, ROWS, stride=2), :] = lower


def rows_kernel(three_ref, two_ref, one_ref, final_ref, ocean_ref):
    space, comp, lev = place()
    own = final_ref[pl.ds(2 * space + comp, FIELDS, stride=ROWS), :]
    for k, cells in enumerate((own, one_ref[...], two_ref[...], three_ref[...])):
        ocean_ref[:, 0, pl.ds(pl.multiple_of((space ^ k) * LANES, LANES), LANES)] = cells


def over(axis, k, array):
    return lax.ppermute(array, axis, [(i, i ^ k) for i in range(lax.axis_size(axis))])


def across(axis, targets, array):
    pairs = [(2 * i + core, 2 * target + 1 - core) for i, target in enumerate(targets) for core in range(2)]
    return lax.ppermute(array, (axis, "lev"), pairs)


def local(kernel, out_shape, spaces, scratch=()):
    single = not isinstance(out_shape, tuple)
    vmem = pl.BlockSpec(memory_space=pltpu.VMEM)
    return pl.pallas_call(
        kernel,
        out_shape=out_shape,
        in_specs=[pl.BlockSpec(memory_space=space) for space in spaces],
        out_specs=vmem if single else (vmem,) * len(out_shape),
        scratch_shapes=list(scratch),
        compiler_params=pltpu.CompilerParams(vmem_limit_bytes=VMEM_LIMIT),
    )


def shards_by_columns(
    atmos_state,
    ocean_state,
    vertical_mixing,
    flux_coupling,
    request_cells,
    margin_slot,
    margin_weight,
    sea_mask,
):
    def values(*shape):
        return jax.ShapeDtypeStruct(shape, jnp.float32)

    arrays = (ocean_state, margin_slot, margin_weight, sea_mask, atmos_state, request_cells)
    arrays += (vertical_mixing, flux_coupling.T)
    letters, strip, mixing, coupling = local(
        tables_kernel,
        (values(4, LETTER, LANES), values(STRIP, LANES), values(LEVELS, LEVELS), values(LEVELS, 2 * FIELDS)),
        [pltpu.HBM] * 8,
        [pltpu.VMEM(a.shape, a.dtype) for a in arrays] + [pltpu.SemaphoreType.DMA((8,))],
    )(*(pltpu.with_memory_space_constraint(a, pltpu.HBM) for a in arrays))
    first, second, last = (across("space", turns, letters[at]) for at, turns in ((1, FIRST), (3, SECOND), (2, LAST)))
    strip_beside = across("comp", (1, 0), strip)
    sheet = local(sheet_kernel, values(SHEET, LANES), [pltpu.VMEM] * 4)(strip, last, second, first)
    sheet_beside = over("comp", 1, sheet)
    halo = sheet[AT_HALO:AT_HALO_ASKED]
    halo_beside = lax.ppermute(halo, ("comp", "lev"), [(0, 3), (3, 0), (1, 2), (2, 1)])
    other = over("lev", 1, jnp.concatenate([strip[:AT_REQUEST], halo], 0))
    factors = local(factors_kernel, values(2 * LEVELS * LEVELS, LANES), [pltpu.VMEM] * 2)(mixing, coupling)
    wet, named = local(
        margins_kernel,
        (values(ROWS, 2 * LANES), values(4, 3, ROWS, LANES)),
        [pltpu.VMEM] * 4,
        [pltpu.VMEM((ROWS * TABLE, LANES), jnp.float32)],
    )(strip, strip_beside, sheet, sheet_beside)
    atmos, final, *back = local(
        column_kernel,
        (values(*atmos_state.shape), values(FIELDS * ROWS, LANES)) + (values(FIELDS, LANES),) * 3,
        [pltpu.VMEM] * 9,
        [
            pltpu.VMEM((LEVELS, 2 * ROWS, 3 * LANES), jnp.float32),
            pltpu.VMEM((3, FIELDS * WIDE, LANES), jnp.float32),
            pltpu.VMEM((ROWS * TABLE, LANES), jnp.float32),
            pltpu.VMEM((ROWS * FIELDS, LANES), jnp.float32),
        ],
    )(factors, strip, strip_beside, sheet, sheet_beside, other, halo_beside, wet, named)
    one, two, three = (across("space", [z ^ k for z in range(4)], piece) for k, piece in zip((1, 2, 3), back))
    final = over("lev", 1, final)
    atmos_next, returned = local(
        returned_kernel,
        (values(*atmos_state.shape), values(FIELDS * 2 * ROWS, LANES)),
        [pltpu.VMEM] * 3,
    )(atmos, final, named)
    ocean_next = local(rows_kernel, values(*ocean_state.shape), [pltpu.VMEM] * 4)(three, two, one, final)
    return (atmos_next, ocean_next, returned.reshape(FIELDS, 2 * ROWS, LANES))


def shards(*arguments):
    atmos_state, ocean_state, mixing, coupling, request_cells, margin_slot = arguments[:6]
    by_columns = (
        (lax.axis_size("space"), lax.axis_size("comp"), lax.axis_size("lev")) == (4, 2, 2)
        and atmos_state.shape == (LEVELS // 2, 2 * ROWS, LANES)
        and ocean_state.shape == (FIELDS, 1, 4 * LANES)
        and request_cells.shape == (1, ROWS, 2 * LANES)
        and margin_slot.shape[0] == MARGINS
    )
    return (shards_by_columns if by_columns else shards_by_neighbours)(*arguments)


def solution(mesh):
    placed = (
        P(("parts", "lev"), None, ("space", "comp")),
        P(("parts", "lev"), ("space", "comp"), None),
        P(),
        P(),
        P(("space", "comp"), None, None),
        P(None, ("space", "comp"), None),
        P(None, ("space", "comp"), None),
        P(("space", "comp"), None),
    )
    return jax.shard_map(
        shards,
        mesh=mesh,
        in_specs=placed,
        out_specs=(
            P(("parts", "lev"), None, ("space", "comp")),
            P(("parts", "lev"), ("space", "comp"), None),
            P(("parts", "lev"), None, ("space", "comp")),
        ),
        check_vma=False,
    )
```

```python
import jax
import jax.numpy as jnp
from jax import lax
from jax.experimental import pallas as pl
from jax.experimental.pallas import tpu as pltpu
from jax.sharding import PartitionSpec as P

ASUB = 2
SUB = 8


DIFFUSE = 0.2
TENDENCY = 0.25
OCEAN_MIX = 0.2
FORCING = 0.15


def with_halo(cells, sides, width):
    for axis, dim in sides:
        count = lax.axis_size(axis)
        ends = count - 1
        head = lax.slice_in_dim(cells, 0, width, axis=dim)
        tail = lax.slice_in_dim(cells, cells.shape[dim] - width, cells.shape[dim], axis=dim)
        cells = jnp.concatenate(
            [
                lax.ppermute(tail, axis, [(i, (i + 1) % count) for i in range(ends)]),
                cells,
                lax.ppermute(head, axis, [((i + 1) % count, i) for i in range(ends)]),
            ],
            axis=dim,
        )
    return cells


def atmos_step(atmos, mixing_rows):
    lev_local = atmos.shape[0]
    padded = with_halo(atmos, ((("space", "comp"), 2),), 1)
    padded = jnp.pad(padded, ((0, 0), (1, 1), (0, 0)))
    beside = padded[:, 2:, 1:-1] + padded[:, :-2, 1:-1] + padded[:, 1:-1, 2:] + padded[:, 1:-1, :-2]
    shaded = jnp.tanh(atmos).reshape(lev_local, -1)
    column = jnp.dot(
        mixing_rows,
        lax.all_gather(shaded, "lev", axis=0, tiled=True),
        precision=lax.Precision.HIGHEST,
    )
    return atmos + DIFFUSE * (beside - 4.0 * atmos) + TENDENCY * column.reshape(atmos.shape)


def advance(padded, wetness, forcing):
    centre = padded[:, 1:-1, 1:-1]
    beside = padded[:, 2:, 1:-1] + padded[:, :-2, 1:-1] + padded[:, 1:-1, 2:] + padded[:, 1:-1, :-2]
    return wetness[None] * (centre + OCEAN_MIX * (beside - 4.0 * centre) + FORCING * forcing)


def shards_by_neighbours(
    atmos_state,
    ocean_state,
    vertical_mixing,
    flux_coupling,
    request_cells,
    margin_slot,
    margin_weight,
    sea_mask,
):
    lev_local, rows_atmos, cols_atmos = atmos_state.shape
    fields_local = ocean_state.shape[0]
    margins = margin_slot.shape[0]
    lev_place = lax.axis_index("lev")
    mixing_rows = lax.dynamic_slice_in_dim(vertical_mixing, lev_place * lev_local, lev_local, 0)
    coupling_cols = lax.dynamic_slice_in_dim(flux_coupling, lev_place * lev_local, lev_local, 1)
    atmos = atmos_state
    for substep in range(ASUB):
        atmos = atmos_step(atmos, mixing_rows)
    flat_atmos = atmos.reshape(lev_local, -1)
    fluxes = lax.psum_scatter(
        jnp.dot(coupling_cols, flat_atmos, precision=lax.Precision.HIGHEST),
        "lev",
        scatter_dimension=0,
        tiled=True,
    )
    requests = request_cells.reshape(-1)
    outgoing = jnp.take(fluxes, requests, axis=1)
    slot_flat = margin_slot.reshape(-1)
    weight_flat = margin_weight.reshape(margins, -1)
    received = lax.all_to_all(outgoing, ("space", "comp"), split_axis=1, concat_axis=1, tiled=True)
    picked = jnp.take(received, slot_flat, axis=1).reshape(received.shape[0], margins, -1)
    remapped = jnp.sum(picked * weight_flat[None], axis=1)
    forcing = remapped.reshape(ocean_state.shape)
    wetness = sea_mask.astype(jnp.float32)
    ocean_now = ocean_state
    for substep in range(SUB):
        padded = with_halo(ocean_now, ((("space", "comp"), 1),), 1)
        padded = jnp.pad(padded, ((0, 0), (0, 0), (1, 1)))
        ocean_now = advance(padded, wetness, forcing)
    weighted = (weight_flat[None] * ocean_now).reshape(fields_local, -1)
    outgoing_back = (
        jnp.zeros((fields_local, requests.shape[0]), jnp.float32).at[:, slot_flat].add(weighted)
    )
    arrived = lax.all_to_all(
        outgoing_back, ("space", "comp"), split_axis=1, concat_axis=1, tiled=True
    )
    returned = (
        jnp.zeros((fields_local, rows_atmos * cols_atmos), jnp.float32).at[:, requests].add(arrived)
    )
    return (atmos, ocean_now, returned.reshape(fields_local, rows_atmos, cols_atmos))


LANES = 128
HALF = 64
ROWS = 8
LEVELS = 8
FIELDS = 8
MARGINS = 4
TABLE = 24
PACKED = 16
TABLES = 4 * TABLE
AT_EDGE = TABLE
AT_ASKED = AT_EDGE + 8
LETTER = AT_ASKED + 16
AT_LEVELS = TABLE
AT_REQUEST = AT_LEVELS + 64
STRIP = AT_REQUEST + 16
AT_HALO = 3 * TABLE
AT_HALO_ASKED = AT_HALO + 8
AT_MORE_LEVELS = AT_HALO_ASKED + 16
SHEET = AT_MORE_LEVELS + 64
OTHER_HALO = AT_REQUEST
EDGE = 16
WIDE = 32
VMEM_LIMIT = 4 * 1024 * 1024


def lane_of(shape=(ROWS, LANES)):
    return lax.broadcasted_iota(jnp.int32, shape, 1)


def row_of(shape=(ROWS, LANES)):
    return lax.broadcasted_iota(jnp.int32, shape, 0)


def pick_lanes(tile, lanes):
    return jnp.take_along_axis(tile, lanes, axis=1, mode="promise_in_bounds")


def turn(tile, by):
    by = by % tile.shape[1]
    return pltpu.roll(tile, by, 1) if by else tile


def rows_down(tile):
    return jnp.where(row_of(tile.shape) == 0, 0.0, pltpu.roll(tile, 1, 0))


def rows_up(tile):
    last = tile.shape[0] - 1
    return jnp.where(row_of(tile.shape) == last, 0.0, pltpu.roll(tile, last, 0))


def place():
    return lax.axis_index("space"), lax.axis_index("comp"), lax.axis_index("lev")


FIRST = (1, 3, 0, 2)
SECOND = (3, 2, 1, 0)
LAST = (2, 0, 3, 1)


def at_end(space):
    return (space == 0) | (space == 3)


def letter_of(k, space):
    return jnp.where((k == 1) | (k == 2), jnp.where(at_end(space), k, 3 - k), k)


def tables_kernel(*refs):
    arrays, (letters_ref, strip_ref, mixed_ref, coupled_ref), held, arrived = refs[:8], refs[8:12], refs[12:-1], refs[-1]
    copies = [pltpu.make_async_copy(a, h, arrived.at[i]) for i, (a, h) in enumerate(zip(arrays, held))]
    for copy in copies:
        copy.start()
    for copy in copies:
        copy.wait()
    ocean_ref, slot_ref, weight_ref, mask_ref, atmos_ref, request_ref, mixing_ref, coupling_ref = held
    space, comp, lev = place()
    lane, row = lane_of(), row_of()
    near = (lane < EDGE // 2) | (lane >= LANES - EDGE // 2)

    def halo(tiles, z):
        beyond = jnp.zeros_like(tiles[0])
        east = tiles[z + 1] if z + 1 < len(tiles) else beyond
        west = tiles[z - 1] if z > 0 else beyond
        wide = lane[: beyond.shape[0]]
        return jnp.where(near[: beyond.shape[0]], jnp.where(wide < HALF, east, west), 0.0)

    def packed(cells):
        return jnp.sum(pltpu.roll(cells, 0, 1, stride=EDGE, stride_axis=0), axis=0, keepdims=True)

    def tiles_of(cells):
        return [cells[:, LANES * z : LANES * (z + 1)] for z in range(4)]

    ocean = tiles_of(ocean_ref[:, 0, :])
    table = tiles_of(jnp.concatenate([slot_ref[:, 0, :].astype(jnp.float32), weight_ref[:, 0, :]], 0))
    mask = tiles_of(mask_ref[...].astype(jnp.float32))
    to_right = jnp.zeros((ROWS, LANES), jnp.float32)
    to_left = jnp.zeros((ROWS, LANES), jnp.float32)
    for group in range(LANES // EDGE):
        tile = atmos_ref[group // 2, ROWS * (group % 2) : ROWS * (group % 2 + 1), :]
        here = lane // EDGE == group
        to_right = jnp.where(here, turn(tile, EDGE * (group + 1)), to_right)
        to_left = jnp.where(here, turn(tile, EDGE * group), to_left)
    edge = jnp.where(comp == 0, to_left, to_right)
    requests = request_ref[0].astype(jnp.float32)
    for z in range(4):
        k = letter_of(z ^ space, space)
        letters_ref[k, :8, :] = ocean[z]
        letters_ref[k, 8:16, :] = table[z]
        last = jnp.where(row == 0, packed(halo(ocean, z)), 0.0)
        last = jnp.where(row == 1, packed(halo(table, z)), last)
        last = jnp.where(row == 2, mask[z], last)
        letters_ref[k, PACKED:TABLE, :] = jnp.where(row == 3, halo(mask, z), last)
        letters_ref[k, AT_EDGE:AT_ASKED, :] = edge
        letters_ref[k, AT_ASKED : AT_ASKED + 8, :] = requests[:, :LANES]
        letters_ref[k, AT_ASKED + 8 :, :] = requests[:, LANES:]
    mixed_ref[...] = mixing_ref[...]
    coupled_ref[...] = coupling_ref[...]
    for level in range(LEVELS // 2):
        strip_ref[AT_LEVELS + 2 * ROWS * level : AT_LEVELS + 2 * ROWS * (level + 1), :] = atmos_ref[level]
    strip_ref[:TABLE, :] = letters_ref[0, :TABLE, :]
    strip_ref[AT_REQUEST : AT_REQUEST + 8, :] = requests[:, :LANES]
    strip_ref[AT_REQUEST + 8 :, :] = requests[:, LANES:]


def factors_kernel(mixing_ref, coupling_ref, factors_ref):
    space, comp, lev = place()
    for other in range(LEVELS):
        factors_ref[LEVELS * other : LEVELS * (other + 1), :] = jnp.broadcast_to(
            TENDENCY * mixing_ref[:, other : other + 1], (ROWS, LANES)
        )
    for field in range(FIELDS):
        other = [coupling_ref[:, FIELDS * i + field : FIELDS * i + field + 1] for i in range(2)]
        at = LEVELS * (LEVELS + field)
        factors_ref[at : at + LEVELS, :] = jnp.broadcast_to(jnp.where(lev == 0, other[1], other[0]), (ROWS, LANES))


def sheet_kernel(strip_ref, last_ref, second_ref, first_ref, sheet_ref):
    space, comp, lev = place()
    end = at_end(space)
    sheet_ref[pl.ds(jnp.where(end, 1, 0) * TABLE, TABLE), :] = first_ref[:TABLE, :]
    sheet_ref[pl.ds(jnp.where(end, 0, 1) * TABLE, TABLE), :] = last_ref[:TABLE, :]
    sheet_ref[2 * TABLE : 3 * TABLE, :] = second_ref[:TABLE, :]
    near = (space + comp) % 2 == 0
    one = jnp.where(end, last_ref[AT_EDGE:, :], first_ref[AT_EDGE:, :])
    sheet_ref[AT_HALO:AT_MORE_LEVELS, :] = jnp.where(near, one, second_ref[AT_EDGE:, :])
    sheet_ref[AT_MORE_LEVELS:, :] = strip_ref[AT_LEVELS:AT_REQUEST, :]


def gather_rows(rows_ref, own, beside):
    space, comp, lev = place()
    for k in range(4):
        for (start_ref, came_ref), c in ((own, comp), (beside, 1 - comp)):
            block = came_ref[TABLE * (k - 1) : TABLE * k, :] if k else start_ref[:TABLE, :]
            rows_ref[pl.ds((2 * (space ^ k) + c) * TABLE, TABLE), :] = block


def margins_kernel(strip_ref, strip_beside_ref, own_ref, beside_ref, wet_ref, named_ref, rows_ref):
    space, comp, lev = place()
    lane, row = lane_of(), row_of()
    gather_rows(rows_ref, (strip_ref, own_ref), (strip_beside_ref, beside_ref))

    def table_row(which):
        return rows_ref[pl.ds(which, ROWS, stride=TABLE), :]

    near = (lane < EDGE // 2) | (lane >= LANES - EDGE // 2)
    wet_ref[:, :LANES] = table_row(PACKED + 2)
    wet_ref[:, LANES:] = jnp.where(near, table_row(PACKED + 3), 0.0)

    def halves(ref, at):
        return [ref[at + 8 * i : at + 8 * (i + 1), :] for i in range(2)]

    def by_comp(mine, theirs):
        return [jnp.where(comp == 0, a, b) for a, b in zip(mine, theirs)]

    strips = halves(strip_ref, AT_REQUEST), halves(strip_beside_ref, AT_REQUEST)
    halos = halves(own_ref, AT_HALO_ASKED), halves(beside_ref, AT_HALO_ASKED)
    tables = (
        (by_comp(*strips), by_comp(*strips[::-1])),
        (by_comp(*halos), by_comp(*halos[::-1])),
    )
    first = ((2 * row - 1) * LANES + 2 * (lane & (HALF - 1))).astype(jnp.float32)
    parity = (lane & 1).astype(jnp.float32)
    pairs = lane >> 1
    spread = ((0, pairs), (0, pairs + HALF), (1, jnp.where(lane < HALF, pairs, pairs + HALF)))
    table_halo = table_row(PACKED + 1)
    named = [[jnp.zeros((ROWS, LANES), jnp.float32) for _ in range(3)] for _ in range(4)]
    for margin in range(MARGINS):
        slots = (table_row(8 + margin), turn(table_halo, -EDGE * margin))
        weights = (table_row(8 + MARGINS + margin), turn(table_halo, -EDGE * (MARGINS + margin)))
        cells = []
        for slot, (low_strip, high_strip) in zip(slots, tables):
            rank = slot.astype(jnp.int32) & (2 * LANES - 1)
            late = rank >= LANES
            rank = rank & (LANES - 1)
            found = [jnp.where(late, pick_lanes(high, rank), pick_lanes(low, rank)) for low, high in (low_strip, high_strip)]
            cells.append(jnp.where(lane < HALF, found[0], found[1]) - first)
        for tile, (ring, lanes) in enumerate(spread):
            beyond = pick_lanes(cells[ring], lanes) - parity
            share = pick_lanes(weights[ring], lanes)
            for step in range(4):
                named[step][tile] = named[step][tile] + jnp.where(beyond == float(step * LANES), share, 0.0)
    for step in range(4):
        for tile in range(3):
            named_ref[step, tile] = named[step][tile]


def mixing_kernel(factors_ref, strip_ref, other_ref, mixed_ref, shaded_ref):
    space, comp, lev = place()
    half = LEVELS // 2
    for level in range(half):
        at = AT_LEVELS + 2 * ROWS * level
        shaded_ref[lev * half + level] = jnp.tanh(strip_ref[at : at + 2 * ROWS, :])
        shaded_ref[(1 - lev) * half + level] = jnp.tanh(other_ref[at : at + 2 * ROWS, :])
    for level in range(LEVELS):
        mixed_ref[level] = sum(
            jnp.broadcast_to(factors_ref[LEVELS * other + level : LEVELS * other + level + 1, :], (2 * ROWS, LANES))
            * shaded_ref[other]
            for other in range(LEVELS)
        )


def column_kernel(
    factors_ref,
    mixed_own_ref,
    strip_ref,
    strip_beside_ref,
    own_ref,
    beside_ref,
    other_ref,
    halo_beside_ref,
    wet_ref,
    named_ref,
    atmos_ref,
    final_ref,
    first_ref,
    second_ref,
    third_ref,
    state_ref,
    flux_ref,
    rows_ref,
    back_ref,
    mixed_ref,
):
    space, comp, lev = place()
    lane, row = lane_of(), row_of()
    half = LEVELS // 2

    mine = pl.ds(pl.multiple_of(comp * LANES, LANES), LANES)
    theirs = pl.ds(pl.multiple_of((1 - comp) * LANES, LANES), LANES)
    for level in range(half):
        here, there = lev * half + level, (1 - lev) * half + level
        at = 2 * ROWS * level
        rows = slice(AT_LEVELS + at, AT_LEVELS + at + 2 * ROWS)
        state_ref[here, :, mine] = strip_ref[rows, :]
        state_ref[there, :, mine] = other_ref[rows, :]
        state_ref[there, :, theirs] = strip_beside_ref[rows, :]
        state_ref[here, :, theirs] = beside_ref[AT_MORE_LEVELS + at : AT_MORE_LEVELS + at + 2 * ROWS, :]
    exists = jnp.where(lane < HALF, space + 1, 4 - space) < 4
    halos = (
        (lev, other_ref[OTHER_HALO:, :], halo_beside_ref[...]),
        (1 - lev, own_ref[AT_HALO:AT_HALO_ASKED, :], beside_ref[AT_HALO:AT_HALO_ASKED, :]),
    )
    for block, own, beside in halos:
        east, west = jnp.where(comp == 0, own, beside), jnp.where(comp == 0, beside, own)
        for group in range(LANES // EDGE):
            tile = jnp.where(
                lane < EDGE,
                turn(east, -EDGE * group),
                jnp.where(lane >= LANES - EDGE, turn(west, -EDGE * (group + 1)), 0.0),
            )
            state_ref[block * half + group // 2, ROWS * (group % 2) : ROWS * (group % 2 + 1), 2 * LANES :] = jnp.where(
                exists, tile, 0.0
            )
    edge_inside = jnp.where(jnp.concatenate([exists] * 2, 0), 1.0, 0.0)
    inside = jnp.concatenate([jnp.ones((2 * ROWS, 2 * LANES), jnp.float32), edge_inside], 1)

    def factor(which, tiles=3):
        return jnp.broadcast_to(jnp.concatenate([factors_ref[which : which + 1, :]] * tiles, 1), (2 * ROWS, tiles * LANES))

    rest = [jnp.tanh(jnp.concatenate([state_ref[i, :, theirs], state_ref[i, :, 2 * LANES :]], 1)) for i in range(LEVELS)]
    for level in range(LEVELS):
        column = sum(factor(LEVELS * other + level, 2) * rest[other] for other in range(LEVELS))
        mixed_ref[level, :, mine] = mixed_own_ref[level]
        mixed_ref[level, :, theirs] = column[:, :LANES]
        mixed_ref[level, :, 2 * LANES :] = column[:, LANES:]
    atmos = [state_ref[level] for level in range(LEVELS)]
    for substep in range(ASUB):
        shaded = [jnp.tanh(cells) for cells in atmos] if substep else None
        later = []
        for level in range(LEVELS):
            cells = atmos[level]
            beside = turn(cells, 1) + turn(cells, -1) + rows_down(cells) + rows_up(cells)
            if substep:
                column = sum(factor(LEVELS * other + level) * shaded[other] for other in range(LEVELS))
            else:
                column = mixed_ref[level]
            cells = DIFFUSE * (cells + beside) + column
            later.append(inside * cells)
        atmos = later
    for level in range(LEVELS):
        state_ref[level] = atmos[level]
    for level in range(half):
        atmos_ref[level] = state_ref[lev * half + level, :, mine]

    for field in range(FIELDS):
        flux = sum(factor(LEVELS * (LEVELS + field) + level) * atmos[level] for level in range(LEVELS))
        for tile in range(3):
            flux_ref[tile, WIDE * field : WIDE * field + 8, :] = jnp.zeros((ROWS, LANES), jnp.float32)
            flux_ref[tile, WIDE * field + 8 : WIDE * field + 24, :] = flux[:, LANES * tile : LANES * (tile + 1)]
            flux_ref[tile, WIDE * field + 24 : WIDE * field + 32, :] = jnp.zeros((ROWS, LANES), jnp.float32)

    gather_rows(rows_ref, (other_ref, own_ref), (strip_beside_ref, beside_ref))
    ocean_halo = rows_ref[pl.ds(PACKED, ROWS, stride=TABLE), :]

    wetness = wet_ref[...]
    pairs = (2 * lane) & (LANES - 1)
    ocean = []
    forcing = []
    for field in range(FIELDS):
        sums = []
        for tile in range(3):
            total = sum(
                named_ref[step, tile] * flux_ref[tile, pl.ds(WIDE * field + 7 + step, ROWS, stride=2), :] for step in range(4)
            )
            sums.append(pick_lanes(total + turn(total, -1), pairs))
        remapped = jnp.concatenate([jnp.where(lane < HALF, sums[0], sums[1]), sums[2]], 1)
        forcing.append(wetness * (FORCING * remapped))
        main = rows_ref[pl.ds(field, ROWS, stride=TABLE), :]
        ocean.append(jnp.concatenate([main, turn(ocean_halo, -EDGE * field)], 1))
    spreading = OCEAN_MIX * wetness
    for substep in range(SUB):
        for field in range(FIELDS):
            cells = ocean[field]
            beside = turn(cells, 1) + turn(cells, -1) + rows_down(cells) + rows_up(cells)
            ocean[field] = spreading * (cells + beside) + forcing[field]
    for field in range(FIELDS):
        cells = ocean[field][:, :LANES]
        final_ref[ROWS * field : ROWS * (field + 1), :] = cells
        back_ref[pl.ds(field, ROWS, stride=FIELDS), :] = cells
    for k, ref in zip((1, 2, 3), (first_ref, second_ref, third_ref)):
        ref[...] = back_ref[pl.ds((2 * (space ^ k) + comp) * FIELDS, FIELDS), :]


def returned_kernel(atmos_ref, final_ref, named_ref, atmos_next_ref, returned_ref):
    space, comp, lev = place()
    lane = lane_of()
    atmos_next_ref[...] = atmos_ref[...]
    named = [jnp.where(comp == 0, named_ref[step, 0], named_ref[step, 1]) for step in range(4)]
    pairs = (lane >> 1) + HALF * comp
    for field in range(FIELDS):
        spread = pick_lanes(final_ref[ROWS * field : ROWS * (field + 1), :], pairs)
        upper = named[1] * spread + rows_down(named[3] * spread)
        lower = named[2] * spread + rows_up(named[0] * spread)
        returned_ref[pl.ds(2 * ROWS * field, ROWS, stride=2), :] = upper
        returned_ref[pl.ds(2 * ROWS * field + 1, ROWS, stride=2), :] = lower


def rows_kernel(three_ref, two_ref, one_ref, final_ref, ocean_ref):
    space, comp, lev = place()
    own = final_ref[pl.ds(2 * space + comp, FIELDS, stride=ROWS), :]
    for k, cells in enumerate((own, one_ref[...], two_ref[...], three_ref[...])):
        ocean_ref[:, 0, pl.ds(pl.multiple_of((space ^ k) * LANES, LANES), LANES)] = cells


def over(axis, k, array):
    return lax.ppermute(array, axis, [(i, i ^ k) for i in range(lax.axis_size(axis))])


def across(axis, targets, array):
    pairs = [(2 * i + core, 2 * target + 1 - core) for i, target in enumerate(targets) for core in range(2)]
    return lax.ppermute(array, (axis, "lev"), pairs)


def local(kernel, out_shape, spaces, scratch=()):
    single = not isinstance(out_shape, tuple)
    vmem = pl.BlockSpec(memory_space=pltpu.VMEM)
    return pl.pallas_call(
        kernel,
        out_shape=out_shape,
        in_specs=[pl.BlockSpec(memory_space=space) for space in spaces],
        out_specs=vmem if single else (vmem,) * len(out_shape),
        scratch_shapes=list(scratch),
        compiler_params=pltpu.CompilerParams(vmem_limit_bytes=VMEM_LIMIT),
    )


def shards_by_columns(
    atmos_state,
    ocean_state,
    vertical_mixing,
    flux_coupling,
    request_cells,
    margin_slot,
    margin_weight,
    sea_mask,
):
    def values(*shape):
        return jax.ShapeDtypeStruct(shape, jnp.float32)

    arrays = (ocean_state, margin_slot, margin_weight, sea_mask, atmos_state, request_cells)
    arrays += (vertical_mixing, flux_coupling.T)
    letters, strip, mixing, coupling = local(
        tables_kernel,
        (values(4, LETTER, LANES), values(STRIP, LANES), values(LEVELS, LEVELS), values(LEVELS, 2 * FIELDS)),
        [pltpu.HBM] * 8,
        [pltpu.VMEM(a.shape, a.dtype) for a in arrays] + [pltpu.SemaphoreType.DMA((8,))],
    )(*(pltpu.with_memory_space_constraint(a, pltpu.HBM) for a in arrays))
    first, second, last = (across("space", turns, letters[at]) for at, turns in ((1, FIRST), (3, SECOND), (2, LAST)))
    strip_beside = across("comp", (1, 0), strip)
    sheet = local(sheet_kernel, values(SHEET, LANES), [pltpu.VMEM] * 4)(strip, last, second, first)
    sheet_beside = over("comp", 1, sheet)
    halo = sheet[AT_HALO:AT_HALO_ASKED]
    halo_beside = lax.ppermute(halo, ("comp", "lev"), [(0, 3), (3, 0), (1, 2), (2, 1)])
    other = over("lev", 1, jnp.concatenate([strip[:AT_REQUEST], halo], 0))
    factors = local(factors_kernel, values(2 * LEVELS * LEVELS, LANES), [pltpu.VMEM] * 2)(mixing, coupling)
    mixed = local(
        mixing_kernel,
        values(LEVELS, 2 * ROWS, LANES),
        [pltpu.VMEM] * 3,
        [pltpu.VMEM((LEVELS, 2 * ROWS, LANES), jnp.float32)],
    )(factors, strip, other)
    wet, named = local(
        margins_kernel,
        (values(ROWS, 2 * LANES), values(4, 3, ROWS, LANES)),
        [pltpu.VMEM] * 4,
        [pltpu.VMEM((ROWS * TABLE, LANES), jnp.float32)],
    )(strip, strip_beside, sheet, sheet_beside)
    atmos, final, *back = local(
        column_kernel,
        (values(*atmos_state.shape), values(FIELDS * ROWS, LANES)) + (values(FIELDS, LANES),) * 3,
        [pltpu.VMEM] * 10,
        [
            pltpu.VMEM((LEVELS, 2 * ROWS, 3 * LANES), jnp.float32),
            pltpu.VMEM((3, FIELDS * WIDE, LANES), jnp.float32),
            pltpu.VMEM((ROWS * TABLE, LANES), jnp.float32),
            pltpu.VMEM((ROWS * FIELDS, LANES), jnp.float32),
            pltpu.VMEM((LEVELS, 2 * ROWS, 3 * LANES), jnp.float32),
        ],
    )(factors, mixed, strip, strip_beside, sheet, sheet_beside, other, halo_beside, wet, named)
    one, two, three = (across("space", [z ^ k for z in range(4)], piece) for k, piece in zip((1, 2, 3), back))
    final = over("lev", 1, final)
    atmos_next, returned = local(
        returned_kernel,
        (values(*atmos_state.shape), values(FIELDS * 2 * ROWS, LANES)),
        [pltpu.VMEM] * 3,
    )(atmos, final, named)
    ocean_next = local(rows_kernel, values(*ocean_state.shape), [pltpu.VMEM] * 4)(three, two, one, final)
    return (atmos_next, ocean_next, returned.reshape(FIELDS, 2 * ROWS, LANES))


def shards(*arguments):
    atmos_state, ocean_state, mixing, coupling, request_cells, margin_slot = arguments[:6]
    by_columns = (
        (lax.axis_size("space"), lax.axis_size("comp"), lax.axis_size("lev")) == (4, 2, 2)
        and atmos_state.shape == (LEVELS // 2, 2 * ROWS, LANES)
        and ocean_state.shape == (FIELDS, 1, 4 * LANES)
        and request_cells.shape == (1, ROWS, 2 * LANES)
        and margin_slot.shape[0] == MARGINS
    )
    return (shards_by_columns if by_columns else shards_by_neighbours)(*arguments)


def solution(mesh):
    placed = (
        P(("parts", "lev"), None, ("space", "comp")),
        P(("parts", "lev"), ("space", "comp"), None),
        P(),
        P(),
        P(("space", "comp"), None, None),
        P(None, ("space", "comp"), None),
        P(None, ("space", "comp"), None),
        P(("space", "comp"), None),
    )
    return jax.shard_map(
        shards,
        mesh=mesh,
        in_specs=placed,
        out_specs=(
            P(("parts", "lev"), None, ("space", "comp")),
            P(("parts", "lev"), ("space", "comp"), None),
            P(("parts", "lev"), None, ("space", "comp")),
        ),
        check_vma=False,
    )
```
